128 devices in a mesh: sub: 4 (over x), dp: 32 (over y, z, core).
Axes of the slice: x: 4, y: 4, z: 4, core: 2. Of those that a mesh axis runs over, the one named last changes fastest.
Arguments:
- enc_in: float32 [4, 64, 128, 640], P('sub', 'dp'), may hold values from -6 to 6
- prev_enc: float32 [4, 64, 128, 640], P('sub', 'dp'), may hold values from -6 to 6
- dec_in: float32 [4, 64, 128, 640], P('sub', 'dp'), may hold values from -6 to 6
- enc_cotan: float32 [4, 64, 128, 640], P('sub', 'dp'), may hold values from -6 to 6
- dec_cotan: float32 [4, 64, 128, 640], P('sub', 'dp'), may hold values from -6 to 6
- src_lengths: int32 [4, 64], P('sub', 'dp'), may hold values from 1 to 128, as said below
- tgt_lengths: int32 [4, 64], P('sub', 'dp'), may hold values from 1 to 128, as said below
- configs: int32 [4, 4], replicated, may hold values from 1 to 3072, as said below
- enc_gains: bfloat16 [640, 2], replicated, may hold values from 0.3984375 to 1.59375
- enc_shifts: bfloat16 [640, 2], replicated, may hold values from -1.5 to 1.5
- enc_triple: bfloat16 [640, 1920], replicated, may hold values from -0.25 to 0.25
- enc_output: bfloat16 [640, 640], replicated, may hold values from -0.625 to 0.625
- enc_biases: bfloat16 [640, 4], replicated, may hold values from -1.5 to 1.5
- enc_up: bfloat16 [640, 3072], replicated, may hold values from -0.25 to 0.25
- enc_up_bias: bfloat16 [3072], replicated, may hold values from -1.5 to 1.5
- enc_down: bfloat16 [3072, 640], replicated, may hold values from -0.109375 to 0.109375
- dec_gains: bfloat16 [640, 3], replicated, may hold values from 0.3984375 to 1.59375
- dec_shifts: bfloat16 [640, 3], replicated, may hold values from -1.5 to 1.5
- dec_triple: bfloat16 [640, 1920], replicated, may hold values from -0.25 to 0.25
- dec_output: bfloat16 [640, 640], replicated, may hold values from -0.625 to 0.625
- dec_cross_query: bfloat16 [640, 640], replicated, may hold values from -0.25 to 0.25
- dec_cross_pair: bfloat16 [640, 1280], replicated, may hold values from -0.25 to 0.25
- dec_cross_out: bfloat16 [640, 640], replicated, may hold values from -0.625 to 0.625
- dec_biases: bfloat16 [640, 7], replicated, may hold values from -1.5 to 1.5
- dec_up: bfloat16 [640, 3072], replicated, may hold values from -0.25 to 0.25
- dec_up_bias: bfloat16 [3072], replicated, may hold values from -1.5 to 1.5
- dec_down: bfloat16 [3072, 640], replicated, may hold values from -0.109375 to 0.109375
Outputs:
- encoded: float32 [4, 64, 128, 640], P('sub', 'dp')
- decoded: float32 [4, 64, 128, 640], P('sub', 'dp')
- enc_in_grad: float32 [4, 64, 128, 640], P('sub', 'dp')
- prev_enc_grad: float32 [4, 64, 128, 640], P('sub', 'dp')
- dec_in_grad: float32 [4, 64, 128, 640], P('sub', 'dp')
- enc_gains_grad: float32 [640, 2], P('dp')
- enc_shifts_grad: float32 [640, 2], P('dp')
- enc_triple_grad: float32 [640, 1920], P('dp')
- enc_output_grad: float32 [640, 640], P('dp')
- enc_biases_grad: float32 [640, 4], P('dp')
- enc_up_grad: float32 [640, 3072], P('dp')
- enc_up_bias_grad: float32 [3072], P('dp')
- enc_down_grad: float32 [3072, 640], P('dp')
- dec_gains_grad: float32 [640, 3], P('dp')
- dec_shifts_grad: float32 [640, 3], P('dp')
- dec_triple_grad: float32 [640, 1920], P('dp')
- dec_output_grad: float32 [640, 640], P('dp')
- dec_cross_query_grad: float32 [640, 640], P('dp')
- dec_cross_pair_grad: float32 [640, 1280], P('dp')
- dec_cross_out_grad: float32 [640, 640], P('dp')
- dec_biases_grad: float32 [640, 7], P('dp')
- dec_up_grad: float32 [640, 3072], P('dp')
- dec_up_bias_grad: float32 [3072], P('dp')
- dec_down_grad: float32 [3072, 640], P('dp')
The draws below stay inside these ranges and needn't reach their ends.
Inputs may be any that keep to these rules, and one draw needn't show every extreme that they name: `src_lengths`: the last sentence of every group has exactly 128. `tgt_lengths`: the last sentence of every group has exactly 128. `configs`: row g: embedding width 640 - 640 // 5 or 640; heads 8 // 2 or 8; feed-forward width k * 1024 for k = 1, 2, 3; cross-layer mask 1 to 7. Some group has 640, 8, 3072 and cross-layer mask 7.
All inputs are finite; a program needn't handle non-finite values.
Results may differ from the reference program's by a relative error of at most 0.00035.
Values sent between devices are 32-bit elements; how exact they have to be, the bound alone decides.
No kernel may reach another device: no remote copies, remote signals or barrier semaphores. Data moves between devices by JAX's collectives and lax.ppermute only.
A program may use at most 320 MiB of HBM per device.

```python
import math
import jax
import jax.numpy as jnp
from jax import lax

D = 640
H = 8
FF = 3072
LEN = 128
HD = 80
GROUPS = 4
SENTS = 64


def ragged_lengths(source_key):
    places = jnp.arange(SENTS)
    ceiling = LEN // 3 + (LEN - LEN // 3) * places // max(SENTS - 1, 1)
    floor_len = jnp.maximum(ceiling // 2, 1)
    raw_values = jax.random.randint(source_key, (GROUPS, SENTS), 0, 1 << 20)
    lengths = floor_len + raw_values % (ceiling - floor_len + 1)
    lengths = jnp.where(places[None, :] == SENTS - 1, LEN, lengths)
    return lengths.astype(jnp.int32)


def draw_src_lengths(key, part):
    key = jax.random.fold_in(key, 5)
    return ragged_lengths(key)


def draw_tgt_lengths(key, part):
    key = jax.random.fold_in(key, 9)
    return ragged_lengths(key)


def draw_configs(key, part):
    key = jax.random.fold_in(key, 13)
    streams = jax.random.split(key, 5)
    embed = jnp.where(jax.random.randint(streams[0], (GROUPS,), 0, 2) == 1, D, D - D // 5)
    heads = jnp.where(jax.random.randint(streams[1], (GROUPS,), 0, 2) == 1, H, H // 2)
    ffn_width = jax.random.randint(streams[2], (GROUPS,), 1, 4) * FF // 3
    cross = jax.random.randint(streams[3], (GROUPS,), 1, 8)
    chosen = jax.random.randint(streams[4], (), 0, GROUPS)
    is_full = jnp.arange(GROUPS) == chosen
    embed = jnp.where(is_full, D, embed)
    heads = jnp.where(is_full, H, heads)
    ffn_width = jnp.where(is_full, FF, ffn_width)
    cross = jnp.where(is_full, 7, cross)
    return jnp.stack([embed, heads, ffn_width, cross], 1).astype(jnp.int32)


def level_of(key, extent, cuts, smallest, high):
    gain, own = 1.0, jax.random.fold_in(key, 6)
    for dim, blocks in cuts:
        heights = jnp.exp(jax.random.uniform(jax.random.fold_in(own, dim), (blocks,), jnp.float32, smallest / len(cuts), high / len(cuts)))
        gain = gain * jnp.repeat(heights, extent[dim] // blocks).reshape([-1 if axis == dim else 1 for axis in range(len(extent))])
    return gain


def bell_draw(rng, dims, scale, most, shards=(), held_as=jnp.bfloat16):
    factor_of = level_of(rng, dims, shards, -0.22, 0.18) if shards else 1.0
    entries = jax.random.normal(rng, dims, jnp.float32) * scale * factor_of
    return jnp.minimum(jnp.maximum(entries, -most), most).astype(held_as)


def setup_inputs(seed: int = 0) -> dict:
    keys = jax.random.split(jax.random.key(seed), 28)
    enc_in = bell_draw(keys[0], (GROUPS, SENTS, LEN, D), 1.0, 6.0, ((0, 4), (1, 32)), jnp.float32)
    prev_enc = bell_draw(keys[1], (GROUPS, SENTS, LEN, D), 1.0, 6.0, ((0, 4), (1, 32)), jnp.float32)
    dec_in = bell_draw(keys[2], (GROUPS, SENTS, LEN, D), 1.0, 6.0, ((0, 4), (1, 32)), jnp.float32)
    enc_cotan = bell_draw(keys[3], (GROUPS, SENTS, LEN, D), 1.0, 6.0, ((0, 4), (1, 32)), jnp.float32)
    dec_cotan = bell_draw(keys[4], (GROUPS, SENTS, LEN, D), 1.0, 6.0, ((0, 4), (1, 32)), jnp.float32)
    src_lengths = draw_src_lengths(jax.random.fold_in(keys[27], 71), 0)
    tgt_lengths = draw_tgt_lengths(jax.random.fold_in(keys[27], 71), 0)
    configs = draw_configs(jax.random.fold_in(keys[27], 71), 0)
    enc_gains = jnp.clip(1.0 + 0.12 * jax.random.normal(keys[8], (D, 2), jnp.float32), 0.3984375, 1.59375).astype(jnp.bfloat16)
    enc_shifts = bell_draw(keys[9], (D, 2), 0.3, 1.5)
    enc_triple = bell_draw(keys[10], (D, 3 * D), D ** -0.5, 0.25)
    enc_output = bell_draw(keys[11], (D, D), (D // 8) ** -0.5, 0.625)
    enc_biases = bell_draw(keys[12], (D, 4), 0.3, 1.5)
    enc_up = bell_draw(keys[13], (D, FF), D ** -0.5, 0.25)
    enc_up_bias = bell_draw(keys[14], (FF,), 0.3, 1.5)
    enc_down = bell_draw(keys[15], (FF, D), FF ** -0.5, 0.109375)
    dec_gains = jnp.clip(1.0 + 0.12 * jax.random.normal(keys[16], (D, 3), jnp.float32), 0.3984375, 1.59375).astype(jnp.bfloat16)
    dec_shifts = bell_draw(keys[17], (D, 3), 0.3, 1.5)
    dec_triple = bell_draw(keys[18], (D, 3 * D), D ** -0.5, 0.25)
    dec_output = bell_draw(keys[19], (D, D), (D // 8) ** -0.5, 0.625)
    dec_cross_query = bell_draw(keys[20], (D, D), D ** -0.5, 0.25)
    dec_cross_pair = bell_draw(keys[21], (D, 2 * D), D ** -0.5, 0.25)
    dec_cross_out = bell_draw(keys[22], (D, D), (D // 8) ** -0.5, 0.625)
    dec_biases = bell_draw(keys[23], (D, 7), 0.3, 1.5)
    dec_up = bell_draw(keys[24], (D, FF), D ** -0.5, 0.25)
    dec_up_bias = bell_draw(keys[25], (FF,), 0.3, 1.5)
    dec_down = bell_draw(keys[26], (FF, D), FF ** -0.5, 0.109375)
    return {"enc_in": enc_in, "prev_enc": prev_enc, "dec_in": dec_in, "enc_cotan": enc_cotan, "dec_cotan": dec_cotan, "src_lengths": src_lengths, "tgt_lengths": tgt_lengths, "configs": configs, "enc_gains": enc_gains, "enc_shifts": enc_shifts, "enc_triple": enc_triple, "enc_output": enc_output, "enc_biases": enc_biases, "enc_up": enc_up, "enc_up_bias": enc_up_bias, "enc_down": enc_down, "dec_gains": dec_gains, "dec_shifts": dec_shifts, "dec_triple": dec_triple, "dec_output": dec_output, "dec_cross_query": dec_cross_query, "dec_cross_pair": dec_cross_pair, "dec_cross_out": dec_cross_out, "dec_biases": dec_biases, "dec_up": dec_up, "dec_up_bias": dec_up_bias, "dec_down": dec_down}


@jax.custom_vjp
def low(v):
    return lax.optimization_barrier(v.astype(jnp.bfloat16)).astype(jnp.float32)

@jax.custom_vjp
def low_back(v):
    return v

def low_keep(v):
    return (low(v), None)

def low_pass(kept, grad):
    return (grad,)

def back_keep(v):
    return (v, None)

def back_low(kept, grad):
    return (low(grad),)
low.defvjp(low_keep, low_pass)
low_back.defvjp(back_keep, back_low)
precise = lax.Precision.HIGHEST

def project(values, weight):
    return jnp.einsum('sli,ij->slj', values, weight, precision=precise)

def layer_norm(inputs, norm_gain, norm_shift, keep_mask, kept_width):
    average = lax.optimization_barrier(jnp.sum(inputs * keep_mask, -1, keepdims=True)) / kept_width
    centred = (inputs - average) * keep_mask
    spread = lax.optimization_barrier(jnp.sum(centred * centred, -1, keepdims=True)) / kept_width
    return (centred * lax.rsqrt(spread + 1e-05) * norm_gain + norm_shift) * keep_mask

def attention_core(queries, key_rows, values, allowed):
    sentences, query_len = (queries.shape[0], queries.shape[1])
    key_len = key_rows.shape[1]
    queries = queries.reshape(sentences, query_len, H, HD)
    key_rows = key_rows.reshape(sentences, key_len, H, HD)
    values = values.reshape(sentences, key_len, H, HD)
    scores = jnp.einsum('sqhd,skhd->shqk', queries, key_rows, precision=precise) / math.sqrt(HD)
    scores = jnp.where(allowed[:, None], scores, -1e+30)
    highest = lax.optimization_barrier(jnp.max(scores, -1, keepdims=True))
    weights = jnp.exp(scores - highest)
    probabilities = weights / lax.optimization_barrier(jnp.sum(weights, -1, keepdims=True))
    mixed = jnp.einsum('shqk,skhd->sqhd', probabilities, values, precision=precise)
    return mixed.reshape(sentences, query_len, H * HD)

def encoder_rows(inputs, params, setting):
    gains, shifts, triple, output, biases, up_proj, up_bias, down_proj = params
    keep_mask, heads, ffn_mask, kept_width, picked, src_ok, tgt_ok = setting
    allowed = src_ok[:, None, :] > 0.5
    normed = layer_norm(inputs, gains[:, 0], shifts[:, 0], keep_mask, kept_width)
    joined = project(normed, triple)
    queries = (joined[..., :D] + biases[:, 0]) * heads
    key_rows = joined[..., D:2 * D] * heads
    values = (joined[..., 2 * D:] + biases[:, 1]) * heads
    mixed = jax.checkpoint(attention_core)(queries, key_rows, values, allowed)
    middle = inputs + (project(mixed, output) + biases[:, 2]) * keep_mask
    normed = layer_norm(middle, gains[:, 1], shifts[:, 1], keep_mask, kept_width)
    hidden = jax.nn.gelu(project(normed, up_proj) + up_bias, approximate=False) * ffn_mask
    result = middle + (project(hidden, down_proj) + biases[:, 3]) * keep_mask
    return result * src_ok[:, :, None]

def decoder_rows(inputs, previous, source, encoded, params, setting):
    gains, shifts, triple, output, cross_query, cross_pair, cross_out, biases, up_proj, up_bias, down_proj = params
    keep_mask, heads, ffn_mask, kept_width, picked, src_ok, tgt_ok = setting
    length = inputs.shape[1]
    causal = jnp.arange(length)[:, None] >= jnp.arange(length)[None, :]
    own_allowed = causal[None] & (tgt_ok[:, None, :] > 0.5)
    cross_allowed = src_ok[:, None, :] > 0.5
    memory = (picked[0] * previous + picked[1] * source + picked[2] * encoded) / jnp.sum(picked)
    normed = layer_norm(inputs, gains[:, 0], shifts[:, 0], keep_mask, kept_width)
    joined = project(normed, triple)
    queries = (joined[..., :D] + biases[:, 0]) * heads
    key_rows = joined[..., D:2 * D] * heads
    values = (joined[..., 2 * D:] + biases[:, 1]) * heads
    mixed = jax.checkpoint(attention_core)(queries, key_rows, values, own_allowed)
    after_self = inputs + (project(mixed, output) + biases[:, 2]) * keep_mask
    normed = layer_norm(after_self, gains[:, 1], shifts[:, 1], keep_mask, kept_width)
    queries = (project(normed, cross_query) + biases[:, 3]) * heads
    pair_rows = project(memory * keep_mask, cross_pair)
    key_rows = pair_rows[..., :D] * heads
    values = (pair_rows[..., D:] + biases[:, 4]) * heads
    mixed = jax.checkpoint(attention_core)(queries, key_rows, values, cross_allowed)
    after_cross = after_self + (project(mixed, cross_out) + biases[:, 5]) * keep_mask
    normed = layer_norm(after_cross, gains[:, 2], shifts[:, 2], keep_mask, kept_width)
    hidden = jax.nn.gelu(project(normed, up_proj) + up_bias, approximate=False) * ffn_mask
    result = after_cross + (project(hidden, down_proj) + biases[:, 6]) * keep_mask
    return result * tgt_ok[:, :, None]

def both_layers(enc_rows, prev_rows, dec_rows, enc_params, dec_params, setting):
    encoded = encoder_rows(enc_rows, enc_params, setting)
    decoded = decoder_rows(dec_rows, prev_rows, enc_rows, encoded, dec_params, setting)
    return (encoded, decoded)

def group_tables(configs):
    places = jnp.arange(D)
    embed = (places[None, :] < configs[:, 0:1]).astype(jnp.float32)
    heads = (places[None, :] < configs[:, 1:2] * HD).astype(jnp.float32)
    ffn_table = (jnp.arange(FF)[None, :] < configs[:, 2:3]).astype(jnp.float32)
    return (embed, heads, ffn_table)

def make_setting(configs, tables, group, src_count, tgt_count):
    embed, heads, ffn_table = tables
    choose = jnp.arange(configs.shape[0]) == group
    weight = choose.astype(jnp.float32)[:, None]
    own_row = lax.optimization_barrier(jnp.sum(configs * choose[:, None].astype(configs.dtype), 0))
    keep_mask = lax.optimization_barrier(jnp.sum(embed * weight, 0))
    head_mask = lax.optimization_barrier(jnp.sum(heads * weight, 0))
    ffn_mask = lax.optimization_barrier(jnp.sum(ffn_table * weight, 0))
    kept_width = own_row[0].astype(jnp.float32)
    picked = (own_row[3] // jnp.array([1, 2, 4], dtype=configs.dtype) % 2).astype(jnp.float32)
    places = jnp.arange(LEN)[None, :]
    src_ok = (places < src_count[:, None]).astype(jnp.float32)
    tgt_ok = (places < tgt_count[:, None]).astype(jnp.float32)
    return (keep_mask, head_mask, ffn_mask, kept_width, picked, src_ok, tgt_ok)

def usage_grid(row_kinds, col_kinds, totals):
    return jnp.dot((row_kinds * totals[:, None]).T, col_kinds, precision=precise)

def usage_columns(kind_list, totals):
    return jnp.stack([jnp.dot(totals, one_kind, precision=precise) for one_kind in kind_list], 1)

def shrink(gradient, usage):
    return gradient * lax.rsqrt(usage)

def rescale(enc_grads, dec_grads, row_tables, col_tables, src_total, tgt_total):
    embed_r, heads_r, ffn_r = row_tables
    embed_c, heads_c, ffn_c = col_tables
    gains, shifts, triple, output, biases, up_proj, up_bias, down_proj = enc_grads
    embed_use = usage_columns((embed_r,), src_total)
    enc_final = (shrink(gains, embed_use), shrink(shifts, embed_use), shrink(triple, usage_grid(embed_r, jnp.concatenate([heads_c] * 3, 1), src_total)), shrink(output, usage_grid(heads_r, embed_c, src_total)), shrink(biases, usage_columns((heads_r, heads_r, embed_r, embed_r), src_total)), shrink(up_proj, usage_grid(embed_r, ffn_c, src_total)), shrink(up_bias, usage_columns((ffn_r,), src_total)[:, 0]), shrink(down_proj, usage_grid(ffn_r, embed_c, src_total)))
    gains, shifts, triple, output, cross_query, cross_pair, cross_out, biases, up_proj, up_bias, down_proj = dec_grads
    embed_use = usage_columns((embed_r,), tgt_total)
    dec_final = (shrink(gains, embed_use), shrink(shifts, embed_use), shrink(triple, usage_grid(embed_r, jnp.concatenate([heads_c] * 3, 1), tgt_total)), shrink(output, usage_grid(heads_r, embed_c, tgt_total)), shrink(cross_query, usage_grid(embed_r, heads_c, tgt_total)), shrink(cross_pair, usage_grid(embed_r, jnp.concatenate([heads_c] * 2, 1), tgt_total)), shrink(cross_out, usage_grid(heads_r, embed_c, tgt_total)), shrink(biases, usage_columns((heads_r, heads_r, embed_r, heads_r, heads_r, embed_r, embed_r), tgt_total)), shrink(up_proj, usage_grid(embed_r, ffn_c, tgt_total)), shrink(up_bias, usage_columns((ffn_r,), tgt_total)[:, 0]), shrink(down_proj, usage_grid(ffn_r, embed_c, tgt_total)))
    return (enc_final, dec_final)

def reference(enc_in, prev_enc, dec_in, enc_cotan, dec_cotan, src_lengths, tgt_lengths, configs, enc_gains, enc_shifts, enc_triple, enc_output, enc_biases, enc_up, enc_up_bias, enc_down, dec_gains, dec_shifts, dec_triple, dec_output, dec_cross_query, dec_cross_pair, dec_cross_out, dec_biases, dec_up, dec_up_bias, dec_down):
    enc_params = tuple((matrix.astype(jnp.float32) for matrix in (enc_gains, enc_shifts, enc_triple, enc_output, enc_biases, enc_up, enc_up_bias, enc_down)))
    dec_params = tuple((matrix.astype(jnp.float32) for matrix in (dec_gains, dec_shifts, dec_triple, dec_output, dec_cross_query, dec_cross_pair, dec_cross_out, dec_biases, dec_up, dec_up_bias, dec_down)))
    tables = group_tables(configs)
    block_sents = math.gcd(SENTS, max(1, 4096 // LEN))
    blocks = GROUPS * SENTS // block_sents

    def to_blocks(array):
        return array.reshape((blocks, block_sents) + array.shape[2:])
    group_of = (jnp.arange(blocks) // (SENTS // block_sents)).astype(jnp.int32)

    def block_step(carry, pieces):
        enc_x, prev_x, dec_x, enc_c, dec_c, src_count, tgt_count, group = pieces
        setting = make_setting(configs, tables, group, src_count, tgt_count)

        def forward(enc_rows, prev_rows, dec_rows, enc_weights, dec_weights):
            return both_layers(enc_rows, prev_rows, dec_rows, enc_weights, dec_weights, setting)
        (enc_y, dec_y), pull_back = jax.vjp(forward, enc_x, prev_x, dec_x, enc_params, dec_params)
        enc_dx, prev_dx, dec_dx, enc_dw, dec_dw = pull_back((enc_c, dec_c))
        carry = jax.tree.map(jnp.add, carry, (enc_dw, dec_dw))
        return (carry, (enc_y, dec_y, enc_dx, prev_dx, dec_dx))
    zeros = jax.tree.map(jnp.zeros_like, (enc_params, dec_params))
    (enc_sums, dec_sums), stacked = lax.scan(block_step, zeros, (to_blocks(enc_in), to_blocks(prev_enc), to_blocks(dec_in), to_blocks(enc_cotan), to_blocks(dec_cotan), to_blocks(src_lengths), to_blocks(tgt_lengths), group_of))
    whole = (GROUPS, SENTS, LEN, D)
    encoded = stacked[0].reshape(whole)
    decoded = stacked[1].reshape(whole)
    enc_in_grad = stacked[2].reshape(whole)
    prev_enc_grad = stacked[3].reshape(whole)
    dec_in_grad = stacked[4].reshape(whole)
    src_total = lax.optimization_barrier(jnp.sum(src_lengths, 1)).astype(jnp.float32)
    tgt_total = lax.optimization_barrier(jnp.sum(tgt_lengths, 1)).astype(jnp.float32)
    enc_final, dec_final = rescale(enc_sums, dec_sums, tables, tables, src_total, tgt_total)
    e_gains, e_shifts, e_triple, e_output, e_biases, e_up, e_up_bias, e_down = enc_final
    d_gains, d_shifts, d_triple, d_output, d_query, d_pair, d_cross_out, d_biases, d_up, d_up_bias, d_down = dec_final
    return (encoded, decoded, enc_in_grad, prev_enc_grad, dec_in_grad, e_gains, e_shifts, e_triple, e_output, e_biases, e_up, e_up_bias, e_down, d_gains, d_shifts, d_triple, d_output, d_query, d_pair, d_cross_out, d_biases, d_up, d_up_bias, d_down)
```

```python
import functools
import math

import jax
import jax.numpy as jnp
from jax import lax
from jax.experimental import pallas as pl
from jax.experimental.pallas import tpu as pltpu
from jax.sharding import PartitionSpec as P

D = 640
H = 8
FF = 3072
LEN = 128
HD = 80
SENT = 2
T = SENT * LEN
TILE = 512
ROWS_FFN = 960
ROWS_ATT = 416
f32 = jnp.float32
bf16 = jnp.bfloat16
NN = (((1,), (0,)), ((), ()))
NT = (((1,), (1,)), ((), ()))
TN = (((0,), (0,)), ((), ()))
MESH_AXES = ("sub", "dp")


def split(x):
    hi = x.astype(bf16)
    lo = (x - hi.astype(f32)).astype(bf16)
    return hi, lo


def stacked(x):
    return jnp.concatenate(split(x), 0)


def halves(r):
    n = r.shape[0] // 2
    return r[:n] + r[n:]


def mm(xs, w, dims=NN):
    return halves(lax.dot_general(xs, w, dims, preferred_element_type=f32))


def dot3(a, b, dims):
    ah, al = a
    bh, bl = b
    dg = functools.partial(lax.dot_general, dimension_numbers=dims, preferred_element_type=f32)
    return dg(al, bh) + dg(ah, bl) + dg(ah, bh)


def lane_mask(width, limit):
    return (lax.broadcasted_iota(jnp.int32, (1, width), 1) < limit).astype(f32)


def row_ok(len0, len1):
    row = lax.broadcasted_iota(jnp.int32, (T, 1), 0)
    limit = jnp.where(row < LEN, len0, LEN + len1)
    return (row < limit).astype(f32)


def norm(x, keep, width):
    mean = jnp.sum(x * keep, -1, keepdims=True) / width
    centred = (x - mean) * keep
    var = jnp.sum(centred * centred, -1, keepdims=True) / width
    rstd = lax.rsqrt(var + 1e-5)
    return centred * rstd, rstd


def norm_back(dy, n, rstd, gain, keep, width):
    dy = dy * keep
    dz = dy * gain
    m1 = jnp.sum(dz, -1, keepdims=True) / width
    m2 = jnp.sum(dz * n, -1, keepdims=True) / width
    dx = keep * rstd * (dz - m1 - n * m2)
    return dx, jnp.sum(dy * n, 0, keepdims=True), jnp.sum(dy, 0, keepdims=True)


def bell(z):
    cdf = 0.5 * (1.0 + lax.erf(z * (1.0 / math.sqrt(2.0))))
    pdf = jnp.exp(-0.5 * z * z) * (1.0 / math.sqrt(2.0 * math.pi))
    return cdf, pdf


def attend(q, k, v, lens, causal, p_ref):
    qs, ks, vs = split(q), split(k), split(v)
    col = lax.broadcasted_iota(jnp.int32, (LEN, LEN), 1)
    rows = []
    for s in range(SENT):
        allowed = col < lens[s]
        if causal:
            allowed = allowed & (lax.broadcasted_iota(jnp.int32, (LEN, LEN), 0) >= col)
        outs = []
        for h in range(H):
            def part(pair):
                return tuple(x[s * LEN:(s + 1) * LEN, h * HD:(h + 1) * HD] for x in pair)
            scores = dot3(part(qs), part(ks), NT) * (1.0 / math.sqrt(HD))
            scores = jnp.where(allowed, scores, -1e30)
            e = jnp.exp(scores - jnp.max(scores, -1, keepdims=True))
            prob = e / jnp.sum(e, -1, keepdims=True)
            p_ref[s * H + h] = prob
            outs.append(dot3(split(prob), part(vs), NN))
        rows.append(jnp.concatenate(outs, 1))
    return jnp.concatenate(rows, 0)


def attend_back(do, q, k, v, p_ref):
    dos, qs, ks, vs = split(do), split(q), split(k), split(v)
    all_q, all_k, all_v = [], [], []
    for s in range(SENT):
        dqs, dks, dvs = [], [], []
        for h in range(H):
            def part(pair):
                return tuple(x[s * LEN:(s + 1) * LEN, h * HD:(h + 1) * HD] for x in pair)
            prob = p_ref[s * H + h]
            dp = dot3(part(dos), part(vs), NT)
            ds = prob * (dp - jnp.sum(dp * prob, -1, keepdims=True)) * (1.0 / math.sqrt(HD))
            dss = split(ds)
            dvs.append(dot3(split(prob), part(dos), TN))
            dqs.append(dot3(dss, part(ks), NN))
            dks.append(dot3(dss, part(qs), TN))
        all_q.append(jnp.concatenate(dqs, 1))
        all_k.append(jnp.concatenate(dks, 1))
        all_v.append(jnp.concatenate(dvs, 1))
    return tuple(jnp.concatenate(x, 0) for x in (all_q, all_k, all_v))


def ffn_forward(ns, up, bias, down, ffn_limit, z_ref, acc_ref):
    acc_ref[...] = jnp.zeros_like(acc_ref)

    def body(j, _):
        sl = pl.ds(pl.multiple_of(j * TILE, TILE), TILE)
        z = mm(ns[...], up[:, sl]) + bias[:, sl]
        z_ref[:, sl] = z
        mask = (lax.broadcasted_iota(jnp.int32, (1, TILE), 1) + j * TILE < ffn_limit).astype(f32)
        u = z * bell(z)[0] * mask
        acc_ref[...] += mm(stacked(u), down[sl, :])
        return 0

    lax.fori_loop(0, FF // TILE, body, 0)


def ffn_backward(dyk, n, z_ref, up, down, ffn_limit, core, dys_ref, keep_ref, send_ref, bias_ref, acc_ref):
    acc_ref[...] = jnp.zeros_like(acc_ref)
    dys_ref[...] = stacked(dyk)
    first = core == 0
    keep_ref[:, :D] = jnp.where(first, n, dyk)
    send_ref[:, :D] = jnp.where(first, dyk, n)

    def body(j, _):
        sl = pl.ds(pl.multiple_of(j * TILE, TILE), TILE)
        out = pl.ds(pl.multiple_of(j * TILE + D, 128), TILE)
        du = mm(dys_ref[...], down[sl, :], NT)
        z = z_ref[:, sl]
        cdf, pdf = bell(z)
        mask = (lax.broadcasted_iota(jnp.int32, (1, TILE), 1) + j * TILE < ffn_limit).astype(f32)
        u = z * cdf * mask
        dz = du * mask * (cdf + z * pdf)
        keep_ref[:, out] = jnp.where(first, dz, u)
        send_ref[:, out] = jnp.where(first, u, dz)
        bias_ref[:, sl] = jnp.sum(dz, 0, keepdims=True)
        acc_ref[...] += mm(stacked(dz), up[:, sl], NT)
        return 0

    lax.fori_loop(0, FF // TILE, body, 0)


def load_vectors(vec_ref):
    return vec_ref[...].astype(f32).T


def fetch(pairs, sems):
    copies = [pltpu.make_async_copy(a, b, sems.at[i]) for i, (a, b) in enumerate(pairs)]
    for c in copies:
        c.start()
    return copies


def encoder_kernel(sc, vec_ref, upb, x_ref, w_triple, w_out, w_up, w_down,
                   encoded, qkv, p_ref, mixed, middle, z_ref,
                   b_triple, b_out, b_up, b_down, ns_ref, acc_ref, sems):
    copies = fetch([(w_triple, b_triple), (w_out, b_out), (w_up, b_up), (w_down, b_down)], sems)
    width = sc[0].astype(f32)
    keep, heads = lane_mask(D, sc[0]), lane_mask(D, sc[1])
    vec = load_vectors(vec_ref)
    x = x_ref[...]
    n, _ = norm(x, keep, width)
    ns = stacked((n * vec[0:1] + vec[2:3]) * keep)
    copies[0].wait()
    qkv[:, :D] = (mm(ns, b_triple[:, :D]) + vec[4:5]) * heads
    qkv[:, D:2 * D] = mm(ns, b_triple[:, D:2 * D]) * heads
    qkv[:, 2 * D:] = (mm(ns, b_triple[:, 2 * D:]) + vec[5:6]) * heads
    o = attend(qkv[:, :D], qkv[:, D:2 * D], qkv[:, 2 * D:], (sc[3], sc[4]), False, p_ref)
    mixed[...] = o
    copies[1].wait()
    mid = x + (mm(stacked(o), b_out[...]) + vec[6:7]) * keep
    middle[...] = mid
    n, _ = norm(mid, keep, width)
    ns_ref[...] = stacked((n * vec[1:2] + vec[3:4]) * keep)
    copies[2].wait()
    copies[3].wait()
    ffn_forward(ns_ref, b_up, upb, b_down, sc[2], z_ref, acc_ref)
    encoded[...] = (mid + (acc_ref[...] + vec[7:8]) * keep) * row_ok(sc[3], sc[4])


def decoder_kernel(sc, pick, vec_ref, upb, x_ref, prev_ref, src_ref, enc_ref, cot_ref,
                   w_triple, w_out, w_query, w_pair, w_cross, w_up, w_down,
                   decoded, qkv, p_self, mixed, a1_ref, mem_ref, qkv_c, p_cross, mixed_c, a2_ref, da2_ref,
                   keep_buf, send_buf, dvec, dupb,
                   b_triple, b_out, b_query, b_pair, b_cross, b_up, b_down, ns_ref, acc_ref, z_ref, sems):
    copies = fetch([(w_triple, b_triple), (w_out, b_out), (w_query, b_query), (w_pair, b_pair),
                    (w_cross, b_cross), (w_up, b_up), (w_down, b_down)], sems)
    width = sc[0].astype(f32)
    keep, heads = lane_mask(D, sc[0]), lane_mask(D, sc[1])
    vec = load_vectors(vec_ref)
    x = x_ref[...]
    n, _ = norm(x, keep, width)
    ns = stacked((n * vec[0:1] + vec[3:4]) * keep)
    copies[0].wait()
    qkv[:, :D] = (mm(ns, b_triple[:, :D]) + vec[6:7]) * heads
    qkv[:, D:2 * D] = mm(ns, b_triple[:, D:2 * D]) * heads
    qkv[:, 2 * D:] = (mm(ns, b_triple[:, 2 * D:]) + vec[7:8]) * heads
    o = attend(qkv[:, :D], qkv[:, D:2 * D], qkv[:, 2 * D:], (sc[5], sc[6]), True, p_self)
    mixed[...] = o
    copies[1].wait()
    a1 = x + (mm(stacked(o), b_out[...]) + vec[8:9]) * keep
    a1_ref[...] = a1
    n, _ = norm(a1, keep, width)
    ns = stacked((n * vec[1:2] + vec[4:5]) * keep)
    copies[2].wait()
    qkv_c[:, :D] = (mm(ns, b_query[...]) + vec[9:10]) * heads
    memory = (pick[0] * prev_ref[...] + pick[1] * src_ref[...] + pick[2] * enc_ref[...]) * keep
    mem_ref[...] = memory
    ns = stacked(memory)
    copies[3].wait()
    qkv_c[:, D:2 * D] = mm(ns, b_pair[:, :D]) * heads
    qkv_c[:, 2 * D:] = (mm(ns, b_pair[:, D:]) + vec[10:11]) * heads
    o = attend(qkv_c[:, :D], qkv_c[:, D:2 * D], qkv_c[:, 2 * D:], (sc[3], sc[4]), False, p_cross)
    mixed_c[...] = o
    copies[4].wait()
    a2_ref[...] = a1_ref[...] + (mm(stacked(o), b_cross[...]) + vec[11:12]) * keep
    n, _ = norm(a2_ref[...], keep, width)
    ns_ref[...] = stacked((n * vec[2:3] + vec[5:6]) * keep)
    copies[5].wait()
    copies[6].wait()
    ffn_forward(ns_ref, b_up, upb, b_down, sc[2], z_ref, acc_ref)
    ok = row_ok(sc[5], sc[6])
    decoded[...] = (a2_ref[...] + (acc_ref[...] + vec[12:13]) * keep) * ok
    dy = cot_ref[...] * ok
    dyk = dy * keep
    n, rstd = norm(a2_ref[...], keep, width)
    ffn_backward(dyk, (n * vec[2:3] + vec[5:6]) * keep, z_ref, b_up, b_down, sc[2], sc[7], ns_ref,
                 keep_buf, send_buf, dupb, acc_ref)
    dx, dg, db = norm_back(acc_ref[...], n, rstd, vec[2:3], keep, width)
    da2_ref[...] = dy + dx
    dvec[...] = jnp.concatenate([dg, db, jnp.sum(dyk, 0, keepdims=True), jnp.zeros((5, D), f32)], 0)


def cross_back_kernel(sc, pick, vec_ref, da2_ref, a1_ref, mem_ref, qkv_c, p_cross, mixed_c,
                      w_query, w_pair, w_cross,
                      da1_ref, dmem_ref, dprev_ref, keep_buf, send_buf, dvec):
    width = sc[0].astype(f32)
    keep, heads = lane_mask(D, sc[0]), lane_mask(D, sc[1])
    vec = load_vectors(vec_ref)
    first = sc[7] == 0
    da2 = da2_ref[...]
    dyk = da2 * keep
    do = mm(stacked(dyk), w_cross[...], NT)
    dq, dk, dv = attend_back(do, qkv_c[:, :D], qkv_c[:, D:2 * D], qkv_c[:, 2 * D:], p_cross)
    dq, dk, dv = dq * heads, dk * heads, dv * heads
    n, rstd = norm(a1_ref[...], keep, width)
    normed = (n * vec[1:2] + vec[4:5]) * keep
    for i, (a, b) in enumerate(((mem_ref[...], normed), (mem_ref[...], mixed_c[...]), (dk, dq), (dv, dyk))):
        keep_buf[:, i * D:(i + 1) * D] = jnp.where(first, a, b)
        send_buf[:, i * D:(i + 1) * D] = jnp.where(first, b, a)
    dn = mm(stacked(dq), w_query[...], NT)
    dx, dg, db = norm_back(dn, n, rstd, vec[1:2], keep, width)
    da1_ref[...] = da2 + dx
    dmem = (mm(stacked(dk), w_pair[:, :D], NT) + mm(stacked(dv), w_pair[:, D:], NT)) * keep
    dmem_ref[...] = dmem
    dprev_ref[...] = dmem * pick[0]
    dvec[...] = jnp.concatenate(
        [dg, db] + [jnp.sum(t, 0, keepdims=True) for t in (dq, dv, dyk)] + [jnp.zeros((3, D), f32)], 0)


def self_back_kernel(gain_row, shift_row, with_memory, sc, pick, vec_ref, dy_ref, x_ref, qkv, p_ref, mixed,
                     dmem_ref, w_triple, w_out, dx_ref, keep_buf, send_buf, dvec):
    width = sc[0].astype(f32)
    keep, heads = lane_mask(D, sc[0]), lane_mask(D, sc[1])
    vec = load_vectors(vec_ref)
    gain, shift = vec[gain_row:gain_row + 1], vec[shift_row:shift_row + 1]
    first = sc[7] == 0
    dy = dy_ref[...]
    dyk = dy * keep
    do = mm(stacked(dyk), w_out[...], NT)
    dq, dk, dv = attend_back(do, qkv[:, :D], qkv[:, D:2 * D], qkv[:, 2 * D:], p_ref)
    dq, dk, dv = dq * heads, dk * heads, dv * heads
    n, rstd = norm(x_ref[...], keep, width)
    normed = (n * gain + shift) * keep
    for i, (a, b) in enumerate(((normed, normed), (normed, mixed[...]), (dq, dv), (dk, dyk))):
        keep_buf[:, i * D:(i + 1) * D] = jnp.where(first, a, b)
        send_buf[:, i * D:(i + 1) * D] = jnp.where(first, b, a)
    dn = mm(stacked(dq), w_triple[:, :D], NT) + mm(stacked(dk), w_triple[:, D:2 * D], NT)
    dn += mm(stacked(dv), w_triple[:, 2 * D:], NT)
    dx, dg, db = norm_back(dn, n, rstd, gain, keep, width)
    dx = dx + dy
    if with_memory:
        dx = dx + pick[1] * dmem_ref[...]
    dx_ref[...] = dx
    dvec[...] = jnp.concatenate(
        [dg, db] + [jnp.sum(t, 0, keepdims=True) for t in (dq, dv, dyk)] + [jnp.zeros((3, D), f32)], 0)


def encoder_ffn_back_kernel(sc, pick, vec_ref, cot_ref, dmem_ref, middle, z_ref, w_up, w_down,
                            dmid_ref, keep_buf, send_buf, dvec, dupb,
                            b_up, b_down, ns_ref, acc_ref, sems):
    copies = fetch([(w_up, b_up), (w_down, b_down)], sems)
    width = sc[0].astype(f32)
    keep = lane_mask(D, sc[0])
    vec = load_vectors(vec_ref)
    dy = (cot_ref[...] + pick[2] * dmem_ref[...]) * row_ok(sc[3], sc[4])
    dyk = dy * keep
    n, rstd = norm(middle[...], keep, width)
    copies[0].wait()
    copies[1].wait()
    ffn_backward(dyk, (n * vec[1:2] + vec[3:4]) * keep, z_ref, b_up, b_down, sc[2], sc[7], ns_ref,
                 keep_buf, send_buf, dupb, acc_ref)
    dx, dg, db = norm_back(acc_ref[...], n, rstd, vec[1:2], keep, width)
    dmid_ref[...] = dy + dx
    dvec[...] = jnp.concatenate([dg, db, jnp.sum(dyk, 0, keepdims=True), jnp.zeros((5, D), f32)], 0)


def ffn_grad_kernel(sc, keep_buf, recv_buf, out, at_s, b_b, b_s, at_b):
    j = pl.program_id(0)
    first = sc[7] == 0

    @pl.when(first & (j == 0))
    def _():
        for i, ref in enumerate((keep_buf, recv_buf)):
            hi, lo = split(ref[:, :D].T)
            at_s[0, :, i * T:(i + 1) * T] = hi
            at_s[1, :, i * T:(i + 1) * T] = lo

            def body(c, _):
                src = pl.ds(pl.multiple_of(c * TILE + D, 128), TILE)
                dst = pl.ds(pl.multiple_of(c * TILE, TILE), TILE)
                hi, lo = split(ref[:, src])
                b_b[0, i * T:(i + 1) * T, dst] = hi
                b_b[1, i * T:(i + 1) * T, dst] = lo
                return 0

            lax.fori_loop(0, FF // TILE, body, 0)

    @pl.when(jnp.logical_not(first) & (j == 0))
    def _():
        for i, ref in enumerate((keep_buf, recv_buf)):
            hi, lo = split(ref[:, :D])
            b_s[0, i * T:(i + 1) * T] = hi
            b_s[1, i * T:(i + 1) * T] = lo

            def body(c, _):
                x = ref[:, pl.ds(pl.multiple_of(c * 384 + D, 128), 384)].T
                hi, lo = split(x.reshape(2, 192, T))
                at_b[0, pl.ds(2 * c, 2), :, i * T:(i + 1) * T] = hi
                at_b[1, pl.ds(2 * c, 2), :, i * T:(i + 1) * T] = lo
                return 0

            lax.fori_loop(0, 8, body, 0)

    @pl.when(first)
    def _():
        cols = pl.ds(pl.multiple_of(j * 256, 256), 256)
        r = dot3((at_s[0], at_s[1]), (b_b[0, :, cols], b_b[1, :, cols]), NN)
        for c in range(2):
            out[:, c * 40:(c + 1) * 40, :] = r[:, c * 128:(c + 1) * 128].reshape(16, 40, 128)

    @pl.when(jnp.logical_not(first))
    def _():
        rows = pl.ds(pl.multiple_of(j * 16, 16), 16)
        a = tuple(at_b[i, :, rows, :].reshape(256, 2 * T) for i in range(2))
        r = dot3(a, (b_s[0], b_s[1]), NN)
        for c in range(5):
            out[:, c * 16:(c + 1) * 16, :] = r[:, c * 128:(c + 1) * 128].reshape(16, 16, 128)


def att_grad_kernel(keep_buf, recv_buf, small, out):
    out[:, 400:, :] = small[...]
    for i in range(2):
        a = jnp.concatenate([keep_buf[:, i * D:(i + 1) * D].T, recv_buf[:, i * D:(i + 1) * D].T], 1)
        b = jnp.concatenate([keep_buf[:, (i + 2) * D:(i + 3) * D], recv_buf[:, (i + 2) * D:(i + 3) * D]], 0)
        a, b = split(a), split(b)
        for c in range(5):
            r = dot3(a, tuple(t[:, c * 128:(c + 1) * 128] for t in b), NN)
            out[:, i * 200 + c * 40:i * 200 + (c + 1) * 40, :] = r.reshape(16, 40, 128)


SMEM = pl.BlockSpec(memory_space=pltpu.SMEM)
VMEM = pl.BlockSpec(memory_space=pltpu.VMEM)
ANY = pl.BlockSpec(memory_space=pl.ANY)


def arr(*shape):
    return jax.ShapeDtypeStruct(shape, f32)


def call(kernel, in_specs, outs, flops, name, scratch=(), limit=56, nbytes=20 << 20):
    return pl.pallas_call(
        kernel,
        in_specs=in_specs,
        out_shape=outs,
        out_specs=[VMEM] * len(outs),
        scratch_shapes=list(scratch),
        name=name,
        compiler_params=pltpu.CompilerParams(vmem_limit_bytes=limit << 20),
        cost_estimate=pl.CostEstimate(flops=flops, bytes_accessed=nbytes, transcendentals=0),
    )


def flat_perm(move):
    pairs = []
    for x in range(4):
        for y in range(4):
            for z in range(4):
                for c in range(2):
                    X, Y, Z, C = move(x, y, z, c)
                    pairs.append((x * 32 + y * 8 + z * 2 + c, (X % 4) * 32 + (Y % 4) * 8 + (Z % 4) * 2 + C % 2))
    return pairs


SWAP = flat_perm(lambda x, y, z, c: (x, y, z, 1 - c))
RING = {
    "x": flat_perm(lambda x, y, z, c: (x + 1 - 2 * c, y, z, c)),
    "y": flat_perm(lambda x, y, z, c: (x, y + 1 - 2 * c, z, c)),
    "z": flat_perm(lambda x, y, z, c: (x, y, z + 1 - 2 * c, c)),
}
SHIFT_X = [flat_perm(lambda x, y, z, c, k=k: (x + k, y, z, c)) for k in range(4)]


def move(x, perm):
    return lax.ppermute(x, MESH_AXES, perm)


def reduce_part(block, order, place, sign):
    dims = ["y", "z", "x"]
    for axis in order:
        d = dims.index(axis)

        def chunk(k):
            index = (place[axis] - sign * k) & 3
            return lax.dynamic_index_in_dim(block, index, d, keepdims=False)

        got = move(chunk(1), RING[axis])
        got = move(got + chunk(2), RING[axis])
        got = move(got + chunk(3), RING[axis])
        block = got + chunk(0)
        dims.remove(axis)
    return block


def reduce_group(g, place, sign):
    rows = g.shape[1]
    quarter = rows // 4
    m = quarter // 24 * 8
    cuts = [0, quarter - 2 * m, quarter - m, quarter]
    g = g.reshape(4, 4, 4, quarter, 128)
    parts = [
        reduce_part(g[:, :, :, a:b], order, place, sign)
        for a, b, order in zip(cuts[:-1], cuts[1:], ("xyz", "yzx", "zxy"))
    ]
    own = jnp.concatenate(parts, 0)
    full = jnp.zeros((4,) + own.shape, f32)
    for k in range(4):
        piece = own if k == 0 else move(own, SHIFT_X[k])
        full = lax.dynamic_update_slice(full, piece[None], ((place["x"] - k) & 3, 0, 0))
    return full.reshape(rows, 128)


def per_device(
    enc_in, prev_enc, dec_in, enc_cotan, dec_cotan, src_lengths, tgt_lengths, configs,
    enc_gains, enc_shifts, enc_triple, enc_output, enc_biases, enc_up, enc_up_bias, enc_down,
    dec_gains, dec_shifts, dec_triple, dec_output, dec_cross_query, dec_cross_pair, dec_cross_out,
    dec_biases, dec_up, dec_up_bias, dec_down,
):
    group = lax.axis_index("sub")
    pos = lax.axis_index("dp")
    core = pos & 1
    place = {"x": group, "y": pos >> 3, "z": (pos >> 1) & 3}
    sign = 1 - 2 * core
    row = lax.dynamic_index_in_dim(configs, group, 0, keepdims=False)
    sc = jnp.stack([row[0], row[1] * HD, row[2], src_lengths[0, 0], src_lengths[0, 1],
                    tgt_lengths[0, 0], tgt_lengths[0, 1], core])
    bits = jnp.stack([row[3] & 1, (row[3] >> 1) & 1, (row[3] >> 2) & 1]).astype(f32)
    pick = bits / jnp.sum(bits)
    evec = jnp.concatenate([enc_gains, enc_shifts, enc_biases], 1)
    dvec = jnp.concatenate([dec_gains, dec_shifts, dec_biases, jnp.zeros((D, 3), bf16)], 1)
    e_upb = enc_up_bias.astype(f32)[None]
    d_upb = dec_up_bias.astype(f32)[None]
    x, prev, y = enc_in.reshape(T, D), prev_enc.reshape(T, D), dec_in.reshape(T, D)
    e_cot, d_cot = enc_cotan.reshape(T, D), dec_cotan.reshape(T, D)
    act, act3, prob = arr(T, D), arr(T, 3 * D), arr(2 * H, LEN, LEN)
    vmem = pltpu.VMEM

    encoded, e_qkv, e_p, e_mixed, e_mid, e_z = call(
        encoder_kernel, [SMEM, VMEM, VMEM, VMEM] + [ANY] * 4,
        [act, act3, prob, act, act, arr(T, FF)], 6 << 30, "encoder_forward",
        [vmem((D, 3 * D), bf16), vmem((D, D), bf16), vmem((D, FF), bf16), vmem((FF, D), bf16),
         vmem((2 * T, D), bf16), vmem((T, D), f32), pltpu.SemaphoreType.DMA((4,))],
    )(sc, evec, e_upb, x, enc_triple, enc_output, enc_up, enc_down)

    (decoded, d_qkv, d_p, d_mixed, a1, mem, c_qkv, c_p, c_mixed, a2, da2, f_keep, f_send, f_vec, f_upb) = call(
        decoder_kernel, [SMEM, SMEM] + [VMEM] * 7 + [ANY] * 7,
        [act, act3, prob, act, act, act, act3, prob, act, act, act,
         arr(T, D + FF), arr(T, D + FF), arr(8, D), arr(1, FF)], 12 << 30, "decoder_forward",
        [vmem((D, 3 * D), bf16), vmem((D, D), bf16), vmem((D, D), bf16), vmem((D, 2 * D), bf16),
         vmem((D, D), bf16), vmem((D, FF), bf16), vmem((FF, D), bf16),
         vmem((2 * T, D), bf16), vmem((T, D), f32), vmem((T, FF), f32), pltpu.SemaphoreType.DMA((7,))],
    )(sc, pick, dvec, d_upb, y, prev, x, encoded, d_cot,
      dec_triple, dec_output, dec_cross_query, dec_cross_pair, dec_cross_out, dec_up, dec_down)
    f_recv = move(f_send, SWAP)

    pair = arr(T, 4 * D)
    da1, dmem, dprev, c_keep, c_send, c_vec = call(
        cross_back_kernel, [SMEM, SMEM] + [VMEM] * 10,
        [act, act, act, pair, pair, arr(8, D)], 3 << 30, "cross_backward", limit=40,
    )(sc, pick, dvec, da2, a1, mem, c_qkv, c_p, c_mixed, dec_cross_query, dec_cross_pair, dec_cross_out)
    c_recv = move(c_send, SWAP)

    def ffn_grad(kept, got, name):
        whole = pl.BlockSpec((T, D + FF), lambda j: (0, 0))
        return pl.pallas_call(
            ffn_grad_kernel,
            grid=(12,),
            in_specs=[SMEM, whole, whole],
            out_shape=arr(16, ROWS_FFN, 128),
            out_specs=pl.BlockSpec((16, 80, 128), lambda j: (0, j, 0)),
            scratch_shapes=[vmem((2, D, 2 * T), bf16), vmem((2, 2 * T, FF), bf16), vmem((2, 2 * T, D), bf16),
                            vmem((2, 16, 192, 2 * T), bf16)],
            name=name,
            compiler_params=pltpu.CompilerParams(vmem_limit_bytes=48 << 20),
            cost_estimate=pl.CostEstimate(flops=6 << 30, bytes_accessed=16 << 20, transcendentals=0),
        )(sc, kept, got)

    def att_grad(kept, got, small, name):
        return call(att_grad_kernel, [VMEM] * 3, [arr(16, ROWS_ATT, 128)], 3 << 30, name, limit=40)(
            kept, got, small)[0]

    def small_rows(vectors, up_bias, totals):
        rows = jnp.concatenate(vectors, 0)
        rows = rows.reshape(rows.shape[0], 16, 40).transpose(1, 0, 2)
        out = jnp.zeros((16, 16, 128), f32)
        out = lax.dynamic_update_slice(out, rows, (0, 0, 0))
        if up_bias is not None:
            out = lax.dynamic_update_slice(out, up_bias.reshape(16, 2, 96), (0, 8, 0))
        if totals is not None:
            out = lax.dynamic_update_slice(out, jnp.broadcast_to(totals, (16, 1, 8)), (0, 15, 0))
        return out

    g_ffn_d = ffn_grad(f_keep, f_recv, "decoder_ffn_grad")
    r_ffn_d = reduce_group(g_ffn_d, place, sign)

    dy_in, s_keep, s_send, s_vec = call(
        functools.partial(self_back_kernel, 0, 3, False), [SMEM, SMEM] + [VMEM] * 9,
        [act, pair, pair, arr(8, D)], 3 << 30, "self_backward", limit=40,
    )(sc, pick, dvec, da1, y, d_qkv, d_p, d_mixed, dmem, dec_triple, dec_output)
    s_recv = move(s_send, SWAP)

    choose = (jnp.arange(4) == group).astype(f32)
    totals = jnp.concatenate([choose * jnp.sum(src_lengths).astype(f32), choose * jnp.sum(tgt_lengths).astype(f32)])
    small_c = small_rows([f_vec[:3], c_vec[:5]], f_upb, totals)
    g_att_c = att_grad(c_keep, c_recv, small_c, "cross_grad")
    r_att_c = reduce_group(g_att_c, place, sign)

    dmid, h_keep, h_send, h_vec, h_upb = call(
        encoder_ffn_back_kernel, [SMEM, SMEM] + [VMEM] * 5 + [ANY] * 2,
        [act, arr(T, D + FF), arr(T, D + FF), arr(8, D), arr(1, FF)], 4 << 30, "encoder_ffn_backward",
        [vmem((D, FF), bf16), vmem((FF, D), bf16), vmem((2 * T, D), bf16), vmem((T, D), f32),
         pltpu.SemaphoreType.DMA((2,))],
    )(sc, pick, evec, e_cot, dmem, e_mid, e_z, enc_up, enc_down)
    h_recv = move(h_send, SWAP)

    small_s = small_rows([s_vec[:5]], None, None)
    g_att_s = att_grad(s_keep, s_recv, small_s, "self_grad")
    r_att_s = reduce_group(g_att_s, place, sign)

    dx_in, e_keep, e_send, e_vec = call(
        functools.partial(self_back_kernel, 0, 2, True), [SMEM, SMEM] + [VMEM] * 9,
        [act, pair, pair, arr(8, D)], 3 << 30, "encoder_attention_backward", limit=40,
    )(sc, pick, evec, dmid, x, e_qkv, e_p, e_mixed, dmem, enc_triple, enc_output)
    e_recv = move(e_send, SWAP)

    g_ffn_e = ffn_grad(h_keep, h_recv, "encoder_ffn_grad")
    r_ffn_e = reduce_group(g_ffn_e, place, sign)
    small_e = small_rows([h_vec[:3], e_vec[:5]], h_upb, None)
    g_att_e = att_grad(e_keep, e_recv, small_e, "encoder_attention_grad")
    r_att_e = reduce_group(g_att_e, place, sign)

    def finish_ffn(r):
        up = r.reshape(24, 2, 20, 128)
        down = r.reshape(2, 480, 128)
        up_mine = lax.dynamic_index_in_dim(up, core, 1, keepdims=False).reshape(480, 128)
        up_other = lax.dynamic_index_in_dim(up, 1 - core, 1, keepdims=False).reshape(480, 128)
        down_mine = lax.dynamic_index_in_dim(down, core, 0, keepdims=False)
        down_other = lax.dynamic_index_in_dim(down, 1 - core, 0, keepdims=False)
        got = move(jnp.where(core == 0, up_other, down_other), SWAP)
        up = jnp.where(core == 0, up_mine, got)
        down = jnp.where(core == 0, got, down_mine)
        up = up.reshape(24, 20, 128).transpose(1, 0, 2).reshape(20, FF)
        down = down.reshape(6, 5, 16, 128).transpose(0, 2, 1, 3).reshape(96, D)
        return up, down

    def finish_att(r):
        big = r[:400].reshape(2, 5, 2, 20, 128)
        mine = lax.dynamic_index_in_dim(big, core, 2, keepdims=False)
        other = lax.dynamic_index_in_dim(big, 1 - core, 2, keepdims=False).reshape(200, 128)
        got = move(jnp.concatenate([other, r[400:]], 0), SWAP)
        small = r[400:] + got[200:]
        got = got[:200].reshape(2, 5, 20, 128)
        jobs = []
        for first in (True, False):
            job = jnp.where((core == 0) == first, mine, got)
            jobs.append(job.transpose(0, 2, 1, 3).reshape(2, 20, D))
        vectors = lax.dynamic_slice(small, (0, core * 20), (8, 20)).T
        up_bias = lax.dynamic_slice(small, (8 + core, 0), (1, 96))[0]
        return jobs, vectors, up_bias, small

    d_up, d_down = finish_ffn(r_ffn_d)
    e_up, e_down = finish_ffn(r_ffn_e)
    (c0, c1), c_small, d_up_b, extra = finish_att(r_att_c)
    (s0, s1), s_small, _, _ = finish_att(r_att_s)
    (e0, e1), e_small, e_up_b, _ = finish_att(r_att_e)
    src_total, tgt_total = extra[15, :4], extra[15, 4:8]

    rows_model = pos * 20 + jnp.arange(20)
    rows_hidden = pos * 96 + jnp.arange(96)
    limits = {"keep": configs[:, 0], "head": configs[:, 1] * HD, "ffn": configs[:, 2]}

    def scaled(grad, row_kind, col_kind, total, period=None):
        rows = rows_hidden if row_kind == "ffn" else rows_model
        usage = 0.0
        for g in range(4):
            ok = (rows < limits[row_kind][g])[:, None]
            if col_kind is not None:
                cols = jnp.arange(grad.shape[1])
                if period is not None:
                    cols = cols % period
                ok = ok & (cols < limits[col_kind][g])[None]
            usage = usage + jnp.where(ok, total[g], 0.0)
        return grad * lax.rsqrt(usage)

    def columns(block, kinds, total):
        return jnp.concatenate([scaled(block[:, i:i + 1], k, None, total) for i, k in kinds], 1)

    enc_out = (
        columns(e_small, ((3, "keep"), (0, "keep")), src_total),
        columns(e_small, ((4, "keep"), (1, "keep")), src_total),
        scaled(jnp.concatenate([e0[0], e0[1], e1[0]], 1), "keep", "head", src_total, D),
        scaled(e1[1], "head", "keep", src_total),
        columns(e_small, ((5, "head"), (6, "head"), (7, "keep"), (2, "keep")), src_total),
        scaled(e_up, "keep", "ffn", src_total),
        scaled(e_up_b[:, None], "ffn", None, src_total)[:, 0],
        scaled(e_down, "ffn", "keep", src_total),
    )
    dec_biases_grad = jnp.concatenate(
        [
            columns(s_small, ((2, "head"), (3, "head"), (4, "keep")), tgt_total),
            columns(c_small, ((5, "head"), (6, "head"), (7, "keep"), (2, "keep")), tgt_total),
        ],
        1,
    )
    dec_out = (
        jnp.concatenate(
            [columns(s_small, ((0, "keep"),), tgt_total), columns(c_small, ((3, "keep"), (0, "keep")), tgt_total)], 1),
        jnp.concatenate(
            [columns(s_small, ((1, "keep"),), tgt_total), columns(c_small, ((4, "keep"), (1, "keep")), tgt_total)], 1),
        scaled(jnp.concatenate([s0[0], s0[1], s1[0]], 1), "keep", "head", tgt_total, D),
        scaled(s1[1], "head", "keep", tgt_total),
        scaled(c1[0], "keep", "head", tgt_total),
        scaled(jnp.concatenate([c0[0], c0[1]], 1), "keep", "head", tgt_total, D),
        scaled(c1[1], "head", "keep", tgt_total),
        dec_biases_grad,
        scaled(d_up, "keep", "ffn", tgt_total),
        scaled(d_up_b[:, None], "ffn", None, tgt_total)[:, 0],
        scaled(d_down, "ffn", "keep", tgt_total),
    )
    whole = (1, SENT, LEN, D)
    return (
        (encoded.reshape(whole), decoded.reshape(whole), dx_in.reshape(whole), dprev.reshape(whole),
         dy_in.reshape(whole)) + enc_out + dec_out
    )


def solution(mesh):
    acts = P("sub", "dp", None, None)
    counts = P("sub", "dp")
    row, vector = P("dp", None), P("dp")
    in_specs = (acts,) * 5 + (counts,) * 2 + (P(),) * 20
    out_specs = (acts,) * 5 + (row,) * 6 + (vector, row) + (row,) * 9 + (vector, row)
    return jax.shard_map(per_device, mesh=mesh, in_specs=in_specs, out_specs=out_specs, check_vma=False)
```

```python
import functools
import math

import jax
import jax.numpy as jnp
from jax import lax
from jax.experimental import pallas as pl
from jax.experimental.pallas import tpu as pltpu
from jax.sharding import PartitionSpec as P

D = 640
H = 8
FF = 3072
LEN = 128
HD = 80
SENT = 2
T = SENT * LEN
TILE = 512
ROWS_FFN = 960
ROWS_ATT = 416
f32 = jnp.float32
bf16 = jnp.bfloat16
NN = (((1,), (0,)), ((), ()))
NT = (((1,), (1,)), ((), ()))
TN = (((0,), (0,)), ((), ()))
MESH_AXES = ("sub", "dp")


def split(x):
    hi = x.astype(bf16)
    lo = (x - hi.astype(f32)).astype(bf16)
    return hi, lo


def stacked(x):
    return jnp.concatenate(split(x), 0)


def halves(r):
    n = r.shape[0] // 2
    return r[:n] + r[n:]


def mm(xs, w, dims=NN):
    return halves(lax.dot_general(xs, w, dims, preferred_element_type=f32))


def dot3(a, b, dims):
    ah, al = a
    bh, bl = b
    dg = functools.partial(lax.dot_general, dimension_numbers=dims, preferred_element_type=f32)
    return dg(al, bh) + dg(ah, bl) + dg(ah, bh)


def lane_mask(width, limit):
    return (lax.broadcasted_iota(jnp.int32, (1, width), 1) < limit).astype(f32)


def row_ok(len0, len1):
    row = lax.broadcasted_iota(jnp.int32, (T, 1), 0)
    limit = jnp.where(row < LEN, len0, LEN + len1)
    return (row < limit).astype(f32)


def norm(x, keep, width):
    mean = jnp.sum(x * keep, -1, keepdims=True) / width
    centred = (x - mean) * keep
    var = jnp.sum(centred * centred, -1, keepdims=True) / width
    rstd = lax.rsqrt(var + 1e-5)
    return centred * rstd, rstd


def norm_back(dy, n, rstd, gain, keep, width):
    dy = dy * keep
    dz = dy * gain
    m1 = jnp.sum(dz, -1, keepdims=True) / width
    m2 = jnp.sum(dz * n, -1, keepdims=True) / width
    dx = keep * rstd * (dz - m1 - n * m2)
    return dx, jnp.sum(dy * n, 0, keepdims=True), jnp.sum(dy, 0, keepdims=True)


def bell(z):
    cdf = 0.5 * (1.0 + lax.erf(z * (1.0 / math.sqrt(2.0))))
    pdf = jnp.exp(-0.5 * z * z) * (1.0 / math.sqrt(2.0 * math.pi))
    return cdf, pdf


def attend(q, k, v, lens, causal, p_ref):
    qs, ks, vs = split(q), split(k), split(v)
    col = lax.broadcasted_iota(jnp.int32, (LEN, LEN), 1)
    rows = []
    for s in range(SENT):
        allowed = col < lens[s]
        if causal:
            allowed = allowed & (lax.broadcasted_iota(jnp.int32, (LEN, LEN), 0) >= col)
        outs = []
        for h in range(H):
            def part(pair):
                return tuple(x[s * LEN:(s + 1) * LEN, h * HD:(h + 1) * HD] for x in pair)
            scores = dot3(part(qs), part(ks), NT) * (1.0 / math.sqrt(HD))
            scores = jnp.where(allowed, scores, -1e30)
            e = jnp.exp(scores - jnp.max(scores, -1, keepdims=True))
            prob = e / jnp.sum(e, -1, keepdims=True)
            p_ref[s * H + h] = prob
            outs.append(dot3(split(prob), part(vs), NN))
        rows.append(jnp.concatenate(outs, 1))
    return jnp.concatenate(rows, 0)


def attend_back(do, q, k, v, p_ref):
    dos, qs, ks, vs = split(do), split(q), split(k), split(v)
    all_q, all_k, all_v = [], [], []
    for s in range(SENT):
        dqs, dks, dvs = [], [], []
        for h in range(H):
            def part(pair):
                return tuple(x[s * LEN:(s + 1) * LEN, h * HD:(h + 1) * HD] for x in pair)
            prob = p_ref[s * H + h]
            dp = dot3(part(dos), part(vs), NT)
            ds = prob * (dp - jnp.sum(dp * prob, -1, keepdims=True)) * (1.0 / math.sqrt(HD))
            dss = split(ds)
            dvs.append(dot3(split(prob), part(dos), TN))
            dqs.append(dot3(dss, part(ks), NN))
            dks.append(dot3(dss, part(qs), TN))
        all_q.append(jnp.concatenate(dqs, 1))
        all_k.append(jnp.concatenate(dks, 1))
        all_v.append(jnp.concatenate(dvs, 1))
    return tuple(jnp.concatenate(x, 0) for x in (all_q, all_k, all_v))


def ffn_forward(ns, up, bias, down, ffn_limit, z_ref, acc_ref):
    acc_ref[...] = jnp.zeros_like(acc_ref)

    def body(j, _):
        sl = pl.ds(pl.multiple_of(j * TILE, TILE), TILE)
        z = mm(ns[...], up[:, sl]) + bias[:, sl].astype(f32)
        z_ref[:, sl] = z
        mask = (lax.broadcasted_iota(jnp.int32, (1, TILE), 1) + j * TILE < ffn_limit).astype(f32)
        u = z * bell(z)[0] * mask
        acc_ref[...] += mm(stacked(u), down[sl, :])
        return 0

    lax.fori_loop(0, FF // TILE, body, 0)


def ffn_backward(dyk, n, z_ref, up, down, ffn_limit, core, dys_ref, keep_ref, send_ref, bias_ref, acc_ref):
    acc_ref[...] = jnp.zeros_like(acc_ref)
    dys_ref[...] = stacked(dyk)
    first = core == 0
    keep_ref[:, :D] = jnp.where(first, n, dyk)
    send_ref[:, :D] = jnp.where(first, dyk, n)

    def body(j, _):
        sl = pl.ds(pl.multiple_of(j * TILE, TILE), TILE)
        out = pl.ds(pl.multiple_of(j * TILE + D, 128), TILE)
        du = mm(dys_ref[...], down[sl, :], NT)
        z = z_ref[:, sl]
        cdf, pdf = bell(z)
        mask = (lax.broadcasted_iota(jnp.int32, (1, TILE), 1) + j * TILE < ffn_limit).astype(f32)
        u = z * cdf * mask
        dz = du * mask * (cdf + z * pdf)
        keep_ref[:, out] = jnp.where(first, dz, u)
        send_ref[:, out] = jnp.where(first, u, dz)
        bias_ref[:, sl] = jnp.sum(dz, 0, keepdims=True)
        acc_ref[...] += mm(stacked(dz), up[:, sl], NT)
        return 0

    lax.fori_loop(0, FF // TILE, body, 0)


def load_vectors(*refs):
    return jnp.concatenate([ref[...].astype(f32) for ref in refs], 0)


def setting(cfg, src, tgt):
    g = lax.axis_index("sub")
    core = lax.axis_index("dp") & 1
    c = cfg[g, 3]
    bits = [(c & 1).astype(f32), ((c >> 1) & 1).astype(f32), ((c >> 2) & 1).astype(f32)]
    total = bits[0] + bits[1] + bits[2]
    sc = (cfg[g, 0], cfg[g, 1] * HD, cfg[g, 2], src[0, 0], src[0, 1], tgt[0, 0], tgt[0, 1], core)
    return sc, [b / total for b in bits]


def fetch(pairs, sems):
    copies = [pltpu.make_async_copy(a, b, sems.at[i]) for i, (a, b) in enumerate(pairs)]
    for c in copies:
        c.start()
    return copies


def encoder_kernel(cfg, src, tgt, v_gain, v_shift, v_bias, upb, x_ref, w_triple, w_out, w_up, w_down,
                   encoded, qkv, p_ref, mixed, middle, z_ref,
                   b_triple, b_out, b_up, b_down, ns_ref, acc_ref, sems):
    copies = fetch([(w_triple, b_triple), (w_out, b_out), (w_up, b_up), (w_down, b_down)], sems)
    sc, pick = setting(cfg, src, tgt)
    width = sc[0].astype(f32)
    keep, heads = lane_mask(D, sc[0]), lane_mask(D, sc[1])
    vec = load_vectors(v_gain, v_shift, v_bias)
    x = x_ref[...]
    n, _ = norm(x, keep, width)
    ns = stacked((n * vec[0:1] + vec[2:3]) * keep)
    copies[0].wait()
    qkv[:, :D] = (mm(ns, b_triple[:, :D]) + vec[4:5]) * heads
    qkv[:, D:2 * D] = mm(ns, b_triple[:, D:2 * D]) * heads
    qkv[:, 2 * D:] = (mm(ns, b_triple[:, 2 * D:]) + vec[5:6]) * heads
    o = attend(qkv[:, :D], qkv[:, D:2 * D], qkv[:, 2 * D:], (sc[3], sc[4]), False, p_ref)
    mixed[...] = o
    copies[1].wait()
    mid = x + (mm(stacked(o), b_out[...]) + vec[6:7]) * keep
    middle[...] = mid
    n, _ = norm(mid, keep, width)
    ns_ref[...] = stacked((n * vec[1:2] + vec[3:4]) * keep)
    copies[2].wait()
    copies[3].wait()
    ffn_forward(ns_ref, b_up, upb, b_down, sc[2], z_ref, acc_ref)
    encoded[...] = (mid + (acc_ref[...] + vec[7:8]) * keep) * row_ok(sc[3], sc[4])


def decoder_kernel(cfg, src, tgt, v_gain, v_shift, v_bias, upb, x_ref, prev_ref, src_ref, enc_ref, cot_ref,
                   w_triple, w_out, w_query, w_pair, w_cross, w_up, w_down,
                   decoded, qkv, p_self, mixed, a1_ref, mem_ref, qkv_c, p_cross, mixed_c, a2_ref, da2_ref,
                   keep_buf, send_buf, dvec, dupb,
                   b_triple, b_out, b_query, b_pair, b_cross, b_up, b_down, ns_ref, acc_ref, z_ref, sems):
    copies = fetch([(w_triple, b_triple), (w_out, b_out), (w_query, b_query), (w_pair, b_pair),
                    (w_cross, b_cross), (w_up, b_up), (w_down, b_down)], sems)
    sc, pick = setting(cfg, src, tgt)
    width = sc[0].astype(f32)
    keep, heads = lane_mask(D, sc[0]), lane_mask(D, sc[1])
    vec = load_vectors(v_gain, v_shift, v_bias)
    x = x_ref[...]
    n, _ = norm(x, keep, width)
    ns = stacked((n * vec[0:1] + vec[3:4]) * keep)
    copies[0].wait()
    qkv[:, :D] = (mm(ns, b_triple[:, :D]) + vec[6:7]) * heads
    qkv[:, D:2 * D] = mm(ns, b_triple[:, D:2 * D]) * heads
    qkv[:, 2 * D:] = (mm(ns, b_triple[:, 2 * D:]) + vec[7:8]) * heads
    o = attend(qkv[:, :D], qkv[:, D:2 * D], qkv[:, 2 * D:], (sc[5], sc[6]), True, p_self)
    mixed[...] = o
    copies[1].wait()
    a1 = x + (mm(stacked(o), b_out[...]) + vec[8:9]) * keep
    a1_ref[...] = a1
    n, _ = norm(a1, keep, width)
    ns = stacked((n * vec[1:2] + vec[4:5]) * keep)
    copies[2].wait()
    qkv_c[:, :D] = (mm(ns, b_query[...]) + vec[9:10]) * heads
    memory = (pick[0] * prev_ref[...] + pick[1] * src_ref[...] + pick[2] * enc_ref[...]) * keep
    mem_ref[...] = memory
    ns = stacked(memory)
    copies[3].wait()
    qkv_c[:, D:2 * D] = mm(ns, b_pair[:, :D]) * heads
    qkv_c[:, 2 * D:] = (mm(ns, b_pair[:, D:]) + vec[10:11]) * heads
    o = attend(qkv_c[:, :D], qkv_c[:, D:2 * D], qkv_c[:, 2 * D:], (sc[3], sc[4]), False, p_cross)
    mixed_c[...] = o
    copies[4].wait()
    a2_ref[...] = a1_ref[...] + (mm(stacked(o), b_cross[...]) + vec[11:12]) * keep
    n, _ = norm(a2_ref[...], keep, width)
    ns_ref[...] = stacked((n * vec[2:3] + vec[5:6]) * keep)
    copies[5].wait()
    copies[6].wait()
    ffn_forward(ns_ref, b_up, upb, b_down, sc[2], z_ref, acc_ref)
    ok = row_ok(sc[5], sc[6])
    decoded[...] = (a2_ref[...] + (acc_ref[...] + vec[12:13]) * keep) * ok
    dy = cot_ref[...] * ok
    dyk = dy * keep
    n, rstd = norm(a2_ref[...], keep, width)
    ffn_backward(dyk, (n * vec[2:3] + vec[5:6]) * keep, z_ref, b_up, b_down, sc[2], sc[7], ns_ref,
                 keep_buf, send_buf, dupb, acc_ref)
    dx, dg, db = norm_back(acc_ref[...], n, rstd, vec[2:3], keep, width)
    da2_ref[...] = dy + dx
    dvec[...] = jnp.concatenate([dg, db, jnp.sum(dyk, 0, keepdims=True), jnp.zeros((5, D), f32)], 0)


def cross_back_kernel(cfg, src, tgt, v_gain, v_shift, v_bias, da2_ref, a1_ref, mem_ref, qkv_c, p_cross, mixed_c,
                      w_query, w_pair, w_cross,
                      da1_ref, dmem_ref, dprev_ref, keep_buf, send_buf, dvec):
    sc, pick = setting(cfg, src, tgt)
    width = sc[0].astype(f32)
    keep, heads = lane_mask(D, sc[0]), lane_mask(D, sc[1])
    vec = load_vectors(v_gain, v_shift, v_bias)
    first = sc[7] == 0
    da2 = da2_ref[...]
    dyk = da2 * keep
    do = mm(stacked(dyk), w_cross[...], NT)
    dq, dk, dv = attend_back(do, qkv_c[:, :D], qkv_c[:, D:2 * D], qkv_c[:, 2 * D:], p_cross)
    dq, dk, dv = dq * heads, dk * heads, dv * heads
    n, rstd = norm(a1_ref[...], keep, width)
    normed = (n * vec[1:2] + vec[4:5]) * keep
    for i, (a, b) in enumerate(((mem_ref[...], normed), (mem_ref[...], mixed_c[...]), (dk, dq), (dv, dyk))):
        keep_buf[:, i * D:(i + 1) * D] = jnp.where(first, a, b)
        send_buf[:, i * D:(i + 1) * D] = jnp.where(first, b, a)
    dn = mm(stacked(dq), w_query[...], NT)
    dx, dg, db = norm_back(dn, n, rstd, vec[1:2], keep, width)
    da1_ref[...] = da2 + dx
    dmem = (mm(stacked(dk), w_pair[:, :D], NT) + mm(stacked(dv), w_pair[:, D:], NT)) * keep
    dmem_ref[...] = dmem
    dprev_ref[...] = dmem * pick[0]
    dvec[...] = jnp.concatenate(
        [dg, db] + [jnp.sum(t, 0, keepdims=True) for t in (dq, dv, dyk)] + [jnp.zeros((3, D), f32)], 0)


def self_back_kernel(gain_row, shift_row, with_memory, cfg, src, tgt, v_gain, v_shift, v_bias, dy_ref, x_ref, qkv, p_ref, mixed,
                     dmem_ref, w_triple, w_out, dx_ref, keep_buf, send_buf, dvec):
    sc, pick = setting(cfg, src, tgt)
    width = sc[0].astype(f32)
    keep, heads = lane_mask(D, sc[0]), lane_mask(D, sc[1])
    vec = load_vectors(v_gain, v_shift, v_bias)
    gain, shift = vec[gain_row:gain_row + 1], vec[shift_row:shift_row + 1]
    first = sc[7] == 0
    dy = dy_ref[...]
    dyk = dy * keep
    do = mm(stacked(dyk), w_out[...], NT)
    dq, dk, dv = attend_back(do, qkv[:, :D], qkv[:, D:2 * D], qkv[:, 2 * D:], p_ref)
    dq, dk, dv = dq * heads, dk * heads, dv * heads
    n, rstd = norm(x_ref[...], keep, width)
    normed = (n * gain + shift) * keep
    for i, (a, b) in enumerate(((normed, normed), (normed, mixed[...]), (dq, dv), (dk, dyk))):
        keep_buf[:, i * D:(i + 1) * D] = jnp.where(first, a, b)
        send_buf[:, i * D:(i + 1) * D] = jnp.where(first, b, a)
    dn = mm(stacked(dq), w_triple[:, :D], NT) + mm(stacked(dk), w_triple[:, D:2 * D], NT)
    dn += mm(stacked(dv), w_triple[:, 2 * D:], NT)
    dx, dg, db = norm_back(dn, n, rstd, gain, keep, width)
    dx = dx + dy
    if with_memory:
        dx = dx + pick[1] * dmem_ref[...]
    dx_ref[...] = dx
    dvec[...] = jnp.concatenate(
        [dg, db] + [jnp.sum(t, 0, keepdims=True) for t in (dq, dv, dyk)] + [jnp.zeros((3, D), f32)], 0)


def encoder_ffn_back_kernel(cfg, src, tgt, v_gain, v_shift, v_bias, cot_ref, dmem_ref, middle, z_ref, w_up, w_down,
                            dmid_ref, keep_buf, send_buf, dvec, dupb,
                            b_up, b_down, ns_ref, acc_ref, sems):
    copies = fetch([(w_up, b_up), (w_down, b_down)], sems)
    sc, pick = setting(cfg, src, tgt)
    width = sc[0].astype(f32)
    keep = lane_mask(D, sc[0])
    vec = load_vectors(v_gain, v_shift, v_bias)
    dy = (cot_ref[...] + pick[2] * dmem_ref[...]) * row_ok(sc[3], sc[4])
    dyk = dy * keep
    n, rstd = norm(middle[...], keep, width)
    copies[0].wait()
    copies[1].wait()
    ffn_backward(dyk, (n * vec[1:2] + vec[3:4]) * keep, z_ref, b_up, b_down, sc[2], sc[7], ns_ref,
                 keep_buf, send_buf, dupb, acc_ref)
    dx, dg, db = norm_back(acc_ref[...], n, rstd, vec[1:2], keep, width)
    dmid_ref[...] = dy + dx
    dvec[...] = jnp.concatenate([dg, db, jnp.sum(dyk, 0, keepdims=True), jnp.zeros((5, D), f32)], 0)


def ffn_grad_kernel(keep_buf, recv_buf, out, at_s, b_b, b_s, at_b):
    j = pl.program_id(0)
    first = (lax.axis_index("dp") & 1) == 0

    @pl.when(first & (j == 0))
    def _():
        for i, ref in enumerate((keep_buf, recv_buf)):
            hi, lo = split(ref[:, :D].T)
            at_s[0, :, i * T:(i + 1) * T] = hi
            at_s[1, :, i * T:(i + 1) * T] = lo

            def body(c, _):
                src = pl.ds(pl.multiple_of(c * TILE + D, 128), TILE)
                dst = pl.ds(pl.multiple_of(c * TILE, TILE), TILE)
                hi, lo = split(ref[:, src])
                b_b[0, i * T:(i + 1) * T, dst] = hi
                b_b[1, i * T:(i + 1) * T, dst] = lo
                return 0

            lax.fori_loop(0, FF // TILE, body, 0)

    @pl.when(jnp.logical_not(first) & (j == 0))
    def _():
        for i, ref in enumerate((keep_buf, recv_buf)):
            hi, lo = split(ref[:, :D])
            b_s[0, i * T:(i + 1) * T] = hi
            b_s[1, i * T:(i + 1) * T] = lo

            def body(c, _):
                x = ref[:, pl.ds(pl.multiple_of(c * 384 + D, 128), 384)].T
                hi, lo = split(x.reshape(2, 192, T))
                at_b[0, pl.ds(2 * c, 2), :, i * T:(i + 1) * T] = hi
                at_b[1, pl.ds(2 * c, 2), :, i * T:(i + 1) * T] = lo
                return 0

            lax.fori_loop(0, 8, body, 0)

    @pl.when(first)
    def _():
        cols = pl.ds(pl.multiple_of(j * 256, 256), 256)
        r = dot3((at_s[0], at_s[1]), (b_b[0, :, cols], b_b[1, :, cols]), NN)
        for c in range(2):
            out[:, c * 40:(c + 1) * 40, :] = r[:, c * 128:(c + 1) * 128].reshape(16, 40, 128)

    @pl.when(jnp.logical_not(first))
    def _():
        rows = pl.ds(pl.multiple_of(j * 16, 16), 16)
        a = tuple(at_b[i, :, rows, :].reshape(256, 2 * T) for i in range(2))
        r = dot3(a, (b_s[0], b_s[1]), NN)
        for c in range(5):
            out[:, c * 16:(c + 1) * 16, :] = r[:, c * 128:(c + 1) * 128].reshape(16, 16, 128)


def small_block(out, base, ffn_vec, att_vec, upb, counts, group):
    lane = lax.broadcasted_iota(jnp.int32, (1, 128), 1)
    totals = jnp.where(lane == group, counts[0], 0) + jnp.where(lane == group + 4, counts[1], 0)
    totals = totals.astype(f32)
    for b in range(16):
        out[b, base:base + 16, :] = jnp.zeros((16, 128), f32)
        if ffn_vec is not None:
            out[b, base:base + 3, :40] = ffn_vec[:3, b * 40:(b + 1) * 40]
        out[b, base + 3:base + 8, :40] = att_vec[:5, b * 40:(b + 1) * 40]
        if upb is not None:
            for c in range(2):
                out[b, base + 8 + c:base + 9 + c, :96] = upb[:, b * 192 + c * 96:b * 192 + (c + 1) * 96]
        out[b, base + 15:base + 16, :] = totals


def att_grad_kernel(with_ffn, *refs):
    src, tgt = refs[0], refs[1]
    whole, out, sem = refs[-3:]
    refs = list(refs[3:-3])
    group = lax.axis_index("sub")
    counts = (src[0, 0] + src[0, 1], tgt[0, 0] + tgt[0, 1])
    copies = []
    for n, ffn in enumerate(with_ffn):
        kept, got, att_vec = refs[:3]
        ffn_vec, upb = (refs[3], refs[4]) if ffn else (None, None)
        refs = refs[5 if ffn else 3:]
        base = n * ROWS_ATT
        small_block(out, base + 400, ffn_vec, att_vec, upb, counts, group)
        for i in range(2):
            a = jnp.concatenate([kept[:, i * D:(i + 1) * D].T, got[:, i * D:(i + 1) * D].T], 1)
            b = jnp.concatenate([kept[:, (i + 2) * D:(i + 3) * D], got[:, (i + 2) * D:(i + 3) * D]], 0)
            a, b = split(a), split(b)
            for c in range(5):
                r = dot3(a, tuple(t[:, c * 128:(c + 1) * 128] for t in b), NN)
                row = base + i * 200 + c * 40
                out[:, row:row + 40, :] = r.reshape(16, 40, 128)
        copy = pltpu.make_async_copy(
            out.at[:, pl.ds(base, ROWS_ATT), :], whole.at[:, pl.ds(ROWS_FFN + base, ROWS_ATT), :], sem.at[n])
        copy.start()
        copies.append(copy)
    for copy in copies:
        copy.wait()


def usage_scale(cfg, totals, row_kind, rows, col_kind, cols):
    limit = {"keep": lambda g: cfg[g, 0], "head": lambda g: cfg[g, 1] * HD, "ffn": lambda g: cfg[g, 2]}
    usage = 0.0
    for g in range(4):
        part = jnp.where(rows < limit[row_kind](g), totals[g], 0.0)
        if col_kind is not None:
            part = jnp.where(cols < limit[col_kind](g), part, 0.0)
        usage = usage + part
    return lax.rsqrt(usage)


def finish_kernel(is_dec, cfg, mine, other, *refs):
    whole = refs[-1]
    outs = refs[:-1]
    pos = lax.axis_index("dp")
    px = lax.axis_index("sub")
    core = pos & 1
    sign = 1 - 2 * core
    first = core == 0
    n, base = (448, 0) if is_dec else (344, 448)
    for k in range(4):
        for ref, owner, from_x in ((mine, core, (px - sign * k) & 3), (other, 1 - core, (px + sign * k) & 3)):
            start = pl.multiple_of(from_x * n, 8)
            whole[owner, pl.ds(start, n), :] = ref[k, base:base + n, :]

    def half(owner, row):
        return jnp.where(first, whole[owner, row:row + 20, :], whole[owner, row + 20:row + 40, :])

    smalls = [whole[0, base + 400:base + 416, :] + whole[1, base + 400:base + 416, :] for base in ((960, 1376) if is_dec else (960,))]
    lane0 = 4 if is_dec else 0
    totals = [smalls[0][15:16, lane0 + g:lane0 + g + 1] for g in range(4)]

    def iota(shape, dim):
        return lax.broadcasted_iota(jnp.int32, shape, dim)

    scale = functools.partial(usage_scale, cfg, totals)
    rows20 = pos * 20 + iota((20, 1), 0)
    rows96 = pos * 96 + iota((96, 1), 0)
    cols = iota((1, D), 1)
    keep_head = scale("keep", rows20, "head", cols)
    head_keep = scale("head", rows20, "keep", cols)
    keep_row = scale("keep", rows20, None, None)
    head_row = scale("head", rows20, None, None)
    keep_ffn = scale("keep", rows20, "ffn", iota((1, FF), 1))
    ffn_keep = scale("ffn", rows96, "keep", cols)

    def job(out, col, owner, base, i, factor):
        for c in range(5):
            out[:, col + c * 128:col + (c + 1) * 128] = (
                half(owner, base + i * 200 + c * 40) * factor[:, c * 128:(c + 1) * 128])

    def vector(small):
        t = small.T
        return jnp.where(first, t[:20], t[20:40])

    def put(out, items):
        for i, (vec, k, factor) in enumerate(items):
            out[:, i:i + 1] = vec[:, k:k + 1] * factor

    if is_dec:
        gains, shifts, triple, output, query, pair, cross, biases, up, up_bias, down = outs
        c_vec, s_vec = vector(smalls[0]), vector(smalls[1])
        c, s = 960, 960 + 416
        put(gains, ((s_vec, 3, keep_row), (c_vec, 3, keep_row), (c_vec, 0, keep_row)))
        put(shifts, ((s_vec, 4, keep_row), (c_vec, 4, keep_row), (c_vec, 1, keep_row)))
        put(biases, ((s_vec, 5, head_row), (s_vec, 6, head_row), (s_vec, 7, keep_row),
                     (c_vec, 5, head_row), (c_vec, 6, head_row), (c_vec, 7, keep_row), (c_vec, 2, keep_row)))
        job(query, 0, 1, c, 0, keep_head)
        job(pair, 0, 0, c, 0, keep_head)
        job(pair, D, 0, c, 1, keep_head)
        job(cross, 0, 1, c, 1, head_keep)
    else:
        gains, shifts, triple, output, biases, up, up_bias, down = outs
        s_vec, s = vector(smalls[0]), 960
        put(gains, ((s_vec, 3, keep_row), (s_vec, 0, keep_row)))
        put(shifts, ((s_vec, 4, keep_row), (s_vec, 1, keep_row)))
        put(biases, ((s_vec, 5, head_row), (s_vec, 6, head_row), (s_vec, 7, keep_row), (s_vec, 2, keep_row)))
    job(triple, 0, 0, s, 0, keep_head)
    job(triple, D, 0, s, 1, keep_head)
    job(triple, 2 * D, 1, s, 0, keep_head)
    job(output, 0, 1, s, 1, head_keep)
    for c in range(24):
        up[:, c * 128:(c + 1) * 128] = half(0, c * 40) * keep_ffn[:, c * 128:(c + 1) * 128]
    for j in range(6):
        for c in range(5):
            start = pl.multiple_of(core * 480 + (j * 80 + c * 16), 16)
            down[j * 16:(j + 1) * 16, c * 128:(c + 1) * 128] = (
                whole[1, pl.ds(start, 16), :] * ffn_keep[j * 16:(j + 1) * 16, c * 128:(c + 1) * 128])
    bias_row = jnp.where(first, smalls[0][8:9, :96], smalls[0][9:10, :96])
    up_bias[...] = bias_row * scale("ffn", pos * 96 + iota((1, 96), 1), None, None)


SMEM = pl.BlockSpec(memory_space=pltpu.SMEM)
VMEM = pl.BlockSpec(memory_space=pltpu.VMEM)
ANY = pl.BlockSpec(memory_space=pl.ANY)


def arr(*shape):
    return jax.ShapeDtypeStruct(shape, f32)


def call(kernel, in_specs, outs, name, scratch=(), limit=56):
    return pl.pallas_call(
        kernel,
        in_specs=in_specs,
        out_shape=outs,
        out_specs=[VMEM] * len(outs),
        scratch_shapes=list(scratch),
        name=name,
        compiler_params=pltpu.CompilerParams(vmem_limit_bytes=limit << 20),
        cost_estimate=pl.CostEstimate(flops=1 << 20, bytes_accessed=1 << 20, transcendentals=0),
    )


def flat_perm(move):
    pairs = []
    for x in range(4):
        for y in range(4):
            for z in range(4):
                for c in range(2):
                    X, Y, Z, C = move(x, y, z, c)
                    pairs.append((x * 32 + y * 8 + z * 2 + c, (X % 4) * 32 + (Y % 4) * 8 + (Z % 4) * 2 + C % 2))
    return pairs


SWAP = flat_perm(lambda x, y, z, c: (x, y, z, 1 - c))
RING = {
    "x": flat_perm(lambda x, y, z, c: (x + 1 - 2 * c, y, z, c)),
    "y": flat_perm(lambda x, y, z, c: (x, y + 1 - 2 * c, z, c)),
    "z": flat_perm(lambda x, y, z, c: (x, y, z + 1 - 2 * c, c)),
}
HOP_X = [flat_perm(lambda x, y, z, c, k=k: (x + k - 2 * c * k, y, z, c)) for k in range(4)]


def turn(p, c):
    return p + (1 - 2 * c) * (1 - 2 * (p & 1))


PAIR = {
    "x": (flat_perm(lambda x, y, z, c: (turn(x, c), y, z, c)), flat_perm(lambda x, y, z, c: (x + 2, y, z, c))),
    "y": (flat_perm(lambda x, y, z, c: (x, turn(y, c), z, c)), flat_perm(lambda x, y, z, c: (x, y + 2, z, c))),
    "z": (flat_perm(lambda x, y, z, c: (x, y, turn(z, c), c)), flat_perm(lambda x, y, z, c: (x, y, z + 2, c))),
}


def move(x, perm):
    return lax.ppermute(x, MESH_AXES, perm)


def barrier(*trees):
    return lax.optimization_barrier(trees)


class Part:
    def __init__(self, array, rows, order, dims):
        self.array, self.rows, self.order, self.dims = array, rows, list(order), list(dims)
        self.step, self.got = 0, []

    @property
    def size(self):
        return self.rows[1] - self.rows[0]


def advance(parts, name):
    inputs = []

    def slot(array):
        for n, a in enumerate(inputs):
            if a is array:
                return n
        inputs.append(array)
        return len(inputs) - 1

    plans, routes, out_shapes = [], {}, []
    for part in parts:
        axis = part.order[0]
        d = part.dims.index(axis)
        plan = dict(src=slot(part.array), rows=part.rows, d=d, axis=axis, step=part.step, nd=len(part.dims),
                    got=[(slot(a), off) for a, off in part.got], m=part.size)
        if part.step == 2:
            plan["out"] = len(out_shapes)
            out_shapes.append((4,) * (len(part.dims) - 1) + (part.size, 128))
            if len(part.order) > 1:
                plan["next_axis"] = part.order[1]
                rest = [t for t in part.dims if t != axis]
                plan["next_d"] = rest.index(part.order[1])
        plans.append(plan)
        send_axis, kind = (axis, part.step) if part.step < 2 else (plan.get("next_axis"), 0)
        if send_axis is not None:
            nd = plan["nd"] if part.step < 2 else plan["nd"] - 1
            chunk_rows = 4 ** (nd - 1) * part.size
            route = routes.setdefault((send_axis, kind), [0, []])
            plan["route"], plan["offset"], plan["chunk"] = (send_axis, kind), route[0], chunk_rows
            route[0] += chunk_rows * (2 if kind == 0 else 1)
    n_state = len(out_shapes)
    route_list = list(routes)
    out_shapes += [(routes[r][0], 128) for r in route_list]
    n_in = len(inputs)

    def kernel(*refs):
        ins, outs = refs[:n_in], refs[n_in:]
        pos = lax.axis_index("dp")
        core = pos & 1
        place = {"x": lax.axis_index("sub"), "y": pos >> 3, "z": (pos >> 1) & 3}

        def chunk(ref, nd, d, k, rows):
            index = [slice(None)] * nd
            index[d] = k & 3
            return ref[tuple(index) + (slice(*rows), slice(None))].reshape(-1, 128)

        for plan in plans:
            src, nd, d, rows, m = ins[plan["src"]], plan["nd"], plan["d"], plan["rows"], plan["m"]
            p = place[plan["axis"]]
            n = 4 ** (nd - 1) * m
            got = [(ins[i], off) for i, off in plan["got"]]
            out = outs[n_state + route_list.index(plan["route"])] if "route" in plan else None
            off = plan.get("offset")
            if plan["step"] == 0:
                q = turn(p, core)
                out[off:off + n, :] = chunk(src, nd, d, q, rows)
                out[off + n:off + 2 * n, :] = chunk(src, nd, d, q + 2, rows)
            elif plan["step"] == 1:
                (a, a_off), = got
                out[off:off + n, :] = chunk(src, nd, d, p + 2, rows) + a[a_off + n:a_off + 2 * n, :]
            else:
                (a, a_off), (b, b_off) = got
                total = chunk(src, nd, d, p, rows) + a[a_off:a_off + n, :] + b[b_off:b_off + n, :]
                state = outs[plan["out"]]
                state[...] = total.reshape(state.shape)
                if out is not None:
                    nn = plan["chunk"]
                    q = turn(place[plan["next_axis"]], core)
                    out[off:off + nn, :] = chunk(state, nd - 1, plan["next_d"], q, (0, m))
                    out[off + nn:off + 2 * nn, :] = chunk(state, nd - 1, plan["next_d"], q + 2, (0, m))

    outs = call(kernel, [VMEM] * n_in, [arr(*t) for t in out_shapes], name, limit=24)(*inputs)
    sent = {r: move(outs[n_state + i], PAIR[r[0]][r[1]]) for i, r in enumerate(route_list)}
    for part, plan in zip(parts, plans):
        if part.step == 2:
            part.array, part.rows = outs[plan["out"]], (0, part.size)
            part.dims.remove(part.order.pop(0))
            part.step, part.got = 0, []
        if "route" in plan:
            part.got.append((plan["route"], plan["offset"]))
            part.step += 1
    return sent


def land(parts, sent):
    for part in parts:
        part.got = [(sent[a], off) if isinstance(a, tuple) else (a, off) for a, off in part.got]


def per_device(
    enc_in, prev_enc, dec_in, enc_cotan, dec_cotan, src_lengths, tgt_lengths, configs,
    enc_gains, enc_shifts, enc_triple, enc_output, enc_biases, enc_up, enc_up_bias, enc_down,
    dec_gains, dec_shifts, dec_triple, dec_output, dec_cross_query, dec_cross_pair, dec_cross_out,
    dec_biases, dec_up, dec_up_bias, dec_down,
):
    group = lax.axis_index("sub")
    pos = lax.axis_index("dp")
    core = pos & 1
    place = {"x": group, "y": pos >> 3, "z": (pos >> 1) & 3}
    sign = 1 - 2 * core
    e_upb = enc_up_bias.reshape(1, FF)
    d_upb = dec_up_bias.reshape(1, FF)
    x, prev, y = enc_in.reshape(T, D), prev_enc.reshape(T, D), dec_in.reshape(T, D)
    e_cot, d_cot = enc_cotan.reshape(T, D), dec_cotan.reshape(T, D)
    act, act3, prob = arr(T, D), arr(T, 3 * D), arr(2 * H, LEN, LEN)
    vmem = pltpu.VMEM
    scalars = (configs, src_lengths, tgt_lengths)
    e_vec = (enc_gains.T, enc_shifts.T, enc_biases.T)
    d_vec = (dec_gains.T, dec_shifts.T, dec_biases.T)
    head = [SMEM] * 3 + [VMEM] * 3

    encoded, e_qkv, e_p, e_mixed, e_mid, e_z = call(
        encoder_kernel, head + [VMEM, VMEM] + [ANY] * 4,
        [act, act3, prob, act, act, arr(T, FF)], "encoder_forward",
        [vmem((D, 3 * D), bf16), vmem((D, D), bf16), vmem((D, FF), bf16), vmem((FF, D), bf16),
         vmem((2 * T, D), bf16), vmem((T, D), f32), pltpu.SemaphoreType.DMA((4,))], limit=24,
    )(*scalars, *e_vec, e_upb, x, enc_triple, enc_output, enc_up, enc_down)

    (decoded, d_qkv, d_p, d_mixed, a1, mem, c_qkv, c_p, c_mixed, a2, da2, f_keep, f_send, f_vec, f_upb) = call(
        decoder_kernel, head + [VMEM] * 6 + [ANY] * 7,
        [act, act3, prob, act, act, act, act3, prob, act, act, act,
         arr(T, D + FF), arr(T, D + FF), arr(8, D), arr(1, FF)], "decoder_forward",
        [vmem((D, 3 * D), bf16), vmem((D, D), bf16), vmem((D, D), bf16), vmem((D, 2 * D), bf16),
         vmem((D, D), bf16), vmem((D, FF), bf16), vmem((FF, D), bf16),
         vmem((2 * T, D), bf16), vmem((T, D), f32), vmem((T, FF), f32), pltpu.SemaphoreType.DMA((7,))], limit=32,
    )(*scalars, *d_vec, d_upb, y, prev, x, encoded, d_cot,
      dec_triple, dec_output, dec_cross_query, dec_cross_pair, dec_cross_out, dec_up, dec_down)

    def ffn_grad(kept, got, rows, name):
        whole = pl.BlockSpec((T, D + FF), lambda j: (0, 0), pipeline_mode=pl.Buffered(1))
        return pl.pallas_call(
            ffn_grad_kernel,
            grid=(12,),
            in_specs=[whole, whole],
            out_shape=arr(16, rows, 128),
            out_specs=pl.BlockSpec((16, 80, 128), lambda j: (0, j, 0)),
            scratch_shapes=[vmem((2, D, 2 * T), bf16), vmem((2, 2 * T, FF), bf16), vmem((2, 2 * T, D), bf16),
                            vmem((2, 16, 192, 2 * T), bf16)],
            name=name,
            compiler_params=pltpu.CompilerParams(vmem_limit_bytes=22 << 20),
            cost_estimate=pl.CostEstimate(flops=1 << 20, bytes_accessed=1 << 20, transcendentals=0),
        )(kept, got)

    def att_grad(with_ffn, whole, operands, name):
        n = len(with_ffn)
        return pl.pallas_call(
            functools.partial(att_grad_kernel, with_ffn),
            in_specs=[SMEM, SMEM, ANY] + [VMEM] * len(operands),
            out_shape=arr(*whole.shape),
            out_specs=ANY,
            scratch_shapes=[vmem((16, ROWS_ATT * n, 128), f32), pltpu.SemaphoreType.DMA((n,))],
            input_output_aliases={2: 0},
            name=name,
            compiler_params=pltpu.CompilerParams(vmem_limit_bytes=24 << 20),
            cost_estimate=pl.CostEstimate(flops=1 << 20, bytes_accessed=1 << 20, transcendentals=0),
        )(src_lengths, tgt_lengths, whole, *operands)

    pair = arr(T, 4 * D)
    f_recv = move(f_send, SWAP)
    da1, dmem, dprev, c_keep, c_send, c_vec = call(
        cross_back_kernel, head + [VMEM] * 9, [act, act, act, pair, pair, arr(8, D)], "cross_backward", limit=12,
    )(*scalars, *d_vec, da2, a1, mem, c_qkv, c_p, c_mixed, dec_cross_query, dec_cross_pair, dec_cross_out)
    c_recv = move(c_send, SWAP)
    dy_in, s_keep, s_send, s_vec = call(
        functools.partial(self_back_kernel, 0, 3, False), head + [VMEM] * 8,
        [act, pair, pair, arr(8, D)], "self_backward", limit=12,
    )(*scalars, *d_vec, da1, y, d_qkv, d_p, d_mixed, dmem, dec_triple, dec_output)
    f_recv, s_send, s_keep, c_recv, dmem = barrier(f_recv, s_send, s_keep, c_recv, dmem)
    s_recv = move(s_send, SWAP)
    g_d = ffn_grad(f_keep, f_recv, ROWS_FFN + 2 * ROWS_ATT, "decoder_ffn_grad")
    g_d, s_recv = barrier(g_d, s_recv)
    g_d = att_grad((True, False), g_d, (c_keep, c_recv, c_vec, f_vec, f_upb, s_keep, s_recv, s_vec),
                   "decoder_attention_grad")
    cores = [[2 * i + c for i in range(16)] for c in range(2)]
    g_d, dmem = barrier(g_d, dmem)
    r_d = lax.psum_scatter(g_d, "dp", scatter_dimension=0, axis_index_groups=cores, tiled=True)

    dmid, h_keep, h_send, h_vec, h_upb = call(
        encoder_ffn_back_kernel, head + [VMEM] * 4 + [ANY] * 2,
        [act, arr(T, D + FF), arr(T, D + FF), arr(8, D), arr(1, FF)], "encoder_ffn_backward",
        [vmem((D, FF), bf16), vmem((FF, D), bf16), vmem((2 * T, D), bf16), vmem((T, D), f32),
         pltpu.SemaphoreType.DMA((2,))], limit=20,
    )(*scalars, *e_vec, e_cot, dmem, e_mid, e_z, enc_up, enc_down)
    h_recv = move(h_send, SWAP)
    dx_in, e_keep, e_send, e_vec_sum = call(
        functools.partial(self_back_kernel, 0, 2, True), head + [VMEM] * 8,
        [act, pair, pair, arr(8, D)], "encoder_attention_backward", limit=12,
    )(*scalars, *e_vec, dmid, x, e_qkv, e_p, e_mixed, dmem, enc_triple, enc_output)
    h_recv, e_send, e_keep = barrier(h_recv, e_send, e_keep)
    e_recv = move(e_send, SWAP)
    g_e = ffn_grad(h_keep, h_recv, ROWS_FFN + ROWS_ATT, "encoder_ffn_grad")
    g_e, e_recv = barrier(g_e, e_recv)
    g_e = att_grad((True,), g_e, (e_keep, e_recv, e_vec_sum, h_vec, h_upb), "encoder_attention_grad")

    g_e = g_e.reshape(4, 4, 4, 344, 128)
    enc_parts = [Part(g_e, rows, order, "yzx")
                 for rows, order in (((0, 120), "xyz"), ((120, 232), "yzx"), ((232, 344), "zxy"))]
    dec_parts = []
    for phase in range(7):
        if phase == 4:
            dec_parts = [Part(r_d.reshape(4, 448, 128), (0, 448), "x", "x")]
        active = enc_parts + dec_parts
        sent = advance(active, "step_%d" % phase)
        if sent:
            keys = list(sent)
            land(active, dict(zip(keys, barrier(*[sent[k] for k in keys]))))

    own = jnp.concatenate([p.array for p in dec_parts + enc_parts], 0)
    mine = jnp.stack([own] + [move(own, HOP_X[k]) for k in (1, 2, 3)], 0)
    other = move(mine, SWAP)

    def finish(is_dec, shapes, name):
        rows = 1792 if is_dec else 1376
        return call(
            functools.partial(finish_kernel, is_dec), [SMEM, VMEM, VMEM], [arr(*s) for s in shapes], name,
            [vmem((2, rows, 128), f32)], limit=16,
        )(configs, mine, other)

    dec_final = finish(True, (
        (20, 3), (20, 3), (20, 3 * D), (20, D), (20, D), (20, 2 * D), (20, D), (20, 7), (20, FF), (1, 96), (96, D)),
        "decoder_finish")
    enc_final = finish(False, (
        (20, 2), (20, 2), (20, 3 * D), (20, D), (20, 4), (20, FF), (1, 96), (96, D)), "encoder_finish")
    enc_final = [t.reshape(96) if t.shape == (1, 96) else t for t in enc_final]
    dec_final = [t.reshape(96) if t.shape == (1, 96) else t for t in dec_final]
    whole = (1, SENT, LEN, D)
    return (
        (encoded.reshape(whole), decoded.reshape(whole), dx_in.reshape(whole), dprev.reshape(whole),
         dy_in.reshape(whole)) + tuple(enc_final) + tuple(dec_final)
    )


def solution(mesh):
    acts = P("sub", "dp", None, None)
    counts = P("sub", "dp")
    row, vector = P("dp", None), P("dp")
    in_specs = (acts,) * 5 + (counts,) * 2 + (P(),) * 20
    out_specs = (acts,) * 5 + (row,) * 6 + (vector, row) + (row,) * 9 + (vector, row)
    return jax.shard_map(per_device, mesh=mesh, in_specs=in_specs, out_specs=out_specs, check_vma=False)
```

```python
import functools
import math

import jax
import jax.numpy as jnp
from jax import lax
from jax.experimental import pallas as pl
from jax.experimental.pallas import tpu as pltpu
from jax.sharding import PartitionSpec as P

D = 640
H = 8
FF = 3072
LEN = 128
HD = 80
SENT = 2
T = SENT * LEN
TILE = 512
ROWS_FFN = 960
ROWS_ATT = 416
f32 = jnp.float32
bf16 = jnp.bfloat16
NN = (((1,), (0,)), ((), ()))
NT = (((1,), (1,)), ((), ()))
TN = (((0,), (0,)), ((), ()))
MESH_AXES = ("sub", "dp")


def split(x):
    hi = x.astype(bf16)
    lo = (x - hi.astype(f32)).astype(bf16)
    return hi, lo


def stacked(x):
    return jnp.concatenate(split(x), 0)


def halves(r):
    n = r.shape[0] // 2
    return r[:n] + r[n:]


def mm(xs, w, dims=NN):
    return halves(lax.dot_general(xs, w, dims, preferred_element_type=f32))


def dot3(a, b, dims):
    ah, al = a
    bh, bl = b
    dg = functools.partial(lax.dot_general, dimension_numbers=dims, preferred_element_type=f32)
    return dg(al, bh) + dg(ah, bl) + dg(ah, bh)


def lane_mask(width, limit):
    return (lax.broadcasted_iota(jnp.int32, (1, width), 1) < limit).astype(f32)


def row_ok(len0, len1):
    row = lax.broadcasted_iota(jnp.int32, (T, 1), 0)
    limit = jnp.where(row < LEN, len0, LEN + len1)
    return (row < limit).astype(f32)


def norm(x, keep, width):
    mean = jnp.sum(x * keep, -1, keepdims=True) / width
    centred = (x - mean) * keep
    var = jnp.sum(centred * centred, -1, keepdims=True) / width
    rstd = lax.rsqrt(var + 1e-5)
    return centred * rstd, rstd


def norm_back(dy, n, rstd, gain, keep, width):
    dy = dy * keep
    dz = dy * gain
    m1 = jnp.sum(dz, -1, keepdims=True) / width
    m2 = jnp.sum(dz * n, -1, keepdims=True) / width
    dx = keep * rstd * (dz - m1 - n * m2)
    return dx, jnp.sum(dy * n, 0, keepdims=True), jnp.sum(dy, 0, keepdims=True)


def bell(z):
    cdf = 0.5 * (1.0 + lax.erf(z * (1.0 / math.sqrt(2.0))))
    pdf = jnp.exp(-0.5 * z * z) * (1.0 / math.sqrt(2.0 * math.pi))
    return cdf, pdf


def rows_of(pair, s, repeat):
    return jnp.concatenate([pair[i][s * LEN:(s + 1) * LEN] for i in repeat], 0)


def head(x, h):
    return x[:, h * HD:(h + 1) * HD]


def corners(r):
    return (r[LEN:, LEN:] + r[LEN:, :LEN]) + (r[:LEN, LEN:] + r[:LEN, :LEN])


def three(x):
    hi, lo = split(x)
    return jnp.concatenate([hi, lo, hi], 1)


def dot(a, b, dims):
    return lax.dot_general(a, b, dims, preferred_element_type=f32)


def attend(q, k, v, lens, causal, p_ref):
    qs, ks, vs = split(q * (1.0 / math.sqrt(HD))), split(k), split(v)
    col = lax.broadcasted_iota(jnp.int32, (LEN, LEN), 1)
    for s in range(SENT):
        allowed = col < lens[s]
        if causal:
            allowed = allowed & (lax.broadcasted_iota(jnp.int32, (LEN, LEN), 0) >= col)
        q2, k2 = rows_of(qs, s, (0, 1)), rows_of(ks, s, (0, 1))
        for h in range(H):
            p_ref[s * H + h] = jnp.where(allowed, corners(dot(head(q2, h), head(k2, h), NT)), -1e30)
    for i in range(SENT * H):
        scores = p_ref[i]
        e = jnp.exp(scores - jnp.max(scores, -1, keepdims=True))
        p_ref[i] = e * (1.0 / jnp.sum(e, -1, keepdims=True))
    rows = []
    for s in range(SENT):
        v3 = rows_of(vs, s, (0, 0, 1))
        rows.append(jnp.concatenate([dot(three(p_ref[s * H + h]), head(v3, h), NN) for h in range(H)], 1))
    return jnp.concatenate(rows, 0)


def attend_back(do, q, k, v, p_ref, ds_ref):
    scale = 1.0 / math.sqrt(HD)
    dos, qs, ks, vs = split(do), split(q * scale), split(k * scale), split(v)
    for s in range(SENT):
        do2, v2 = rows_of(dos, s, (0, 1)), rows_of(vs, s, (0, 1))
        for h in range(H):
            ds_ref[s * H + h] = corners(dot(head(do2, h), head(v2, h), NT))
    for i in range(SENT * H):
        prob, dp = p_ref[i], ds_ref[i]
        ds_ref[i] = prob * (dp - jnp.sum(dp * prob, -1, keepdims=True))
    all_q, all_k, all_v = [], [], []
    for s in range(SENT):
        k3, q3, do3 = rows_of(ks, s, (0, 0, 1)), rows_of(qs, s, (0, 0, 1)), rows_of(dos, s, (0, 0, 1))
        ids = [(s * H + h, h) for h in range(H)]
        all_q.append(jnp.concatenate([dot(three(ds_ref[i]), head(k3, h), NN) for i, h in ids], 1))
        all_k.append(jnp.concatenate([dot(three(ds_ref[i].T), head(q3, h), NN) for i, h in ids], 1))
        all_v.append(jnp.concatenate([dot(three(p_ref[i].T), head(do3, h), NN) for i, h in ids], 1))
    return tuple(jnp.concatenate(x, 0) for x in (all_q, all_k, all_v))


def ffn_forward(ns, up, bias, down, ffn_limit, z_ref, acc_ref):
    acc_ref[...] = jnp.zeros_like(acc_ref)

    def body(j, _):
        sl = pl.ds(pl.multiple_of(j * TILE, TILE), TILE)
        z = mm(ns[...], up[:, sl]) + bias[:, sl].astype(f32)
        z_ref[:, sl] = z
        mask = (lax.broadcasted_iota(jnp.int32, (1, TILE), 1) + j * TILE < ffn_limit).astype(f32)
        u = z * bell(z)[0] * mask
        acc_ref[...] += mm(stacked(u), down[sl, :])
        return 0

    lax.fori_loop(0, FF // TILE, body, 0)


def ffn_backward(dyk, n, z_ref, up, down, ffn_limit, core, dys_ref, keep_ref, send_ref, bias_ref, acc_ref,
                 arrive=None):
    acc_ref[...] = jnp.zeros_like(acc_ref)
    dys_ref[...] = stacked(dyk)
    first = core == 0
    keep_ref[:, :D] = jnp.where(first, n, dyk)
    send_ref[:, :D] = jnp.where(first, dyk, n)

    def body(j, _):
        sl = pl.ds(pl.multiple_of(j * TILE, TILE), TILE)
        out = pl.ds(pl.multiple_of(j * TILE + D, 128), TILE)
        if arrive is not None:
            arrive(sl, j)
        du = mm(dys_ref[...], down[sl, :], NT)
        z = z_ref[:, sl]
        cdf, pdf = bell(z)
        mask = (lax.broadcasted_iota(jnp.int32, (1, TILE), 1) + j * TILE < ffn_limit).astype(f32)
        u = z * cdf * mask
        dz = du * mask * (cdf + z * pdf)
        keep_ref[:, out] = jnp.where(first, dz, u)
        send_ref[:, out] = jnp.where(first, u, dz)
        bias_ref[:, sl] = jnp.sum(dz, 0, keepdims=True)
        acc_ref[...] += mm(stacked(dz), up[:, sl], NT)
        return 0

    lax.fori_loop(0, FF // TILE, body, 0)


def load_vectors(*refs):
    return jnp.concatenate([ref[...].astype(f32) for ref in refs], 0)


def setting(cfg, src, tgt):
    g = lax.axis_index("sub")
    core = lax.axis_index("dp") & 1
    c = cfg[g, 3]
    bits = [(c & 1).astype(f32), ((c >> 1) & 1).astype(f32), ((c >> 2) & 1).astype(f32)]
    total = bits[0] + bits[1] + bits[2]
    sc = (cfg[g, 0], cfg[g, 1] * HD, cfg[g, 2], src[0, 0], src[0, 1], tgt[0, 0], tgt[0, 1], core)
    return sc, [b / total for b in bits]


def fetch(pairs, sems):
    copies = [pltpu.make_async_copy(a, b, sems.at[i]) for i, (a, b) in enumerate(pairs)]
    for c in copies:
        c.start()
    return copies


def encoder_kernel(cfg, src, tgt, v_gain, v_shift, v_bias, upb, x_ref, w_triple, w_out, w_up, w_down,
                   encoded, qkv, p_ref, mixed, middle, z_ref,
                   b_triple, b_out, b_up, b_down, ns_ref, acc_ref, sems):
    copies = fetch([(w_triple, b_triple), (w_out, b_out), (w_up, b_up), (w_down, b_down)], sems)
    sc, pick = setting(cfg, src, tgt)
    width = sc[0].astype(f32)
    keep, heads = lane_mask(D, sc[0]), lane_mask(D, sc[1])
    vec = load_vectors(v_gain, v_shift, v_bias)
    x = x_ref[...]
    n, _ = norm(x, keep, width)
    ns = stacked((n * vec[0:1] + vec[2:3]) * keep)
    copies[0].wait()
    qkv[:, :D] = (mm(ns, b_triple[:, :D]) + vec[4:5]) * heads
    qkv[:, D:2 * D] = mm(ns, b_triple[:, D:2 * D]) * heads
    qkv[:, 2 * D:] = (mm(ns, b_triple[:, 2 * D:]) + vec[5:6]) * heads
    o = attend(qkv[:, :D], qkv[:, D:2 * D], qkv[:, 2 * D:], (sc[3], sc[4]), False, p_ref)
    mixed[...] = o
    copies[1].wait()
    mid = x + (mm(stacked(o), b_out[...]) + vec[6:7]) * keep
    middle[...] = mid
    n, _ = norm(mid, keep, width)
    ns_ref[...] = stacked((n * vec[1:2] + vec[3:4]) * keep)
    copies[2].wait()
    copies[3].wait()
    ffn_forward(ns_ref, b_up, upb, b_down, sc[2], z_ref, acc_ref)
    encoded[...] = (mid + (acc_ref[...] + vec[7:8]) * keep) * row_ok(sc[3], sc[4])


def decoder_kernel(cfg, src, tgt, v_gain, v_shift, v_bias, upb, x_ref, prev_ref, src_ref, enc_ref, cot_ref,
                   w_triple, w_out, w_query, w_pair, w_cross, w_up, w_down,
                   decoded, qkv, p_self, mixed, a1_ref, mem_ref, qkv_c, p_cross, mixed_c, a2_ref, da2_ref,
                   keep_buf, send_buf, dvec, dupb,
                   b_triple, b_out, b_query, b_pair, b_cross, b_up, b_down, ns_ref, acc_ref, z_ref, sems):
    copies = fetch([(w_triple, b_triple), (w_out, b_out), (w_query, b_query), (w_pair, b_pair),
                    (w_cross, b_cross), (w_up, b_up), (w_down, b_down)], sems)
    sc, pick = setting(cfg, src, tgt)
    width = sc[0].astype(f32)
    keep, heads = lane_mask(D, sc[0]), lane_mask(D, sc[1])
    vec = load_vectors(v_gain, v_shift, v_bias)
    x = x_ref[...]
    n, _ = norm(x, keep, width)
    ns = stacked((n * vec[0:1] + vec[3:4]) * keep)
    copies[0].wait()
    qkv[:, :D] = (mm(ns, b_triple[:, :D]) + vec[6:7]) * heads
    qkv[:, D:2 * D] = mm(ns, b_triple[:, D:2 * D]) * heads
    qkv[:, 2 * D:] = (mm(ns, b_triple[:, 2 * D:]) + vec[7:8]) * heads
    o = attend(qkv[:, :D], qkv[:, D:2 * D], qkv[:, 2 * D:], (sc[5], sc[6]), True, p_self)
    mixed[...] = o
    copies[1].wait()
    a1 = x + (mm(stacked(o), b_out[...]) + vec[8:9]) * keep
    a1_ref[...] = a1
    n, _ = norm(a1, keep, width)
    ns = stacked((n * vec[1:2] + vec[4:5]) * keep)
    copies[2].wait()
    qkv_c[:, :D] = (mm(ns, b_query[...]) + vec[9:10]) * heads
    memory = (pick[0] * prev_ref[...] + pick[1] * src_ref[...] + pick[2] * enc_ref[...]) * keep
    mem_ref[...] = memory
    ns = stacked(memory)
    copies[3].wait()
    qkv_c[:, D:2 * D] = mm(ns, b_pair[:, :D]) * heads
    qkv_c[:, 2 * D:] = (mm(ns, b_pair[:, D:]) + vec[10:11]) * heads
    o = attend(qkv_c[:, :D], qkv_c[:, D:2 * D], qkv_c[:, 2 * D:], (sc[3], sc[4]), False, p_cross)
    mixed_c[...] = o
    copies[4].wait()
    a2_ref[...] = a1_ref[...] + (mm(stacked(o), b_cross[...]) + vec[11:12]) * keep
    n, _ = norm(a2_ref[...], keep, width)
    ns_ref[...] = stacked((n * vec[2:3] + vec[5:6]) * keep)
    copies[5].wait()
    copies[6].wait()
    ffn_forward(ns_ref, b_up, upb, b_down, sc[2], z_ref, acc_ref)
    ok = row_ok(sc[5], sc[6])
    decoded[...] = (a2_ref[...] + (acc_ref[...] + vec[12:13]) * keep) * ok
    dy = cot_ref[...] * ok
    dyk = dy * keep
    n, rstd = norm(a2_ref[...], keep, width)
    ffn_backward(dyk, (n * vec[2:3] + vec[5:6]) * keep, z_ref, b_up, b_down, sc[2], sc[7], ns_ref,
                 keep_buf, send_buf, dupb, acc_ref)
    dx, dg, db = norm_back(acc_ref[...], n, rstd, vec[2:3], keep, width)
    da2_ref[...] = dy + dx
    dvec[...] = jnp.concatenate([dg, db, jnp.sum(dyk, 0, keepdims=True), jnp.zeros((5, D), f32)], 0)


def cross_back_kernel(cfg, src, tgt, v_gain, v_shift, v_bias, da2_ref, a1_ref, mem_ref, qkv_c, p_cross, mixed_c,
                      w_query, w_pair, w_cross,
                      da1_ref, dmem_ref, dprev_ref, keep_buf, send_buf, dvec, ds_ref):
    sc, pick = setting(cfg, src, tgt)
    width = sc[0].astype(f32)
    keep, heads = lane_mask(D, sc[0]), lane_mask(D, sc[1])
    vec = load_vectors(v_gain, v_shift, v_bias)
    first = sc[7] == 0
    da2 = da2_ref[...]
    dyk = da2 * keep
    do = mm(stacked(dyk), w_cross[...], NT)
    dq, dk, dv = attend_back(do, qkv_c[:, :D], qkv_c[:, D:2 * D], qkv_c[:, 2 * D:], p_cross, ds_ref)
    dq, dk, dv = dq * heads, dk * heads, dv * heads
    n, rstd = norm(a1_ref[...], keep, width)
    normed = (n * vec[1:2] + vec[4:5]) * keep
    for i, (a, b) in enumerate(((mem_ref[...], normed), (mem_ref[...], mixed_c[...]), (dk, dq), (dv, dyk))):
        keep_buf[:, i * D:(i + 1) * D] = jnp.where(first, a, b)
        send_buf[:, i * D:(i + 1) * D] = jnp.where(first, b, a)
    dn = mm(stacked(dq), w_query[...], NT)
    dx, dg, db = norm_back(dn, n, rstd, vec[1:2], keep, width)
    da1_ref[...] = da2 + dx
    dmem = (mm(stacked(dk), w_pair[:, :D], NT) + mm(stacked(dv), w_pair[:, D:], NT)) * keep
    dmem_ref[...] = dmem
    dprev_ref[...] = dmem * pick[0]
    dvec[...] = jnp.concatenate(
        [dg, db] + [jnp.sum(t, 0, keepdims=True) for t in (dq, dv, dyk)] + [jnp.zeros((3, D), f32)], 0)


def self_back_kernel(gain_row, shift_row, with_memory, cfg, src, tgt, v_gain, v_shift, v_bias, dy_ref, x_ref, qkv, p_ref, mixed,
                     dmem_ref, w_triple, w_out, dx_ref, keep_buf, send_buf, dvec, ds_ref):
    sc, pick = setting(cfg, src, tgt)
    width = sc[0].astype(f32)
    keep, heads = lane_mask(D, sc[0]), lane_mask(D, sc[1])
    vec = load_vectors(v_gain, v_shift, v_bias)
    gain, shift = vec[gain_row:gain_row + 1], vec[shift_row:shift_row + 1]
    first = sc[7] == 0
    dy = dy_ref[...]
    dyk = dy * keep
    do = mm(stacked(dyk), w_out[...], NT)
    dq, dk, dv = attend_back(do, qkv[:, :D], qkv[:, D:2 * D], qkv[:, 2 * D:], p_ref, ds_ref)
    dq, dk, dv = dq * heads, dk * heads, dv * heads
    n, rstd = norm(x_ref[...], keep, width)
    normed = (n * gain + shift) * keep
    for i, (a, b) in enumerate(((normed, normed), (normed, mixed[...]), (dq, dv), (dk, dyk))):
        keep_buf[:, i * D:(i + 1) * D] = jnp.where(first, a, b)
        send_buf[:, i * D:(i + 1) * D] = jnp.where(first, b, a)
    dn = mm(stacked(dq), w_triple[:, :D], NT) + mm(stacked(dk), w_triple[:, D:2 * D], NT)
    dn += mm(stacked(dv), w_triple[:, 2 * D:], NT)
    dx, dg, db = norm_back(dn, n, rstd, gain, keep, width)
    dx = dx + dy
    if with_memory:
        dx = dx + pick[1] * dmem_ref[...]
    dx_ref[...] = dx
    dvec[...] = jnp.concatenate(
        [dg, db] + [jnp.sum(t, 0, keepdims=True) for t in (dq, dv, dyk)] + [jnp.zeros((3, D), f32)], 0)


def encoder_ffn_back_kernel(cfg, src, tgt, v_gain, v_shift, v_bias, cot_ref, dmem_ref, middle, z_ref, w_up, w_down,
                            dmid_ref, keep_buf, send_buf, dvec, dupb,
                            b_up, b_down, ns_ref, acc_ref, sems):
    def tile_copies(sl, j):
        return (pltpu.make_async_copy(w_down.at[sl, :], b_down.at[sl, :], sems.at[0, j]),
                pltpu.make_async_copy(w_up.at[:, sl], b_up.at[:, sl], sems.at[1, j]))

    for j in range(FF // TILE):
        for copy in tile_copies(pl.ds(j * TILE, TILE), j):
            copy.start()

    def arrive(sl, j):
        for copy in tile_copies(sl, j):
            copy.wait()

    sc, pick = setting(cfg, src, tgt)
    width = sc[0].astype(f32)
    keep = lane_mask(D, sc[0])
    vec = load_vectors(v_gain, v_shift, v_bias)
    dy = (cot_ref[...] + pick[2] * dmem_ref[...]) * row_ok(sc[3], sc[4])
    dyk = dy * keep
    n, rstd = norm(middle[...], keep, width)
    ffn_backward(dyk, (n * vec[1:2] + vec[3:4]) * keep, z_ref, b_up, b_down, sc[2], sc[7], ns_ref,
                 keep_buf, send_buf, dupb, acc_ref, arrive)
    dx, dg, db = norm_back(acc_ref[...], n, rstd, vec[1:2], keep, width)
    dmid_ref[...] = dy + dx
    dvec[...] = jnp.concatenate([dg, db, jnp.sum(dyk, 0, keepdims=True), jnp.zeros((5, D), f32)], 0)


def ffn_grad_kernel(keep_buf, recv_buf, out, at_s, b_b, b_s, at_b):
    j = pl.program_id(0)
    first = (lax.axis_index("dp") & 1) == 0

    @pl.when(first & (j == 0))
    def _():
        for i, ref in enumerate((keep_buf, recv_buf)):
            hi, lo = split(ref[:, :D].T)
            at_s[0, :, i * T:(i + 1) * T] = hi
            at_s[1, :, i * T:(i + 1) * T] = lo

            def body(c, _):
                src = pl.ds(pl.multiple_of(c * TILE + D, 128), TILE)
                dst = pl.ds(pl.multiple_of(c * TILE, TILE), TILE)
                hi, lo = split(ref[:, src])
                b_b[0, i * T:(i + 1) * T, dst] = hi
                b_b[1, i * T:(i + 1) * T, dst] = lo
                return 0

            lax.fori_loop(0, FF // TILE, body, 0)

    @pl.when(jnp.logical_not(first) & (j == 0))
    def _():
        for i, ref in enumerate((keep_buf, recv_buf)):
            hi, lo = split(ref[:, :D])
            b_s[0, i * T:(i + 1) * T] = hi
            b_s[1, i * T:(i + 1) * T] = lo

            def body(c, _):
                x = ref[:, pl.ds(pl.multiple_of(c * 384 + D, 128), 384)].T
                hi, lo = split(x.reshape(2, 192, T))
                at_b[0, pl.ds(2 * c, 2), :, i * T:(i + 1) * T] = hi
                at_b[1, pl.ds(2 * c, 2), :, i * T:(i + 1) * T] = lo
                return 0

            lax.fori_loop(0, 8, body, 0)

    @pl.when(first)
    def _():
        cols = pl.ds(pl.multiple_of(j * 256, 256), 256)
        r = dot3((at_s[0], at_s[1]), (b_b[0, :, cols], b_b[1, :, cols]), NN)
        for c in range(2):
            out[:, c * 40:(c + 1) * 40, :] = r[:, c * 128:(c + 1) * 128].reshape(16, 40, 128)

    @pl.when(jnp.logical_not(first))
    def _():
        rows = pl.ds(pl.multiple_of(j * 16, 16), 16)
        a = tuple(at_b[i, :, rows, :].reshape(256, 2 * T) for i in range(2))
        r = dot3(a, (b_s[0], b_s[1]), NN)
        for c in range(5):
            out[:, c * 16:(c + 1) * 16, :] = r[:, c * 128:(c + 1) * 128].reshape(16, 16, 128)


def small_block(out, base, ffn_vec, att_vec, upb, counts, group):
    lane = lax.broadcasted_iota(jnp.int32, (1, 128), 1)
    totals = jnp.where(lane == group, counts[0], 0) + jnp.where(lane == group + 4, counts[1], 0)
    totals = totals.astype(f32)
    for b in range(16):
        out[b, base:base + 16, :] = jnp.zeros((16, 128), f32)
        if ffn_vec is not None:
            out[b, base:base + 3, :40] = ffn_vec[:3, b * 40:(b + 1) * 40]
        out[b, base + 3:base + 8, :40] = att_vec[:5, b * 40:(b + 1) * 40]
        if upb is not None:
            for c in range(2):
                out[b, base + 8 + c:base + 9 + c, :96] = upb[:, b * 192 + c * 96:b * 192 + (c + 1) * 96]
        out[b, base + 15:base + 16, :] = totals


def att_grad_kernel(with_ffn, *refs):
    src, tgt = refs[0], refs[1]
    whole, out, sem = refs[-3:]
    refs = list(refs[3:-3])
    group = lax.axis_index("sub")
    counts = (src[0, 0] + src[0, 1], tgt[0, 0] + tgt[0, 1])
    copies = []
    for n, ffn in enumerate(with_ffn):
        kept, got, att_vec = refs[:3]
        ffn_vec, upb = (refs[3], refs[4]) if ffn else (None, None)
        refs = refs[5 if ffn else 3:]
        base = n * ROWS_ATT
        small_block(out, base + 400, ffn_vec, att_vec, upb, counts, group)
        for i in range(2):
            a = jnp.concatenate([kept[:, i * D:(i + 1) * D].T, got[:, i * D:(i + 1) * D].T], 1)
            b = jnp.concatenate([kept[:, (i + 2) * D:(i + 3) * D], got[:, (i + 2) * D:(i + 3) * D]], 0)
            a, b = split(a), split(b)
            for c in range(5):
                r = dot3(a, tuple(t[:, c * 128:(c + 1) * 128] for t in b), NN)
                row = base + i * 200 + c * 40
                out[:, row:row + 40, :] = r.reshape(16, 40, 128)
        copy = pltpu.make_async_copy(
            out.at[:, pl.ds(base, ROWS_ATT), :], whole.at[:, pl.ds(ROWS_FFN + base, ROWS_ATT), :], sem.at[n])
        copy.start()
        copies.append(copy)
    for copy in copies:
        copy.wait()


def usage_scale(cfg, totals, row_kind, rows, col_kind, cols):
    limit = {"keep": lambda g: cfg[g, 0], "head": lambda g: cfg[g, 1] * HD, "ffn": lambda g: cfg[g, 2]}
    usage = 0.0
    for g in range(4):
        part = jnp.where(rows < limit[row_kind](g), totals[g], 0.0)
        if col_kind is not None:
            part = jnp.where(cols < limit[col_kind](g), part, 0.0)
        usage = usage + part
    return lax.rsqrt(usage)


def finish_kernel(cfg, mine, other, *refs):
    whole = refs[-1]
    outs = refs[:-1]
    pos = lax.axis_index("dp")
    px = lax.axis_index("sub")
    core = pos & 1
    sign = 1 - 2 * core
    first = core == 0
    for k in range(4):
        for ref, owner, from_x in ((mine, core, (px - sign * k) & 3), (other, 1 - core, (px + sign * k) & 3)):
            for off, n, base in ((0, 448, 0), (448, 344, 1792)):
                start = pl.multiple_of(base + from_x * n, 8)
                whole[owner, pl.ds(start, n), :] = ref[k, off:off + n, :]

    def half(owner, row):
        return jnp.where(first, whole[owner, row:row + 20, :], whole[owner, row + 20:row + 40, :])

    def iota(shape, dim):
        return lax.broadcasted_iota(jnp.int32, shape, dim)

    cols = iota((1, D), 1)
    rows20, rows96 = pos * 20 + iota((20, 1), 0), pos * 96 + iota((96, 1), 0)
    lanes20, lanes96 = pos * 20 + iota((1, 20), 1), pos * 96 + iota((1, 96), 1)

    def job(out, col, owner, base, i, factor):
        for c in range(5):
            out[:, col + c * 128:col + (c + 1) * 128] = (
                half(owner, base + i * 200 + c * 40) * factor[:, c * 128:(c + 1) * 128])

    def small(base):
        both = whole[0, base + 400:base + 416, :] + whole[1, base + 400:base + 416, :]
        return both, jnp.where(first, both[:, :20], both[:, 20:40])

    def put(out, items):
        for i, (vec, k, factor) in enumerate(items):
            out[i:i + 1, :] = vec[k:k + 1, :] * factor

    c, s, a = 960, 960 + 416, 1792 + 960
    (c_all, c_vec), (_, s_vec), (a_all, a_vec) = small(c), small(s), small(a)
    for is_dec in (True, False):
        lane0 = 4 if is_dec else 0
        scale = functools.partial(usage_scale, cfg, [a_all[15:16, lane0 + g:lane0 + g + 1] for g in range(4)])
        keep_head = scale("keep", rows20, "head", cols)
        head_keep = scale("head", rows20, "keep", cols)
        keep_row = scale("keep", lanes20, None, None)
        head_row = scale("head", lanes20, None, None)
        keep_ffn = scale("keep", rows20, "ffn", iota((1, FF), 1))
        ffn_keep = scale("ffn", rows96, "keep", cols)
        if is_dec:
            gains, shifts, triple, output, query, pair, cross, biases, up, up_bias, down = outs[8:]
            put(gains, ((s_vec, 3, keep_row), (c_vec, 3, keep_row), (c_vec, 0, keep_row)))
            put(shifts, ((s_vec, 4, keep_row), (c_vec, 4, keep_row), (c_vec, 1, keep_row)))
            put(biases, ((s_vec, 5, head_row), (s_vec, 6, head_row), (s_vec, 7, keep_row),
                         (c_vec, 5, head_row), (c_vec, 6, head_row), (c_vec, 7, keep_row), (c_vec, 2, keep_row)))
            job(query, 0, 1, c, 0, keep_head)
            job(pair, 0, 0, c, 0, keep_head)
            job(pair, D, 0, c, 1, keep_head)
            job(cross, 0, 1, c, 1, head_keep)
            att, ffn, bias = s, 0, c_all
        else:
            gains, shifts, triple, output, biases, up, up_bias, down = outs[:8]
            put(gains, ((a_vec, 3, keep_row), (a_vec, 0, keep_row)))
            put(shifts, ((a_vec, 4, keep_row), (a_vec, 1, keep_row)))
            put(biases, ((a_vec, 5, head_row), (a_vec, 6, head_row), (a_vec, 7, keep_row), (a_vec, 2, keep_row)))
            att, ffn, bias = a, 1792, a_all
        job(triple, 0, 0, att, 0, keep_head)
        job(triple, D, 0, att, 1, keep_head)
        job(triple, 2 * D, 1, att, 0, keep_head)
        job(output, 0, 1, att, 1, head_keep)
        for t in range(24):
            up[:, t * 128:(t + 1) * 128] = half(0, ffn + t * 40) * keep_ffn[:, t * 128:(t + 1) * 128]
        for j in range(6):
            for t in range(5):
                start = pl.multiple_of(core * 480 + (ffn + j * 80 + t * 16), 16)
                down[j * 16:(j + 1) * 16, t * 128:(t + 1) * 128] = (
                    whole[1, pl.ds(start, 16), :] * ffn_keep[j * 16:(j + 1) * 16, t * 128:(t + 1) * 128])
        bias_row = jnp.where(first, bias[8:9, :96], bias[9:10, :96])
        up_bias[...] = bias_row * scale("ffn", lanes96, None, None)


SMEM = pl.BlockSpec(memory_space=pltpu.SMEM)
VMEM = pl.BlockSpec(memory_space=pltpu.VMEM)
ANY = pl.BlockSpec(memory_space=pl.ANY)
HBM = pl.BlockSpec(memory_space=pltpu.HBM)


def arr(*shape):
    return jax.ShapeDtypeStruct(shape, f32)


def hbm(*shape):
    return pltpu.HBM(shape, f32)


def call(kernel, in_specs, outs, name, scratch=(), limit=56, flops=1 << 20, nbytes=1 << 20):
    return pl.pallas_call(
        kernel,
        in_specs=in_specs,
        out_shape=outs,
        out_specs=[VMEM] * len(outs),
        scratch_shapes=list(scratch),
        name=name,
        compiler_params=pltpu.CompilerParams(vmem_limit_bytes=limit << 20),
        cost_estimate=pl.CostEstimate(flops=flops, bytes_accessed=nbytes, transcendentals=0),
    )


def in_hbm(*arrays):
    return tuple(pltpu.with_memory_space_constraint(a, pltpu.HBM) for a in arrays)


def flat_perm(move):
    pairs = []
    for x in range(4):
        for y in range(4):
            for z in range(4):
                for c in range(2):
                    X, Y, Z, C = move(x, y, z, c)
                    pairs.append((x * 32 + y * 8 + z * 2 + c, (X % 4) * 32 + (Y % 4) * 8 + (Z % 4) * 2 + C % 2))
    return pairs


SWAP = flat_perm(lambda x, y, z, c: (x, y, z, 1 - c))
RING = {
    "x": flat_perm(lambda x, y, z, c: (x + 1 - 2 * c, y, z, c)),
    "y": flat_perm(lambda x, y, z, c: (x, y + 1 - 2 * c, z, c)),
    "z": flat_perm(lambda x, y, z, c: (x, y, z + 1 - 2 * c, c)),
}
HOP_X = [flat_perm(lambda x, y, z, c, k=k: (x + k - 2 * c * k, y, z, c)) for k in range(4)]


def turn(p, c):
    return p + (1 - 2 * c) * (1 - 2 * (p & 1))


PAIR = {
    "x": (flat_perm(lambda x, y, z, c: (turn(x, c), y, z, c)), flat_perm(lambda x, y, z, c: (x + 2, y, z, c))),
    "y": (flat_perm(lambda x, y, z, c: (x, turn(y, c), z, c)), flat_perm(lambda x, y, z, c: (x, y + 2, z, c))),
    "z": (flat_perm(lambda x, y, z, c: (x, y, turn(z, c), c)), flat_perm(lambda x, y, z, c: (x, y, z + 2, c))),
}


def move(x, perm):
    return lax.ppermute(x, MESH_AXES, perm)


def barrier(*trees):
    return lax.optimization_barrier(trees)


class Part:
    def __init__(self, array, rows, order, dims):
        self.array, self.rows, self.order, self.dims = array, rows, list(order), list(dims)
        self.step, self.got = 0, []

    @property
    def size(self):
        return self.rows[1] - self.rows[0]


def advance(parts, name):
    inputs = []

    def slot(array):
        for n, a in enumerate(inputs):
            if a is array:
                return n
        inputs.append(array)
        return len(inputs) - 1

    plans, routes, out_shapes = [], {}, []
    for part in parts:
        axis = part.order[0]
        d = part.dims.index(axis)
        plan = dict(src=slot(part.array), rows=part.rows, d=d, axis=axis, step=part.step, nd=len(part.dims),
                    got=[(slot(a), off) for a, off in part.got], m=part.size)
        if part.step == 2:
            plan["out"] = len(out_shapes)
            out_shapes.append((4,) * (len(part.dims) - 1) + (part.size, 128))
            if len(part.order) > 1:
                plan["next_axis"] = part.order[1]
                rest = [t for t in part.dims if t != axis]
                plan["next_d"] = rest.index(part.order[1])
        plans.append(plan)
        send_axis, kind = (axis, part.step) if part.step < 2 else (plan.get("next_axis"), 0)
        if send_axis is not None:
            nd = plan["nd"] if part.step < 2 else plan["nd"] - 1
            chunk_rows = 4 ** (nd - 1) * part.size
            route = routes.setdefault((send_axis, kind), [0, []])
            plan["route"], plan["offset"], plan["chunk"] = (send_axis, kind), route[0], chunk_rows
            route[0] += chunk_rows * (2 if kind == 0 else 1)
    n_state = len(out_shapes)
    route_list = list(routes)
    out_shapes += [(routes[r][0], 128) for r in route_list]
    n_in = len(inputs)

    def kernel(*refs):
        ins, outs = refs[:n_in], refs[n_in:]
        pos = lax.axis_index("dp")
        core = pos & 1
        place = {"x": lax.axis_index("sub"), "y": pos >> 3, "z": (pos >> 1) & 3}

        def chunk(ref, nd, d, k, rows):
            index = [slice(None)] * nd
            index[d] = k & 3
            return ref[tuple(index) + (slice(*rows), slice(None))].reshape(-1, 128)

        for plan in plans:
            src, nd, d, rows, m = ins[plan["src"]], plan["nd"], plan["d"], plan["rows"], plan["m"]
            p = place[plan["axis"]]
            n = 4 ** (nd - 1) * m
            got = [(ins[i], off) for i, off in plan["got"]]
            out = outs[n_state + route_list.index(plan["route"])] if "route" in plan else None
            off = plan.get("offset")
            if plan["step"] == 0:
                q = turn(p, core)
                out[off:off + n, :] = chunk(src, nd, d, q, rows)
                out[off + n:off + 2 * n, :] = chunk(src, nd, d, q + 2, rows)
            elif plan["step"] == 1:
                (a, a_off), = got
                out[off:off + n, :] = chunk(src, nd, d, p + 2, rows) + a[a_off + n:a_off + 2 * n, :]
            else:
                (a, a_off), (b, b_off) = got
                total = chunk(src, nd, d, p, rows) + a[a_off:a_off + n, :] + b[b_off:b_off + n, :]
                state = outs[plan["out"]]
                state[...] = total.reshape(state.shape)
                if out is not None:
                    nn = plan["chunk"]
                    q = turn(place[plan["next_axis"]], core)
                    out[off:off + nn, :] = chunk(state, nd - 1, plan["next_d"], q, (0, m))
                    out[off + nn:off + 2 * nn, :] = chunk(state, nd - 1, plan["next_d"], q + 2, (0, m))

    outs = call(kernel, [VMEM] * n_in, [arr(*t) for t in out_shapes], name, limit=24)(*inputs)
    sent = {r: move(outs[n_state + i], PAIR[r[0]][r[1]]) for i, r in enumerate(route_list)}
    for part, plan in zip(parts, plans):
        if part.step == 2:
            part.array, part.rows = outs[plan["out"]], (0, part.size)
            part.dims.remove(part.order.pop(0))
            part.step, part.got = 0, []
        if "route" in plan:
            part.got.append((plan["route"], plan["offset"]))
            part.step += 1
    return sent


def land(parts, sent):
    for part in parts:
        part.got = [(sent[a], off) if isinstance(a, tuple) else (a, off) for a, off in part.got]


def per_device(
    enc_in, prev_enc, dec_in, enc_cotan, dec_cotan, src_lengths, tgt_lengths, configs,
    enc_gains, enc_shifts, enc_triple, enc_output, enc_biases, enc_up, enc_up_bias, enc_down,
    dec_gains, dec_shifts, dec_triple, dec_output, dec_cross_query, dec_cross_pair, dec_cross_out,
    dec_biases, dec_up, dec_up_bias, dec_down,
):
    group = lax.axis_index("sub")
    pos = lax.axis_index("dp")
    core = pos & 1
    place = {"x": group, "y": pos >> 3, "z": (pos >> 1) & 3}
    sign = 1 - 2 * core
    e_upb = enc_up_bias.reshape(1, FF)
    d_upb = dec_up_bias.reshape(1, FF)
    x, prev, y = enc_in.reshape(T, D), prev_enc.reshape(T, D), dec_in.reshape(T, D)
    e_cot, d_cot = enc_cotan.reshape(T, D), dec_cotan.reshape(T, D)
    act, act3, prob = arr(T, D), arr(T, 3 * D), arr(2 * H, LEN, LEN)
    act_out = hbm(T, D)
    vmem = pltpu.VMEM
    scalars = (configs, src_lengths, tgt_lengths)
    e_vec = (enc_gains.T, enc_shifts.T, enc_biases.T)
    d_vec = (dec_gains.T, dec_shifts.T, dec_biases.T)
    head = [SMEM] * 3 + [VMEM] * 3

    encoded, e_qkv, e_p, e_mixed, e_mid, e_z = call(
        encoder_kernel, head + [VMEM, VMEM] + [HBM] * 4,
        [act_out, hbm(T, 3 * D), hbm(2 * H, LEN, LEN), act_out, act_out, hbm(T, FF)], "encoder_forward",
        [vmem((D, 3 * D), bf16), vmem((D, D), bf16), vmem((D, FF), bf16), vmem((FF, D), bf16),
         vmem((2 * T, D), bf16), vmem((T, D), f32), pltpu.SemaphoreType.DMA((4,))], limit=24, flops=8 << 30, nbytes=24 << 20,
    )(*scalars, *e_vec, e_upb, x, *in_hbm(enc_triple, enc_output, enc_up, enc_down))

    (decoded, d_qkv, d_p, d_mixed, a1, mem, c_qkv, c_p, c_mixed, a2, da2, f_keep, f_send, f_vec, f_upb) = call(
        decoder_kernel, head + [VMEM] * 6 + [HBM] * 7,
        [act_out, act3, prob, act, act, act, act3, prob, act, act, act,
         arr(T, D + FF), arr(T, D + FF), arr(8, D), arr(1, FF)], "decoder_forward",
        [vmem((D, 3 * D), bf16), vmem((D, D), bf16), vmem((D, D), bf16), vmem((D, 2 * D), bf16),
         vmem((D, D), bf16), vmem((D, FF), bf16), vmem((FF, D), bf16),
         vmem((2 * T, D), bf16), vmem((T, D), f32), vmem((T, FF), f32), pltpu.SemaphoreType.DMA((7,))], limit=32, flops=16 << 30, nbytes=48 << 20,
    )(*scalars, *d_vec, d_upb, y, prev, x, encoded, d_cot,
      *in_hbm(dec_triple, dec_output, dec_cross_query, dec_cross_pair, dec_cross_out, dec_up, dec_down))

    def ffn_grad(kept, got, rows, name, pinned=False):
        whole = pl.BlockSpec((T, D + FF), lambda j: (0, 0), pipeline_mode=pl.Buffered(1))
        return pl.pallas_call(
            ffn_grad_kernel,
            grid=(12,),
            in_specs=[whole, whole],
            out_shape=pltpu.HBM((16, rows, 128), f32) if pinned else arr(16, rows, 128),
            out_specs=pl.BlockSpec((16, 80, 128), lambda j: (0, j, 0)),
            scratch_shapes=[vmem((2, D, 2 * T), bf16), vmem((2, 2 * T, FF), bf16), vmem((2, 2 * T, D), bf16),
                            vmem((2, 16, 192, 2 * T), bf16)],
            name=name,
            compiler_params=pltpu.CompilerParams(vmem_limit_bytes=22 << 20),
            cost_estimate=pl.CostEstimate(flops=6 << 30, bytes_accessed=16 << 20, transcendentals=0),
        )(kept, got)

    def att_grad(with_ffn, whole, operands, name, pinned=False):
        n = len(with_ffn)
        return pl.pallas_call(
            functools.partial(att_grad_kernel, with_ffn),
            in_specs=[SMEM, SMEM, ANY] + [VMEM] * len(operands),
            out_shape=pltpu.HBM(whole.shape, f32) if pinned else arr(*whole.shape),
            out_specs=ANY,
            scratch_shapes=[vmem((16, ROWS_ATT * n, 128), f32), pltpu.SemaphoreType.DMA((n,))],
            input_output_aliases={2: 0},
            name=name,
            compiler_params=pltpu.CompilerParams(vmem_limit_bytes=24 << 20),
            cost_estimate=pl.CostEstimate(flops=3 << 30, bytes_accessed=10 << 20, transcendentals=0),
        )(src_lengths, tgt_lengths, whole, *operands)

    pair = arr(T, 4 * D)
    f_recv = move(f_send, SWAP)
    da1, dmem, dprev, c_keep, c_send, c_vec = call(
        cross_back_kernel, head + [VMEM] * 9, [act, act, act_out, pair, pair, arr(8, D)], "cross_backward", [vmem((2 * H, LEN, LEN), f32)], limit=14, flops=3 << 30, nbytes=16 << 20,
    )(*scalars, *d_vec, da2, a1, mem, c_qkv, c_p, c_mixed, dec_cross_query, dec_cross_pair, dec_cross_out)
    c_recv = move(c_send, SWAP)
    dy_in, s_keep, s_send, s_vec = call(
        functools.partial(self_back_kernel, 0, 3, False), head + [VMEM] * 8,
        [act_out, pair, pair, arr(8, D)], "self_backward", [vmem((2 * H, LEN, LEN), f32)], limit=14, flops=3 << 30, nbytes=16 << 20,
    )(*scalars, *d_vec, da1, y, d_qkv, d_p, d_mixed, dmem, dec_triple, dec_output)
    f_recv, s_send, s_keep, c_recv, dmem = barrier(f_recv, s_send, s_keep, c_recv, dmem)
    s_recv = move(s_send, SWAP)
    g_d = ffn_grad(f_keep, f_recv, ROWS_FFN + 2 * ROWS_ATT, "decoder_ffn_grad", True)
    g_d, s_recv = barrier(g_d, s_recv)
    g_d = att_grad((True, False), g_d, (c_keep, c_recv, c_vec, f_vec, f_upb, s_keep, s_recv, s_vec),
                   "decoder_attention_grad", True)
    cores = [[2 * i + c for i in range(16)] for c in range(2)]
    g_d, dmem = barrier(g_d, dmem)
    r_d = lax.psum_scatter(g_d, "dp", scatter_dimension=0, axis_index_groups=cores, tiled=True)

    dmid, h_keep, h_send, h_vec, h_upb = call(
        encoder_ffn_back_kernel, head + [VMEM] * 4 + [HBM] * 2,
        [act, arr(T, D + FF), arr(T, D + FF), arr(8, D), arr(1, FF)], "encoder_ffn_backward",
        [vmem((D, FF), bf16), vmem((FF, D), bf16), vmem((2 * T, D), bf16), vmem((T, D), f32),
         pltpu.SemaphoreType.DMA((2, FF // TILE))], limit=20, flops=4 << 30, nbytes=24 << 20,
    )(*scalars, *e_vec, e_cot, dmem, e_mid, e_z, *in_hbm(enc_up, enc_down))
    h_recv = move(h_send, SWAP)
    dx_in, e_keep, e_send, e_vec_sum = call(
        functools.partial(self_back_kernel, 0, 2, True), head + [VMEM] * 8,
        [act_out, pair, pair, arr(8, D)], "encoder_attention_backward", [vmem((2 * H, LEN, LEN), f32)], limit=14, flops=3 << 30, nbytes=16 << 20,
    )(*scalars, *e_vec, dmid, x, e_qkv, e_p, e_mixed, dmem, enc_triple, enc_output)
    h_recv, e_send, e_keep = barrier(h_recv, e_send, e_keep)
    e_recv = move(e_send, SWAP)
    g_e = ffn_grad(h_keep, h_recv, ROWS_FFN + ROWS_ATT, "encoder_ffn_grad")
    g_e, e_recv = barrier(g_e, e_recv)
    g_e = att_grad((True,), g_e, (e_keep, e_recv, e_vec_sum, h_vec, h_upb), "encoder_attention_grad")

    g_e = g_e.reshape(4, 4, 4, 344, 128)
    enc_parts = [Part(g_e, rows, order, "yzx")
                 for rows, order in (((0, 160), "xyz"), ((160, 256), "yzx"), ((256, 344), "zxy"))]
    dec_parts = []
    for phase in range(7):
        if phase == 4:
            dec_parts = [Part(r_d.reshape(4, 448, 128), (0, 448), "x", "x")]
        active = enc_parts + dec_parts
        sent = advance(active, "step_%d" % phase)
        if sent:
            keys = list(sent)
            land(active, dict(zip(keys, barrier(*[sent[k] for k in keys]))))

    own = jnp.concatenate([p.array for p in dec_parts + enc_parts], 0)
    mine = jnp.stack([own] + [move(own, HOP_X[k]) for k in (1, 2, 3)], 0)
    other = move(mine, SWAP)

    enc_shapes = ((2, 20), (2, 20), (20, 3 * D), (20, D), (4, 20), (20, FF), (1, 96), (96, D))
    dec_shapes = ((3, 20), (3, 20), (20, 3 * D), (20, D), (20, D), (20, 2 * D), (20, D), (7, 20), (20, FF),
                  (1, 96), (96, D))
    grads = call(
        finish_kernel, [SMEM] + [VMEM] * 2, [arr(*t) for t in enc_shapes + dec_shapes], "finish",
        [vmem((2, 3168, 128), f32)], limit=24,
    )(configs, mine, other)
    grads = tuple(t.reshape(96) if t.shape == (1, 96) else t.T if t.shape[1] == 20 else t for t in grads)
    whole = (1, SENT, LEN, D)
    return (
        (encoded.reshape(whole), decoded.reshape(whole), dx_in.reshape(whole), dprev.reshape(whole),
         dy_in.reshape(whole)) + grads
    )


def solution(mesh):
    acts = P("sub", "dp", None, None)
    counts = P("sub", "dp")
    row, vector = P("dp", None), P("dp")
    in_specs = (acts,) * 5 + (counts,) * 2 + (P(),) * 20
    out_specs = (acts,) * 5 + (row,) * 6 + (vector, row) + (row,) * 9 + (vector, row)
    return jax.shard_map(per_device, mesh=mesh, in_specs=in_specs, out_specs=out_specs, check_vma=False)
```

```python
import functools
import math

import jax
import jax.numpy as jnp
from jax import lax
from jax.experimental import pallas as pl
from jax.experimental.pallas import tpu as pltpu
from jax.sharding import PartitionSpec as P

D = 640
H = 8
FF = 3072
LEN = 128
HD = 80
SENT = 2
T = SENT * LEN
TILE = 1024
ROWS_FFN = 960
ROWS_ATT = 416
f32 = jnp.float32
bf16 = jnp.bfloat16
NN = (((1,), (0,)), ((), ()))
NT = (((1,), (1,)), ((), ()))
TN = (((0,), (0,)), ((), ()))
MESH_AXES = ("sub", "dp")


def split(x):
    hi = x.astype(bf16)
    lo = (x - hi.astype(f32)).astype(bf16)
    return hi, lo


def stacked(x):
    return jnp.concatenate(split(x), 0)


def halves(r):
    n = r.shape[0] // 2
    return r[:n] + r[n:]


def mm(xs, w, dims=NN):
    return halves(lax.dot_general(xs, w, dims, preferred_element_type=f32))


def dot3(a, b, dims):
    ah, al = a
    bh, bl = b
    dg = functools.partial(lax.dot_general, dimension_numbers=dims, preferred_element_type=f32)
    if dims == NN:
        return dg(jnp.concatenate([al, ah, ah], 1), jnp.concatenate([bh, bl, bh], 0))
    return dg(al, bh) + dg(ah, bl) + dg(ah, bh)


def lane_mask(width, limit):
    return (lax.broadcasted_iota(jnp.int32, (1, width), 1) < limit).astype(f32)


def row_ok(len0, len1):
    row = lax.broadcasted_iota(jnp.int32, (T, 1), 0)
    limit = jnp.where(row < LEN, len0, LEN + len1)
    return (row < limit).astype(f32)


def norm(x, keep, width):
    mean = jnp.sum(x * keep, -1, keepdims=True) / width
    centred = (x - mean) * keep
    var = jnp.sum(centred * centred, -1, keepdims=True) / width
    rstd = lax.rsqrt(var + 1e-5)
    return centred * rstd, rstd


def norm_back(dy, n, rstd, gain, keep, width):
    dy = dy * keep
    dz = dy * gain
    m1 = jnp.sum(dz, -1, keepdims=True) / width
    m2 = jnp.sum(dz * n, -1, keepdims=True) / width
    dx = keep * rstd * (dz - m1 - n * m2)
    return dx, jnp.sum(dy * n, 0, keepdims=True), jnp.sum(dy, 0, keepdims=True)


def bell(z):
    cdf = 0.5 * (1.0 + lax.erf(z * (1.0 / math.sqrt(2.0))))
    pdf = jnp.exp(-0.5 * z * z) * (1.0 / math.sqrt(2.0 * math.pi))
    return cdf, pdf


def rows_of(pair, s, repeat):
    return jnp.concatenate([pair[i][s * LEN:(s + 1) * LEN] for i in repeat], 0)


def head(x, h):
    return x[:, h * HD:(h + 1) * HD]


def corners(r):
    return (r[LEN:, LEN:] + r[LEN:, :LEN]) + (r[:LEN, LEN:] + r[:LEN, :LEN])


def three(x):
    hi, lo = split(x)
    return jnp.concatenate([hi, lo, hi], 1)


def dot(a, b, dims):
    return lax.dot_general(a, b, dims, preferred_element_type=f32)


def attend(q, k, v, lens, causal, p_ref):
    qs, ks, vs = split(q * (1.0 / math.sqrt(HD))), split(k), split(v)
    col = lax.broadcasted_iota(jnp.int32, (LEN, LEN), 1)
    for s in range(SENT):
        allowed = col < lens[s]
        if causal:
            allowed = allowed & (lax.broadcasted_iota(jnp.int32, (LEN, LEN), 0) >= col)
        q2, k2 = rows_of(qs, s, (0, 1)), rows_of(ks, s, (0, 1))
        for h in range(H):
            p_ref[s * H + h] = jnp.where(allowed, corners(dot(head(q2, h), head(k2, h), NT)), -1e30)
    for i in range(SENT * H):
        scores = p_ref[i]
        e = jnp.exp(scores - jnp.max(scores, -1, keepdims=True))
        p_ref[i] = e * (1.0 / jnp.sum(e, -1, keepdims=True))
    rows = []
    for s in range(SENT):
        v3 = rows_of(vs, s, (0, 0, 1))
        rows.append(jnp.concatenate([dot(three(p_ref[s * H + h]), head(v3, h), NN) for h in range(H)], 1))
    return jnp.concatenate(rows, 0)


def attend_back(do, q, k, v, p_ref, ds_ref):
    scale = 1.0 / math.sqrt(HD)
    dos, qs, ks, vs = split(do), split(q * scale), split(k * scale), split(v)
    for s in range(SENT):
        do2, v2 = rows_of(dos, s, (0, 1)), rows_of(vs, s, (0, 1))
        for h in range(H):
            ds_ref[s * H + h] = corners(dot(head(do2, h), head(v2, h), NT))
    for i in range(SENT * H):
        prob, dp = p_ref[i], ds_ref[i]
        ds_ref[i] = prob * (dp - jnp.sum(dp * prob, -1, keepdims=True))
    all_q, all_k, all_v = [], [], []
    for s in range(SENT):
        k3, q3, do3 = rows_of(ks, s, (0, 0, 1)), rows_of(qs, s, (0, 0, 1)), rows_of(dos, s, (0, 0, 1))
        ids = [(s * H + h, h) for h in range(H)]
        all_q.append(jnp.concatenate([dot(three(ds_ref[i]), head(k3, h), NN) for i, h in ids], 1))
        all_k.append(jnp.concatenate([dot(three(ds_ref[i].T), head(q3, h), NN) for i, h in ids], 1))
        all_v.append(jnp.concatenate([dot(three(p_ref[i].T), head(do3, h), NN) for i, h in ids], 1))
    return tuple(jnp.concatenate(x, 0) for x in (all_q, all_k, all_v))


def ffn_forward(ns, up, bias, bias_row, down, ffn_limit, z_ref, acc_ref):
    acc_ref[...] = jnp.zeros_like(acc_ref)

    def body(j, _):
        sl = pl.ds(pl.multiple_of(j * TILE, TILE), TILE)
        z = mm(ns[...], up[:, sl]) + bias[bias_row:bias_row + 1, sl].astype(f32)
        z_ref[:, sl] = z
        mask = (lax.broadcasted_iota(jnp.int32, (1, TILE), 1) + j * TILE < ffn_limit).astype(f32)
        u = z * bell(z)[0] * mask
        acc_ref[...] += mm(stacked(u), down[sl, :])
        return 0

    lax.fori_loop(0, FF // TILE, body, 0)


def ffn_backward(dyk, n, z_ref, up, down, ffn_limit, core, dys_ref, keep_ref, send_ref, bias_ref, acc_ref,
                 arrive=None):
    acc_ref[...] = jnp.zeros_like(acc_ref)
    dys_ref[...] = stacked(dyk)
    first = core == 0
    keep_ref[:, :D] = jnp.where(first, n, dyk)
    send_ref[:, :D] = jnp.where(first, dyk, n)

    def body(j, _):
        sl = pl.ds(pl.multiple_of(j * TILE, TILE), TILE)
        out = pl.ds(pl.multiple_of(j * TILE + D, 128), TILE)
        if arrive is not None:
            arrive(sl, j)
        du = mm(dys_ref[...], down[sl, :], NT)
        z = z_ref[:, sl]
        cdf, pdf = bell(z)
        mask = (lax.broadcasted_iota(jnp.int32, (1, TILE), 1) + j * TILE < ffn_limit).astype(f32)
        u = z * cdf * mask
        dz = du * mask * (cdf + z * pdf)
        keep_ref[:, out] = jnp.where(first, dz, u)
        send_ref[:, out] = jnp.where(first, u, dz)
        bias_ref[:, sl] = jnp.sum(dz, 0, keepdims=True)
        acc_ref[...] += mm(stacked(dz), up[:, sl], NT)
        return 0

    lax.fori_loop(0, FF // TILE, body, 0)


def load_vectors(ref):
    return ref[...].astype(f32)


def setting(table):
    g = lax.axis_index("sub")
    core = lax.axis_index("dp") & 1
    c = table[4 * g + 3]
    bits = [(c & 1).astype(f32), ((c >> 1) & 1).astype(f32), ((c >> 2) & 1).astype(f32)]
    total = bits[0] + bits[1] + bits[2]
    sc = (table[4 * g], table[4 * g + 1] * HD, table[4 * g + 2], table[16], table[17], table[18], table[19], core)
    return sc, [b / total for b in bits]


def fetch(pairs, sems):
    copies = [pltpu.make_async_copy(a, b, sems.at[i]) for i, (a, b) in enumerate(pairs)]
    for c in copies:
        c.start()
    return copies


def encoder_kernel(table, vec_ref, upb, x_ref, w_triple, w_out, w_up, w_down,
                   o_encoded, o_qkv, o_p, o_mixed, o_middle, o_z,
                   b_triple, b_out, b_up, b_down, ns_ref, acc_ref, b_x,
                   encoded, qkv, p_ref, mixed, middle, z_ref, sems, out_sems):
    read_x, *copies = fetch([(x_ref, b_x), (w_triple, b_triple), (w_out, b_out), (w_up, b_up), (w_down, b_down)], sems)
    leaving = []

    def leave(src, dst):
        copy = pltpu.make_async_copy(src, dst, out_sems.at[len(leaving)])
        copy.start()
        leaving.append(copy)

    sc, pick = setting(table)
    width = sc[0].astype(f32)
    keep, heads = lane_mask(D, sc[0]), lane_mask(D, sc[1])
    vec = load_vectors(vec_ref)
    read_x.wait()
    x = b_x[...]
    n, _ = norm(x, keep, width)
    ns = stacked((n * vec[0:1] + vec[2:3]) * keep)
    copies[0].wait()
    qkv[:, :D] = (mm(ns, b_triple[:, :D]) + vec[4:5]) * heads
    qkv[:, D:2 * D] = mm(ns, b_triple[:, D:2 * D]) * heads
    qkv[:, 2 * D:] = (mm(ns, b_triple[:, 2 * D:]) + vec[5:6]) * heads
    leave(qkv, o_qkv)
    o = attend(qkv[:, :D], qkv[:, D:2 * D], qkv[:, 2 * D:], (sc[3], sc[4]), False, p_ref)
    mixed[...] = o
    leave(p_ref, o_p)
    leave(mixed, o_mixed)
    copies[1].wait()
    mid = x + (mm(stacked(o), b_out[...]) + vec[6:7]) * keep
    middle[...] = mid
    leave(middle, o_middle)
    n, _ = norm(mid, keep, width)
    ns_ref[...] = stacked((n * vec[1:2] + vec[3:4]) * keep)
    copies[2].wait()
    copies[3].wait()
    ffn_forward(ns_ref, b_up, upb, 0, b_down, sc[2], z_ref, acc_ref)
    leave(z_ref, o_z)
    encoded[...] = (middle[...] + (acc_ref[...] + vec[7:8]) * keep) * row_ok(sc[3], sc[4])
    leave(encoded, o_encoded)
    for copy in leaving:
        copy.wait()


def decoder_kernel(table, vec_ref, upb, x_ref, prev_ref, src_ref, cot_ref, enc_in,
                   w_triple, w_out, w_query, w_pair, w_cross, w_up, w_down,
                   o_decoded, o_qkv, o_p, o_mixed, a1_ref, mem_ref, qkv_c, p_cross, mixed_c, a2_ref, da2_ref,
                   keep_buf, send_buf, dvec, dupb,
                   b_triple, b_out, b_query, b_pair, b_cross, b_up, b_down, ns_ref, acc_ref, z_ref, enc_ref,
                   decoded, qkv, p_self, mixed, sems, out_sems):
    copies = fetch([(w_triple, b_triple), (w_out, b_out), (w_query, b_query), (w_pair, b_pair),
                    (w_cross, b_cross), (w_up, b_up), (w_down, b_down), (enc_in, enc_ref)], sems)
    leaving = []

    def leave(src, dst):
        copy = pltpu.make_async_copy(src, dst, out_sems.at[len(leaving)])
        copy.start()
        leaving.append(copy)

    sc, pick = setting(table)
    width = sc[0].astype(f32)
    keep, heads = lane_mask(D, sc[0]), lane_mask(D, sc[1])
    vec = load_vectors(vec_ref)
    x = x_ref[...]
    n, _ = norm(x, keep, width)
    ns = stacked((n * vec[0:1] + vec[3:4]) * keep)
    copies[0].wait()
    qkv[:, :D] = (mm(ns, b_triple[:, :D]) + vec[6:7]) * heads
    qkv[:, D:2 * D] = mm(ns, b_triple[:, D:2 * D]) * heads
    qkv[:, 2 * D:] = (mm(ns, b_triple[:, 2 * D:]) + vec[7:8]) * heads
    o = attend(qkv[:, :D], qkv[:, D:2 * D], qkv[:, 2 * D:], (sc[5], sc[6]), True, p_self)
    mixed[...] = o
    leave(qkv, o_qkv)
    leave(p_self, o_p)
    leave(mixed, o_mixed)
    copies[1].wait()
    a1 = x + (mm(stacked(o), b_out[...]) + vec[8:9]) * keep
    a1_ref[...] = a1
    n, _ = norm(a1, keep, width)
    ns = stacked((n * vec[1:2] + vec[4:5]) * keep)
    copies[2].wait()
    qkv_c[:, :D] = (mm(ns, b_query[...]) + vec[9:10]) * heads
    copies[7].wait()
    memory = (pick[0] * prev_ref[...] + pick[1] * src_ref[...] + pick[2] * enc_ref[...]) * keep
    mem_ref[...] = memory
    ns = stacked(memory)
    copies[3].wait()
    qkv_c[:, D:2 * D] = mm(ns, b_pair[:, :D]) * heads
    qkv_c[:, 2 * D:] = (mm(ns, b_pair[:, D:]) + vec[10:11]) * heads
    o = attend(qkv_c[:, :D], qkv_c[:, D:2 * D], qkv_c[:, 2 * D:], (sc[3], sc[4]), False, p_cross)
    mixed_c[...] = o
    copies[4].wait()
    a2_ref[...] = a1_ref[...] + (mm(stacked(o), b_cross[...]) + vec[11:12]) * keep
    n, _ = norm(a2_ref[...], keep, width)
    ns_ref[...] = stacked((n * vec[2:3] + vec[5:6]) * keep)
    copies[5].wait()
    copies[6].wait()
    ffn_forward(ns_ref, b_up, upb, 1, b_down, sc[2], z_ref, acc_ref)
    ok = row_ok(sc[5], sc[6])
    decoded[...] = (a2_ref[...] + (acc_ref[...] + vec[12:13]) * keep) * ok
    leave(decoded, o_decoded)
    dy = cot_ref[...] * ok
    dyk = dy * keep
    n, rstd = norm(a2_ref[...], keep, width)
    ffn_backward(dyk, (n * vec[2:3] + vec[5:6]) * keep, z_ref, b_up, b_down, sc[2], sc[7], ns_ref,
                 keep_buf, send_buf, dupb, acc_ref)
    dx, dg, db = norm_back(acc_ref[...], n, rstd, vec[2:3], keep, width)
    da2_ref[...] = dy + dx
    dvec[...] = jnp.concatenate([dg, db, jnp.sum(dyk, 0, keepdims=True), jnp.zeros((5, D), f32)], 0)
    for copy in leaving:
        copy.wait()


def cross_back_kernel(table, vec_ref, da2_ref, a1_ref, mem_ref, qkv_c, p_cross, mixed_c,
                      w_query, w_pair, w_cross,
                      da1_ref, dmem_ref, dprev_ref, keep_buf, send_buf, dvec, ds_ref):
    sc, pick = setting(table)
    width = sc[0].astype(f32)
    keep, heads = lane_mask(D, sc[0]), lane_mask(D, sc[1])
    vec = load_vectors(vec_ref)
    first = sc[7] == 0
    da2 = da2_ref[...]
    dyk = da2 * keep
    do = mm(stacked(dyk), w_cross[...], NT)
    dq, dk, dv = attend_back(do, qkv_c[:, :D], qkv_c[:, D:2 * D], qkv_c[:, 2 * D:], p_cross, ds_ref)
    dq, dk, dv = dq * heads, dk * heads, dv * heads
    n, rstd = norm(a1_ref[...], keep, width)
    normed = (n * vec[1:2] + vec[4:5]) * keep
    for i, (a, b) in enumerate(((mem_ref[...], normed), (mem_ref[...], mixed_c[...]), (dk, dq), (dv, dyk))):
        keep_buf[:, i * D:(i + 1) * D] = jnp.where(first, a, b)
        send_buf[:, i * D:(i + 1) * D] = jnp.where(first, b, a)
    dn = mm(stacked(dq), w_query[...], NT)
    dx, dg, db = norm_back(dn, n, rstd, vec[1:2], keep, width)
    da1_ref[...] = da2 + dx
    dmem = (mm(stacked(dk), w_pair[:, :D], NT) + mm(stacked(dv), w_pair[:, D:], NT)) * keep
    dmem_ref[...] = dmem
    dprev_ref[...] = dmem * pick[0]
    dvec[...] = jnp.concatenate(
        [dg, db] + [jnp.sum(t, 0, keepdims=True) for t in (dq, dv, dyk)] + [jnp.zeros((3, D), f32)], 0)


def self_back_kernel(gain_row, shift_row, with_memory, table, vec_ref, dy_ref, x_ref, qkv, p_ref, mixed,
                     dmem_ref, w_triple, w_out, dx_ref, keep_buf, send_buf, dvec, ds_ref):
    sc, pick = setting(table)
    width = sc[0].astype(f32)
    keep, heads = lane_mask(D, sc[0]), lane_mask(D, sc[1])
    vec = load_vectors(vec_ref)
    gain, shift = vec[gain_row:gain_row + 1], vec[shift_row:shift_row + 1]
    first = sc[7] == 0
    dy = dy_ref[...]
    dyk = dy * keep
    do = mm(stacked(dyk), w_out[...], NT)
    dq, dk, dv = attend_back(do, qkv[:, :D], qkv[:, D:2 * D], qkv[:, 2 * D:], p_ref, ds_ref)
    dq, dk, dv = dq * heads, dk * heads, dv * heads
    n, rstd = norm(x_ref[...], keep, width)
    normed = (n * gain + shift) * keep
    for i, (a, b) in enumerate(((normed, normed), (normed, mixed[...]), (dq, dv), (dk, dyk))):
        keep_buf[:, i * D:(i + 1) * D] = jnp.where(first, a, b)
        send_buf[:, i * D:(i + 1) * D] = jnp.where(first, b, a)
    dn = mm(stacked(dq), w_triple[:, :D], NT) + mm(stacked(dk), w_triple[:, D:2 * D], NT)
    dn += mm(stacked(dv), w_triple[:, 2 * D:], NT)
    dx, dg, db = norm_back(dn, n, rstd, gain, keep, width)
    dx = dx + dy
    if with_memory:
        dx = dx + pick[1] * dmem_ref[...]
    dx_ref[...] = dx
    dvec[...] = jnp.concatenate(
        [dg, db] + [jnp.sum(t, 0, keepdims=True) for t in (dq, dv, dyk)] + [jnp.zeros((3, D), f32)], 0)


def encoder_ffn_back_kernel(table, vec_ref, h_cot, h_dmem, h_middle, h_z, w_up, w_down,
                            dmid_ref, keep_buf, send_buf, dvec, dupb,
                            b_up, b_down, ns_ref, acc_ref, cot_ref, dmem_ref, middle, z_ref, sems, first_sems):
    first = fetch([(h_cot, cot_ref), (h_dmem, dmem_ref), (h_middle, middle)], first_sems)

    def tile_copies(sl, j):
        return (pltpu.make_async_copy(h_z.at[:, sl], z_ref.at[:, sl], sems.at[2, j]),
                pltpu.make_async_copy(w_down.at[sl, :], b_down.at[sl, :], sems.at[0, j]),
                pltpu.make_async_copy(w_up.at[:, sl], b_up.at[:, sl], sems.at[1, j]))

    for j in range(FF // TILE):
        for copy in tile_copies(pl.ds(j * TILE, TILE), j):
            copy.start()

    def arrive(sl, j):
        for copy in tile_copies(sl, j):
            copy.wait()

    sc, pick = setting(table)
    width = sc[0].astype(f32)
    keep = lane_mask(D, sc[0])
    vec = load_vectors(vec_ref)
    for copy in first:
        copy.wait()
    dy = (cot_ref[...] + pick[2] * dmem_ref[...]) * row_ok(sc[3], sc[4])
    dyk = dy * keep
    n, rstd = norm(middle[...], keep, width)
    ffn_backward(dyk, (n * vec[1:2] + vec[3:4]) * keep, z_ref, b_up, b_down, sc[2], sc[7], ns_ref,
                 keep_buf, send_buf, dupb, acc_ref, arrive)
    dx, dg, db = norm_back(acc_ref[...], n, rstd, vec[1:2], keep, width)
    dmid_ref[...] = dy + dx
    dvec[...] = jnp.concatenate([dg, db, jnp.sum(dyk, 0, keepdims=True), jnp.zeros((5, D), f32)], 0)


def ffn_grad_kernel(keep_buf, recv_buf, out, at_s, b_b, b_s, at_b):
    j = pl.program_id(0)
    first = (lax.axis_index("dp") & 1) == 0

    @pl.when(first & (j == 0))
    def _():
        for i, ref in enumerate((keep_buf, recv_buf)):
            hi, lo = split(ref[:, :D].T)
            at_s[0, :, i * T:(i + 1) * T] = hi
            at_s[1, :, i * T:(i + 1) * T] = lo

            def body(c, _):
                src = pl.ds(pl.multiple_of(c * TILE + D, 128), TILE)
                dst = pl.ds(pl.multiple_of(c * TILE, TILE), TILE)
                hi, lo = split(ref[:, src])
                b_b[0, i * T:(i + 1) * T, dst] = hi
                b_b[1, i * T:(i + 1) * T, dst] = lo
                return 0

            lax.fori_loop(0, FF // TILE, body, 0)

    @pl.when(jnp.logical_not(first) & (j == 0))
    def _():
        for i, ref in enumerate((keep_buf, recv_buf)):
            hi, lo = split(ref[:, :D])
            b_s[0, i * T:(i + 1) * T] = hi
            b_s[1, i * T:(i + 1) * T] = lo

            def body(c, _):
                x = ref[:, pl.ds(pl.multiple_of(c * 384 + D, 128), 384)].T
                hi, lo = split(x.reshape(2, 192, T))
                at_b[0, pl.ds(2 * c, 2), :, i * T:(i + 1) * T] = hi
                at_b[1, pl.ds(2 * c, 2), :, i * T:(i + 1) * T] = lo
                return 0

            lax.fori_loop(0, 8, body, 0)

    @pl.when(first)
    def _():
        cols = pl.ds(pl.multiple_of(j * 512, 512), 512)
        r = dot3((at_s[0], at_s[1]), (b_b[0, :, cols], b_b[1, :, cols]), NN)
        for c in range(4):
            out[:, c * 40:(c + 1) * 40, :] = r[:, c * 128:(c + 1) * 128].reshape(16, 40, 128)

    @pl.when(jnp.logical_not(first))
    def _():
        rows = pl.ds(pl.multiple_of(j * 32, 32), 32)
        a = tuple(at_b[i, :, rows, :].reshape(512, 2 * T) for i in range(2))
        r = dot3(a, (b_s[0], b_s[1]), NN)
        for c in range(5):
            out[:, c * 32:(c + 1) * 32, :] = r[:, c * 128:(c + 1) * 128].reshape(16, 32, 128)


def small_block(out, base, ffn_vec, att_vec, upb, counts, group):
    lane = lax.broadcasted_iota(jnp.int32, (1, 128), 1)
    totals = jnp.where(lane == group, counts[0], 0) + jnp.where(lane == group + 4, counts[1], 0)
    totals = totals.astype(f32)
    for b in range(16):
        out[b, base:base + 16, :] = jnp.zeros((16, 128), f32)
        if ffn_vec is not None:
            out[b, base:base + 3, :40] = ffn_vec[:3, b * 40:(b + 1) * 40]
        out[b, base + 3:base + 8, :40] = att_vec[:5, b * 40:(b + 1) * 40]
        if upb is not None:
            for c in range(2):
                out[b, base + 8 + c:base + 9 + c, :96] = upb[:, b * 192 + c * 96:b * 192 + (c + 1) * 96]
        out[b, base + 15:base + 16, :] = totals


def att_grad_kernel(with_ffn, *refs):
    table = refs[0]
    whole, out, sem = refs[-3:]
    refs = list(refs[2:-3])
    group = lax.axis_index("sub")
    counts = (table[16] + table[17], table[18] + table[19])
    copies = []
    for n, ffn in enumerate(with_ffn):
        kept, got, att_vec = refs[:3]
        ffn_vec, upb = (refs[3], refs[4]) if ffn else (None, None)
        refs = refs[5 if ffn else 3:]
        base = n * ROWS_ATT
        small_block(out, base + 400, ffn_vec, att_vec, upb, counts, group)
        for i in range(2):
            a = jnp.concatenate([kept[:, i * D:(i + 1) * D].T, got[:, i * D:(i + 1) * D].T], 1)
            b = jnp.concatenate([kept[:, (i + 2) * D:(i + 3) * D], got[:, (i + 2) * D:(i + 3) * D]], 0)
            a, b = split(a), split(b)
            r = dot3(a, b, NN)
            for c in range(5):
                row = base + i * 200 + c * 40
                out[:, row:row + 40, :] = r[:, c * 128:(c + 1) * 128].reshape(16, 40, 128)
        copy = pltpu.make_async_copy(
            out.at[:, pl.ds(base, ROWS_ATT), :], whole.at[:, pl.ds(ROWS_FFN + base, ROWS_ATT), :], sem.at[n])
        copy.start()
        copies.append(copy)
    for copy in copies:
        copy.wait()


def usage_scale(cfg, totals, row_kind, rows, col_kind, cols):
    limit = {"keep": lambda g: cfg[4 * g], "head": lambda g: cfg[4 * g + 1] * HD, "ffn": lambda g: cfg[4 * g + 2]}
    usage = 0.0
    for g in range(4):
        part = jnp.where(rows < limit[row_kind](g), totals[g], 0.0)
        if col_kind is not None:
            part = jnp.where(cols < limit[col_kind](g), part, 0.0)
        usage = usage + part
    return lax.rsqrt(usage)


def finish_kernel(cfg, mine_d, other_d, mine_e, other_e, *refs):
    whole = refs[-1]
    outs = refs[:-1]
    pos = lax.axis_index("dp")
    px = lax.axis_index("sub")
    core = pos & 1
    sign = 1 - 2 * core
    first = core == 0
    for k in range(4):
        for refs_k, owner, from_x in (((mine_d, mine_e), core, (px - sign * k) & 3),
                                      ((other_d, other_e), 1 - core, (px + sign * k) & 3)):
            for ref, n, base in zip(refs_k, (448, 344), (0, 1792)):
                start = pl.multiple_of(base + from_x * n, 8)
                whole[owner, pl.ds(start, n), :] = ref[k]

    def half(owner, row):
        return jnp.where(first, whole[owner, row:row + 20, :], whole[owner, row + 20:row + 40, :])

    def iota(shape, dim):
        return lax.broadcasted_iota(jnp.int32, shape, dim)

    cols = iota((1, D), 1)
    rows20, rows96 = pos * 20 + iota((20, 1), 0), pos * 96 + iota((96, 1), 0)
    lanes20, lanes96 = pos * 20 + iota((1, 20), 1), pos * 96 + iota((1, 96), 1)

    def job(out, col, owner, base, i, factor):
        for c in range(5):
            out[:, col + c * 128:col + (c + 1) * 128] = (
                half(owner, base + i * 200 + c * 40) * factor[:, c * 128:(c + 1) * 128])

    def small(base):
        both = whole[0, base + 400:base + 416, :] + whole[1, base + 400:base + 416, :]
        return both, jnp.where(first, both[:, :20], both[:, 20:40])

    def put(out, items):
        for i, (vec, k, factor) in enumerate(items):
            out[i:i + 1, :] = vec[k:k + 1, :] * factor

    c, s, a = 960, 960 + 416, 1792 + 960
    (c_all, c_vec), (_, s_vec), (a_all, a_vec) = small(c), small(s), small(a)
    for is_dec in (True, False):
        lane0 = 4 if is_dec else 0
        scale = functools.partial(usage_scale, cfg, [a_all[15:16, lane0 + g:lane0 + g + 1] for g in range(4)])
        keep_head = scale("keep", rows20, "head", cols)
        head_keep = scale("head", rows20, "keep", cols)
        keep_row = scale("keep", lanes20, None, None)
        head_row = scale("head", lanes20, None, None)
        keep_ffn = scale("keep", rows20, "ffn", iota((1, FF), 1))
        ffn_keep = scale("ffn", rows96, "keep", cols)
        if is_dec:
            gains, shifts, triple, output, query, pair, cross, biases, up, up_bias, down = outs[8:]
            put(gains, ((s_vec, 3, keep_row), (c_vec, 3, keep_row), (c_vec, 0, keep_row)))
            put(shifts, ((s_vec, 4, keep_row), (c_vec, 4, keep_row), (c_vec, 1, keep_row)))
            put(biases, ((s_vec, 5, head_row), (s_vec, 6, head_row), (s_vec, 7, keep_row),
                         (c_vec, 5, head_row), (c_vec, 6, head_row), (c_vec, 7, keep_row), (c_vec, 2, keep_row)))
            job(query, 0, 1, c, 0, keep_head)
            job(pair, 0, 0, c, 0, keep_head)
            job(pair, D, 0, c, 1, keep_head)
            job(cross, 0, 1, c, 1, head_keep)
            att, ffn, bias = s, 0, c_all
        else:
            gains, shifts, triple, output, biases, up, up_bias, down = outs[:8]
            put(gains, ((a_vec, 3, keep_row), (a_vec, 0, keep_row)))
            put(shifts, ((a_vec, 4, keep_row), (a_vec, 1, keep_row)))
            put(biases, ((a_vec, 5, head_row), (a_vec, 6, head_row), (a_vec, 7, keep_row), (a_vec, 2, keep_row)))
            att, ffn, bias = a, 1792, a_all
        job(triple, 0, 0, att, 0, keep_head)
        job(triple, D, 0, att, 1, keep_head)
        job(triple, 2 * D, 1, att, 0, keep_head)
        job(output, 0, 1, att, 1, head_keep)
        for t in range(24):
            up[:, t * 128:(t + 1) * 128] = half(0, ffn + t * 40) * keep_ffn[:, t * 128:(t + 1) * 128]
        for j in range(3):
            for t in range(5):
                start = pl.multiple_of(core * 480 + (ffn + j * 160 + t * 32), 32)
                down[j * 32:(j + 1) * 32, t * 128:(t + 1) * 128] = (
                    whole[1, pl.ds(start, 32), :] * ffn_keep[j * 32:(j + 1) * 32, t * 128:(t + 1) * 128])
        bias_row = jnp.where(first, bias[8:9, :96], bias[9:10, :96])
        up_bias[...] = bias_row * scale("ffn", lanes96, None, None)


SMEM = pl.BlockSpec(memory_space=pltpu.SMEM)
VMEM = pl.BlockSpec(memory_space=pltpu.VMEM)
ANY = pl.BlockSpec(memory_space=pl.ANY)
HBM = pl.BlockSpec(memory_space=pltpu.HBM)


def arr(*shape):
    return jax.ShapeDtypeStruct(shape, f32)


def hbm(*shape):
    return pltpu.HBM(shape, f32)


def call(kernel, in_specs, outs, name, scratch=(), limit=56, flops=1 << 20, nbytes=1 << 20, out_spec=None):
    return pl.pallas_call(
        kernel,
        in_specs=in_specs,
        out_shape=outs,
        out_specs=out_spec or [VMEM] * len(outs),
        scratch_shapes=list(scratch),
        name=name,
        compiler_params=pltpu.CompilerParams(vmem_limit_bytes=limit << 20),
        cost_estimate=pl.CostEstimate(flops=flops, bytes_accessed=nbytes, transcendentals=0),
    )


def in_hbm(*arrays):
    return tuple(pltpu.with_memory_space_constraint(a, pltpu.HBM) for a in arrays)


def flat_perm(move):
    pairs = []
    for x in range(4):
        for y in range(4):
            for z in range(4):
                for c in range(2):
                    X, Y, Z, C = move(x, y, z, c)
                    pairs.append((x * 32 + y * 8 + z * 2 + c, (X % 4) * 32 + (Y % 4) * 8 + (Z % 4) * 2 + C % 2))
    return pairs


SWAP = flat_perm(lambda x, y, z, c: (x, y, z, 1 - c))
RING = {
    "x": flat_perm(lambda x, y, z, c: (x + 1 - 2 * c, y, z, c)),
    "y": flat_perm(lambda x, y, z, c: (x, y + 1 - 2 * c, z, c)),
    "z": flat_perm(lambda x, y, z, c: (x, y, z + 1 - 2 * c, c)),
}
HOP_X = [flat_perm(lambda x, y, z, c, k=k: (x + k - 2 * c * k, y, z, c)) for k in range(4)]


def turn(p, c):
    return p + (1 - 2 * c) * (1 - 2 * (p & 1))


PAIR = {
    "x": (flat_perm(lambda x, y, z, c: (turn(x, c), y, z, c)), flat_perm(lambda x, y, z, c: (x + 2, y, z, c))),
    "y": (flat_perm(lambda x, y, z, c: (x, turn(y, c), z, c)), flat_perm(lambda x, y, z, c: (x, y + 2, z, c))),
    "z": (flat_perm(lambda x, y, z, c: (x, y, turn(z, c), c)), flat_perm(lambda x, y, z, c: (x, y, z + 2, c))),
}


def move(x, perm):
    return lax.ppermute(x, MESH_AXES, perm)


def barrier(*trees):
    return lax.optimization_barrier(trees)


class Part:
    def __init__(self, array, rows, order, dims):
        self.array, self.rows, self.order, self.dims = array, rows, list(order), list(dims)
        self.step, self.got = 0, []

    @property
    def size(self):
        return self.rows[1] - self.rows[0]


def advance(parts, name):
    inputs = []

    def slot(array):
        for n, a in enumerate(inputs):
            if a is array:
                return n
        inputs.append(array)
        return len(inputs) - 1

    plans, routes, out_shapes = [], {}, []
    for part in parts:
        axis = part.order[0]
        d = part.dims.index(axis)
        plan = dict(src=slot(part.array), rows=part.rows, d=d, axis=axis, step=part.step, nd=len(part.dims),
                    got=[(slot(a), off) for a, off in part.got], m=part.size)
        if part.step == 2:
            plan["out"] = len(out_shapes)
            out_shapes.append((4,) * (len(part.dims) - 1) + (part.size, 128))
            if len(part.order) > 1:
                plan["next_axis"] = part.order[1]
                rest = [t for t in part.dims if t != axis]
                plan["next_d"] = rest.index(part.order[1])
        plans.append(plan)
        send_axis, kind = (axis, part.step) if part.step < 2 else (plan.get("next_axis"), 0)
        if send_axis is not None:
            nd = plan["nd"] if part.step < 2 else plan["nd"] - 1
            chunk_rows = 4 ** (nd - 1) * part.size
            route = routes.setdefault((send_axis, kind), [0, []])
            plan["route"], plan["offset"], plan["chunk"] = (send_axis, kind), route[0], chunk_rows
            route[0] += chunk_rows * (2 if kind == 0 else 1)
    n_state = len(out_shapes)
    route_list = list(routes)
    out_shapes += [(routes[r][0], 128) for r in route_list]
    n_in = len(inputs)

    def kernel(*refs):
        ins, outs = refs[:n_in], refs[n_in:]
        pos = lax.axis_index("dp")
        core = pos & 1
        place = {"x": lax.axis_index("sub"), "y": pos >> 3, "z": (pos >> 1) & 3}

        def chunk(ref, nd, d, k, rows):
            index = [slice(None)] * nd
            index[d] = k & 3
            return ref[tuple(index) + (slice(*rows), slice(None))].reshape(-1, 128)

        for plan in plans:
            src, nd, d, rows, m = ins[plan["src"]], plan["nd"], plan["d"], plan["rows"], plan["m"]
            p = place[plan["axis"]]
            n = 4 ** (nd - 1) * m
            got = [(ins[i], off) for i, off in plan["got"]]
            out = outs[n_state + route_list.index(plan["route"])] if "route" in plan else None
            off = plan.get("offset")
            if plan["step"] == 0:
                q = turn(p, core)
                out[off:off + n, :] = chunk(src, nd, d, q, rows)
                out[off + n:off + 2 * n, :] = chunk(src, nd, d, q + 2, rows)
            elif plan["step"] == 1:
                (a, a_off), = got
                out[off:off + n, :] = chunk(src, nd, d, p + 2, rows) + a[a_off + n:a_off + 2 * n, :]
            else:
                (a, a_off), (b, b_off) = got
                total = chunk(src, nd, d, p, rows) + a[a_off:a_off + n, :] + b[b_off:b_off + n, :]
                state = outs[plan["out"]]
                state[...] = total.reshape(state.shape)
                if out is not None:
                    nn = plan["chunk"]
                    q = turn(place[plan["next_axis"]], core)
                    out[off:off + nn, :] = chunk(state, nd - 1, plan["next_d"], q, (0, m))
                    out[off + nn:off + 2 * nn, :] = chunk(state, nd - 1, plan["next_d"], q + 2, (0, m))

    outs = call(kernel, [VMEM] * n_in, [arr(*t) for t in out_shapes], name, limit=24)(*inputs)
    sent = {r: move(outs[n_state + i], PAIR[r[0]][r[1]]) for i, r in enumerate(route_list)}
    for part, plan in zip(parts, plans):
        if part.step == 2:
            part.array, part.rows = outs[plan["out"]], (0, part.size)
            part.dims.remove(part.order.pop(0))
            part.step, part.got = 0, []
        if "route" in plan:
            part.got.append((plan["route"], plan["offset"]))
            part.step += 1
    return sent


def land(parts, sent):
    for part in parts:
        part.got = [(sent[a], off) if isinstance(a, tuple) else (a, off) for a, off in part.got]


def per_device(
    enc_in, prev_enc, dec_in, enc_cotan, dec_cotan, src_lengths, tgt_lengths, configs,
    enc_gains, enc_shifts, enc_triple, enc_output, enc_biases, enc_up, enc_up_bias, enc_down,
    dec_gains, dec_shifts, dec_triple, dec_output, dec_cross_query, dec_cross_pair, dec_cross_out,
    dec_biases, dec_up, dec_up_bias, dec_down,
):
    group = lax.axis_index("sub")
    pos = lax.axis_index("dp")
    core = pos & 1
    place = {"x": group, "y": pos >> 3, "z": (pos >> 1) & 3}
    sign = 1 - 2 * core
    upb = jnp.stack([enc_up_bias, dec_up_bias])
    table = jnp.concatenate([configs.reshape(16), src_lengths.reshape(2), tgt_lengths.reshape(2)])
    x, prev, y = enc_in.reshape(T, D), prev_enc.reshape(T, D), dec_in.reshape(T, D)
    e_cot, d_cot = enc_cotan.reshape(T, D), dec_cotan.reshape(T, D)
    act, act3, prob = arr(T, D), arr(T, 3 * D), arr(2 * H, LEN, LEN)
    act_out = hbm(T, D)
    vmem = pltpu.VMEM
    e_vec = jnp.concatenate([enc_gains.T, enc_shifts.T, enc_biases.T], 0)
    d_vec = jnp.concatenate([dec_gains.T, dec_shifts.T, dec_biases.T], 0)
    head = [SMEM, VMEM]

    encoded, e_qkv, e_p, e_mixed, e_mid, e_z = call(
        encoder_kernel, head + [VMEM] + [HBM] * 5,
        [act_out, hbm(T, 3 * D), hbm(2 * H, LEN, LEN), act_out, act_out, hbm(T, FF)], "encoder_forward", out_spec=[HBM] * 6, scratch=
        [vmem((D, 3 * D), bf16), vmem((D, D), bf16), vmem((D, FF), bf16), vmem((FF, D), bf16),
         vmem((2 * T, D), bf16), vmem((T, D), f32), vmem((T, D), f32),
         vmem((T, D), f32), vmem((T, 3 * D), f32), vmem((2 * H, LEN, LEN), f32), vmem((T, D), f32), vmem((T, D), f32),
         vmem((T, FF), f32), pltpu.SemaphoreType.DMA((5,)), pltpu.SemaphoreType.DMA((6,))], limit=30, flops=8 << 30, nbytes=24 << 20,
    )(table, e_vec, upb, *in_hbm(x, enc_triple, enc_output, enc_up, enc_down))

    (decoded, d_qkv, d_p, d_mixed, a1, mem, c_qkv, c_p, c_mixed, a2, da2, f_keep, f_send, f_vec, f_upb) = call(
        decoder_kernel, head + [VMEM] * 5 + [HBM] * 8,
        [act_out, hbm(T, 3 * D), hbm(2 * H, LEN, LEN), act_out, act, act, act3, prob, act, act, act,
         arr(T, D + FF), arr(T, D + FF), arr(8, D), arr(1, FF)], "decoder_forward",
        [vmem((D, 3 * D), bf16), vmem((D, D), bf16), vmem((D, D), bf16), vmem((D, 2 * D), bf16),
         vmem((D, D), bf16), vmem((D, FF), bf16), vmem((FF, D), bf16),
         vmem((2 * T, D), bf16), vmem((T, D), f32), vmem((T, FF), f32), vmem((T, D), f32),
         vmem((T, D), f32), vmem((T, 3 * D), f32), vmem((2 * H, LEN, LEN), f32), vmem((T, D), f32),
         pltpu.SemaphoreType.DMA((8,)), pltpu.SemaphoreType.DMA((4,))], limit=32, out_spec=[HBM] * 4 + [VMEM] * 11, flops=16 << 30, nbytes=48 << 20,
    )(table, d_vec, upb, y, prev, x, d_cot,
      *in_hbm(encoded, dec_triple, dec_output, dec_cross_query, dec_cross_pair, dec_cross_out, dec_up, dec_down))

    def ffn_grad(kept, got, rows, name, pinned=False):
        whole = pl.BlockSpec((T, D + FF), lambda j: (0, 0), pipeline_mode=pl.Buffered(1))
        return pl.pallas_call(
            ffn_grad_kernel,
            grid=(6,),
            in_specs=[whole, whole],
            out_shape=pltpu.HBM((16, rows, 128), f32) if pinned else arr(16, rows, 128),
            out_specs=pl.BlockSpec((16, 160, 128), lambda j: (0, j, 0)),
            scratch_shapes=[vmem((2, D, 2 * T), bf16), vmem((2, 2 * T, FF), bf16), vmem((2, 2 * T, D), bf16),
                            vmem((2, 16, 192, 2 * T), bf16)],
            name=name,
            compiler_params=pltpu.CompilerParams(vmem_limit_bytes=26 << 20),
            cost_estimate=pl.CostEstimate(flops=6 << 30, bytes_accessed=16 << 20, transcendentals=0),
        )(kept, got)

    def att_grad(with_ffn, whole, operands, name, pinned=False):
        n = len(with_ffn)
        return pl.pallas_call(
            functools.partial(att_grad_kernel, with_ffn),
            in_specs=[SMEM, ANY] + [VMEM] * len(operands),
            out_shape=pltpu.HBM(whole.shape, f32) if pinned else arr(*whole.shape),
            out_specs=ANY,
            scratch_shapes=[vmem((16, ROWS_ATT * n, 128), f32), pltpu.SemaphoreType.DMA((n,))],
            input_output_aliases={1: 0},
            name=name,
            compiler_params=pltpu.CompilerParams(vmem_limit_bytes=24 << 20),
            cost_estimate=pl.CostEstimate(flops=3 << 30, bytes_accessed=10 << 20, transcendentals=0),
        )(table, whole, *operands)

    pair = arr(T, 4 * D)
    f_recv = move(f_send, SWAP)
    da1, dmem, dprev, c_keep, c_send, c_vec = call(
        cross_back_kernel, head + [VMEM] * 9, [act, act, act_out, pair, pair, arr(8, D)], "cross_backward", [vmem((2 * H, LEN, LEN), f32)], limit=14, flops=3 << 30, nbytes=16 << 20,
    )(table, d_vec, da2, a1, mem, c_qkv, c_p, c_mixed, dec_cross_query, dec_cross_pair, dec_cross_out)
    c_recv = move(c_send, SWAP)
    dy_in, s_keep, s_send, s_vec = call(
        functools.partial(self_back_kernel, 0, 3, False), head + [VMEM] * 8,
        [act_out, pair, pair, arr(8, D)], "self_backward", [vmem((2 * H, LEN, LEN), f32)], limit=14, flops=3 << 30, nbytes=16 << 20,
    )(table, d_vec, da1, y, d_qkv, d_p, d_mixed, dmem, dec_triple, dec_output)
    f_recv, s_send, s_keep, c_recv, dmem = barrier(f_recv, s_send, s_keep, c_recv, dmem)
    s_recv = move(s_send, SWAP)
    g_d = ffn_grad(f_keep, f_recv, ROWS_FFN + 2 * ROWS_ATT, "decoder_ffn_grad", True)
    g_d, s_recv = barrier(g_d, s_recv)
    g_d = att_grad((True, False), g_d, (c_keep, c_recv, c_vec, f_vec, f_upb, s_keep, s_recv, s_vec),
                   "decoder_attention_grad", True)
    cores = [[2 * i + c for i in range(16)] for c in range(2)]
    g_d, dmem = barrier(g_d, dmem)
    r_d = lax.psum_scatter(g_d, "dp", scatter_dimension=0, axis_index_groups=cores, tiled=True)

    dmid, h_keep, h_send, h_vec, h_upb = call(
        encoder_ffn_back_kernel, head + [HBM] * 6,
        [act, arr(T, D + FF), arr(T, D + FF), arr(8, D), arr(1, FF)], "encoder_ffn_backward",
        [vmem((D, FF), bf16), vmem((FF, D), bf16), vmem((2 * T, D), bf16), vmem((T, D), f32),
         vmem((T, D), f32), vmem((T, D), f32), vmem((T, D), f32), vmem((T, FF), f32),
         pltpu.SemaphoreType.DMA((3, FF // TILE)), pltpu.SemaphoreType.DMA((3,))], limit=24, flops=4 << 30, nbytes=24 << 20,
    )(table, e_vec, *in_hbm(e_cot, dmem, e_mid, e_z, enc_up, enc_down))
    h_recv = move(h_send, SWAP)
    dx_in, e_keep, e_send, e_vec_sum = call(
        functools.partial(self_back_kernel, 0, 2, True), head + [VMEM] * 8,
        [act_out, pair, pair, arr(8, D)], "encoder_attention_backward", [vmem((2 * H, LEN, LEN), f32)], limit=14, flops=3 << 30, nbytes=16 << 20,
    )(table, e_vec, dmid, x, e_qkv, e_p, e_mixed, dmem, enc_triple, enc_output)
    h_recv, e_send, e_keep = barrier(h_recv, e_send, e_keep)
    e_recv = move(e_send, SWAP)
    g_e = ffn_grad(h_keep, h_recv, ROWS_FFN + ROWS_ATT, "encoder_ffn_grad")
    g_e, e_recv = barrier(g_e, e_recv)
    g_e = att_grad((True,), g_e, (e_keep, e_recv, e_vec_sum, h_vec, h_upb), "encoder_attention_grad")

    g_e = g_e.reshape(4, 4, 4, 344, 128)
    enc_parts = [Part(g_e, rows, order, "yzx")
                 for rows, order in (((0, 184), "xyz"), ((184, 264), "yzx"), ((264, 344), "zxy"))]
    def settle(parts, sent, *others):
        keys = list(sent)
        arrived, others = barrier([sent[k] for k in keys], others)
        land(parts, dict(zip(keys, arrived)))
        return others

    def gather(parts):
        own = jnp.concatenate([p.array for p in parts], 0) if len(parts) > 1 else parts[0].array
        return [own] + [move(own, HOP_X[k]) for k in (1, 2, 3)]

    dec_parts, pieces = [], []
    for step in range(7):
        if step == 3:
            dec_parts = [Part(r_d.reshape(4, 448, 128), (0, 448), "x", "x")]
        active = [p for p in enc_parts + dec_parts if p.order]
        sent = advance(active, "step_%d" % step)
        if step == 2:
            (r_d,) = settle(active, sent, r_d)
        elif step == 5:
            pieces = settle(active, sent, *gather(dec_parts))
        elif step < 6:
            settle(active, sent)

    mine_d = jnp.stack(pieces, 0)
    other_d = move(mine_d, SWAP)
    pieces = gather(enc_parts)
    pieces, other_d = barrier(pieces, other_d)
    mine_e = jnp.stack(pieces, 0)
    other_e = move(mine_e, SWAP)

    enc_shapes = ((2, 20), (2, 20), (20, 3 * D), (20, D), (4, 20), (20, FF), (1, 96), (96, D))
    dec_shapes = ((3, 20), (3, 20), (20, 3 * D), (20, D), (20, D), (20, 2 * D), (20, D), (7, 20), (20, FF),
                  (1, 96), (96, D))
    grads = call(
        finish_kernel, [SMEM] + [VMEM] * 4, [arr(*t) for t in enc_shapes + dec_shapes], "finish",
        [vmem((2, 3168, 128), f32)], limit=24,
    )(table, mine_d, other_d, mine_e, other_e)
    grads = tuple(t.reshape(96) if t.shape == (1, 96) else t.T if t.shape[1] == 20 else t for t in grads)
    whole = (1, SENT, LEN, D)
    return (
        (encoded.reshape(whole), decoded.reshape(whole), dx_in.reshape(whole), dprev.reshape(whole),
         dy_in.reshape(whole)) + grads
    )


def solution(mesh):
    acts = P("sub", "dp", None, None)
    counts = P("sub", "dp")
    row, vector = P("dp", None), P("dp")
    in_specs = (acts,) * 5 + (counts,) * 2 + (P(),) * 20
    out_specs = (acts,) * 5 + (row,) * 6 + (vector, row) + (row,) * 9 + (vector, row)
    return jax.shard_map(per_device, mesh=mesh, in_specs=in_specs, out_specs=out_specs, check_vma=False)
```

```python
import functools
import math

import jax
import jax.numpy as jnp
from jax import lax
from jax.experimental import pallas as pl
from jax.experimental.pallas import tpu as pltpu
from jax.sharding import PartitionSpec as P

D = 640
H = 8
FF = 3072
LEN = 128
HD = 80
SENT = 2
T = SENT * LEN
TILE = 1024
ROWS_FFN = 960
ROWS_ATT = 416
f32 = jnp.float32
bf16 = jnp.bfloat16
NN = (((1,), (0,)), ((), ()))
NT = (((1,), (1,)), ((), ()))
TN = (((0,), (0,)), ((), ()))
MESH_AXES = ("sub", "dp")


def split(x):
    hi = x.astype(bf16)
    lo = (x - hi.astype(f32)).astype(bf16)
    return hi, lo


def stacked(x):
    return jnp.concatenate(split(x), 0)


def halves(r):
    n = r.shape[0] // 2
    return r[:n] + r[n:]


def mm(xs, w, dims=NN):
    return halves(lax.dot_general(xs, w, dims, preferred_element_type=f32))


def dot3(a, b, dims):
    ah, al = a
    bh, bl = b
    dg = functools.partial(lax.dot_general, dimension_numbers=dims, preferred_element_type=f32)
    if dims == NN:
        return dg(jnp.concatenate([al, ah, ah], 1), jnp.concatenate([bh, bl, bh], 0))
    return dg(al, bh) + dg(ah, bl) + dg(ah, bh)


def lane_mask(width, limit):
    return (lax.broadcasted_iota(jnp.int32, (1, width), 1) < limit).astype(f32)


def row_ok(len0, len1):
    row = lax.broadcasted_iota(jnp.int32, (T, 1), 0)
    limit = jnp.where(row < LEN, len0, LEN + len1)
    return (row < limit).astype(f32)


def norm(x, keep, width):
    mean = jnp.sum(x * keep, -1, keepdims=True) / width
    centred = (x - mean) * keep
    var = jnp.sum(centred * centred, -1, keepdims=True) / width
    rstd = lax.rsqrt(var + 1e-5)
    return centred * rstd, rstd


def norm_back(dy, n, rstd, gain, keep, width):
    dy = dy * keep
    dz = dy * gain
    m1 = jnp.sum(dz, -1, keepdims=True) / width
    m2 = jnp.sum(dz * n, -1, keepdims=True) / width
    dx = keep * rstd * (dz - m1 - n * m2)
    return dx, jnp.sum(dy * n, 0, keepdims=True), jnp.sum(dy, 0, keepdims=True)


def bell(z):
    cdf = 0.5 * (1.0 + lax.erf(z * (1.0 / math.sqrt(2.0))))
    pdf = jnp.exp(-0.5 * z * z) * (1.0 / math.sqrt(2.0 * math.pi))
    return cdf, pdf


def rows_of(pair, s, repeat):
    return jnp.concatenate([pair[i][s * LEN:(s + 1) * LEN] for i in repeat], 0)


def head(x, h):
    return x[:, h * HD:(h + 1) * HD]


def corners(r):
    return (r[LEN:, LEN:] + r[LEN:, :LEN]) + (r[:LEN, LEN:] + r[:LEN, :LEN])


def three(x):
    hi, lo = split(x)
    return jnp.concatenate([hi, lo, hi], 1)


def beside(pair, s, h):
    hi, lo = (head(x[s * LEN:(s + 1) * LEN], h) for x in pair)
    return jnp.concatenate([hi, jnp.zeros((LEN, LEN - HD), bf16), lo], 1)


def times(x, right):
    r = dot(stacked(x), right, NN)
    return (r[LEN:, :HD] + r[:LEN, LEN:]) + r[:LEN, :HD]


def dot(a, b, dims):
    return lax.dot_general(a, b, dims, preferred_element_type=f32)


def attend(q, k, v, lens, causal, p_ref):
    qs, ks, vs = split(q * (1.0 / math.sqrt(HD))), split(k), split(v)
    col = lax.broadcasted_iota(jnp.int32, (LEN, LEN), 1)
    for s in range(SENT):
        allowed = col < lens[s]
        if causal:
            allowed = allowed & (lax.broadcasted_iota(jnp.int32, (LEN, LEN), 0) >= col)
        q2, k2 = rows_of(qs, s, (0, 1)), rows_of(ks, s, (0, 1))
        for h in range(H):
            p_ref[s * H + h] = jnp.where(allowed, corners(dot(head(q2, h), head(k2, h), NT)), -1e30)
    for i in range(SENT * H):
        scores = p_ref[i]
        e = jnp.exp(scores - jnp.max(scores, -1, keepdims=True))
        p_ref[i] = e * (1.0 / jnp.sum(e, -1, keepdims=True))
    rows = []
    for s in range(SENT):
        v3 = rows_of(vs, s, (0, 0, 1))
        rows.append(jnp.concatenate([dot(three(p_ref[s * H + h]), head(v3, h), NN) for h in range(H)], 1))
    return jnp.concatenate(rows, 0)


def attend_back(do, q, k, v, p_ref, ds_ref):
    scale = 1.0 / math.sqrt(HD)
    dos, qs, ks, vs = split(do), split(q * scale), split(k * scale), split(v)
    for s in range(SENT):
        do2, v2 = rows_of(dos, s, (0, 1)), rows_of(vs, s, (0, 1))
        for h in range(H):
            ds_ref[s * H + h] = corners(dot(head(do2, h), head(v2, h), NT))
    for i in range(SENT * H):
        prob, dp = p_ref[i], ds_ref[i]
        ds_ref[i] = prob * (dp - jnp.sum(dp * prob, -1, keepdims=True))
    all_q, all_k, all_v = [], [], []
    for s in range(SENT):
        ids = [(s * H + h, h) for h in range(H)]
        all_q.append(jnp.concatenate([times(ds_ref[i], beside(ks, s, h)) for i, h in ids], 1))
        all_k.append(jnp.concatenate([times(ds_ref[i].T, beside(qs, s, h)) for i, h in ids], 1))
        all_v.append(jnp.concatenate([times(p_ref[i].T, beside(dos, s, h)) for i, h in ids], 1))
    return tuple(jnp.concatenate(x, 0) for x in (all_q, all_k, all_v))


def ffn_forward(ns, up, bias, bias_row, down, ffn_limit, z_ref, acc_ref):
    acc_ref[...] = jnp.zeros_like(acc_ref)

    def body(j, _):
        sl = pl.ds(pl.multiple_of(j * TILE, TILE), TILE)
        z = mm(ns[...], up[:, sl]) + bias[bias_row:bias_row + 1, sl].astype(f32)
        z_ref[:, sl] = z
        mask = (lax.broadcasted_iota(jnp.int32, (1, TILE), 1) + j * TILE < ffn_limit).astype(f32)
        u = z * bell(z)[0] * mask
        acc_ref[...] += mm(stacked(u), down[sl, :])
        return 0

    lax.fori_loop(0, FF // TILE, body, 0)


def ffn_backward(dyk, n, z_ref, up, down, ffn_limit, core, dys_ref, keep_ref, send_ref, bias_ref, acc_ref,
                 arrive=None):
    acc_ref[...] = jnp.zeros_like(acc_ref)
    dys_ref[...] = stacked(dyk)
    first = core == 0
    keep_ref[:, :D] = jnp.where(first, n, dyk)
    send_ref[:, :D] = jnp.where(first, dyk, n)

    def body(j, _):
        sl = pl.ds(pl.multiple_of(j * TILE, TILE), TILE)
        out = pl.ds(pl.multiple_of(j * TILE + D, 128), TILE)
        if arrive is not None:
            arrive(sl, j)
        du = mm(dys_ref[...], down[sl, :], NT)
        z = z_ref[:, sl]
        cdf, pdf = bell(z)
        mask = (lax.broadcasted_iota(jnp.int32, (1, TILE), 1) + j * TILE < ffn_limit).astype(f32)
        u = z * cdf * mask
        dz = du * mask * (cdf + z * pdf)
        keep_ref[:, out] = jnp.where(first, dz, u)
        send_ref[:, out] = jnp.where(first, u, dz)
        bias_ref[:, sl] = jnp.sum(dz, 0, keepdims=True)
        acc_ref[...] += mm(stacked(dz), up[:, sl], NT)
        return 0

    lax.fori_loop(0, FF // TILE, body, 0)


def load_vectors(ref):
    return ref[...].astype(f32)


def setting(table):
    g = lax.axis_index("sub")
    core = lax.axis_index("dp") & 1
    c = table[4 * g + 3]
    bits = [(c & 1).astype(f32), ((c >> 1) & 1).astype(f32), ((c >> 2) & 1).astype(f32)]
    total = bits[0] + bits[1] + bits[2]
    sc = (table[4 * g], table[4 * g + 1] * HD, table[4 * g + 2], table[16], table[17], table[18], table[19], core)
    return sc, [b / total for b in bits]


def fetch(pairs, sems):
    copies = [pltpu.make_async_copy(a, b, sems.at[i]) for i, (a, b) in enumerate(pairs)]
    for c in copies:
        c.start()
    return copies


def encoder_kernel(table, vec_ref, upb, x_ref, w_triple, w_out, w_up, w_down,
                   o_encoded, o_qkv, o_p, o_mixed, o_middle, o_z,
                   b_triple, b_out, b_up, b_down, ns_ref, acc_ref, b_x,
                   encoded, qkv, p_ref, mixed, middle, z_ref, sems, out_sems):
    read_x, *copies = fetch([(x_ref, b_x), (w_triple, b_triple), (w_out, b_out), (w_up, b_up), (w_down, b_down)], sems)
    leaving = []

    def leave(src, dst):
        copy = pltpu.make_async_copy(src, dst, out_sems.at[len(leaving)])
        copy.start()
        leaving.append(copy)

    sc, pick = setting(table)
    width = sc[0].astype(f32)
    keep, heads = lane_mask(D, sc[0]), lane_mask(D, sc[1])
    vec = load_vectors(vec_ref)
    read_x.wait()
    x = b_x[...]
    n, _ = norm(x, keep, width)
    ns = stacked((n * vec[0:1] + vec[2:3]) * keep)
    copies[0].wait()
    qkv[:, :D] = (mm(ns, b_triple[:, :D]) + vec[4:5]) * heads
    qkv[:, D:2 * D] = mm(ns, b_triple[:, D:2 * D]) * heads
    qkv[:, 2 * D:] = (mm(ns, b_triple[:, 2 * D:]) + vec[5:6]) * heads
    leave(qkv, o_qkv)
    o = attend(qkv[:, :D], qkv[:, D:2 * D], qkv[:, 2 * D:], (sc[3], sc[4]), False, p_ref)
    mixed[...] = o
    leave(p_ref, o_p)
    leave(mixed, o_mixed)
    copies[1].wait()
    mid = x + (mm(stacked(o), b_out[...]) + vec[6:7]) * keep
    middle[...] = mid
    leave(middle, o_middle)
    n, _ = norm(mid, keep, width)
    ns_ref[...] = stacked((n * vec[1:2] + vec[3:4]) * keep)
    copies[2].wait()
    copies[3].wait()
    ffn_forward(ns_ref, b_up, upb, 0, b_down, sc[2], z_ref, acc_ref)
    leave(z_ref, o_z)
    encoded[...] = (middle[...] + (acc_ref[...] + vec[7:8]) * keep) * row_ok(sc[3], sc[4])
    leave(encoded, o_encoded)
    for copy in leaving:
        copy.wait()


def decoder_kernel(table, vec_ref, upb, x_ref, prev_ref, src_ref, cot_ref, enc_in,
                   w_triple, w_out, w_query, w_pair, w_cross, w_up, w_down,
                   o_decoded, o_qkv, o_p, o_mixed, a1_ref, mem_ref, qkv_c, p_cross, mixed_c, da2_ref,
                   o_keep, send_buf, dvec, dupb,
                   b_triple, b_out, b_query, b_pair, b_cross, b_up, b_down, ns_ref, acc_ref, z_ref, enc_ref,
                   decoded, qkv, p_self, mixed, a2_ref, keep_buf, sems, out_sems):
    copies = fetch([(w_triple, b_triple), (w_out, b_out), (w_query, b_query), (w_pair, b_pair),
                    (w_cross, b_cross), (w_up, b_up), (w_down, b_down), (enc_in, enc_ref)], sems)
    leaving = []

    def leave(src, dst):
        copy = pltpu.make_async_copy(src, dst, out_sems.at[len(leaving)])
        copy.start()
        leaving.append(copy)

    sc, pick = setting(table)
    width = sc[0].astype(f32)
    keep, heads = lane_mask(D, sc[0]), lane_mask(D, sc[1])
    vec = load_vectors(vec_ref)
    x = x_ref[...]
    n, _ = norm(x, keep, width)
    ns = stacked((n * vec[0:1] + vec[3:4]) * keep)
    copies[0].wait()
    qkv[:, :D] = (mm(ns, b_triple[:, :D]) + vec[6:7]) * heads
    qkv[:, D:2 * D] = mm(ns, b_triple[:, D:2 * D]) * heads
    qkv[:, 2 * D:] = (mm(ns, b_triple[:, 2 * D:]) + vec[7:8]) * heads
    o = attend(qkv[:, :D], qkv[:, D:2 * D], qkv[:, 2 * D:], (sc[5], sc[6]), True, p_self)
    mixed[...] = o
    leave(qkv, o_qkv)
    leave(p_self, o_p)
    leave(mixed, o_mixed)
    copies[1].wait()
    a1 = x + (mm(stacked(o), b_out[...]) + vec[8:9]) * keep
    a1_ref[...] = a1
    n, _ = norm(a1, keep, width)
    ns = stacked((n * vec[1:2] + vec[4:5]) * keep)
    copies[2].wait()
    qkv_c[:, :D] = (mm(ns, b_query[...]) + vec[9:10]) * heads
    copies[7].wait()
    memory = (pick[0] * prev_ref[...] + pick[1] * src_ref[...] + pick[2] * enc_ref[...]) * keep
    mem_ref[...] = memory
    ns = stacked(memory)
    copies[3].wait()
    qkv_c[:, D:2 * D] = mm(ns, b_pair[:, :D]) * heads
    qkv_c[:, 2 * D:] = (mm(ns, b_pair[:, D:]) + vec[10:11]) * heads
    o = attend(qkv_c[:, :D], qkv_c[:, D:2 * D], qkv_c[:, 2 * D:], (sc[3], sc[4]), False, p_cross)
    mixed_c[...] = o
    copies[4].wait()
    a2_ref[...] = a1_ref[...] + (mm(stacked(o), b_cross[...]) + vec[11:12]) * keep
    n, _ = norm(a2_ref[...], keep, width)
    ns_ref[...] = stacked((n * vec[2:3] + vec[5:6]) * keep)
    copies[5].wait()
    copies[6].wait()
    ffn_forward(ns_ref, b_up, upb, 1, b_down, sc[2], z_ref, acc_ref)
    ok = row_ok(sc[5], sc[6])
    decoded[...] = (a2_ref[...] + (acc_ref[...] + vec[12:13]) * keep) * ok
    leave(decoded, o_decoded)
    dy = cot_ref[...] * ok
    dyk = dy * keep
    n, rstd = norm(a2_ref[...], keep, width)
    ffn_backward(dyk, (n * vec[2:3] + vec[5:6]) * keep, z_ref, b_up, b_down, sc[2], sc[7], ns_ref,
                 keep_buf, send_buf, dupb, acc_ref)
    leave(keep_buf, o_keep)
    dx, dg, db = norm_back(acc_ref[...], n, rstd, vec[2:3], keep, width)
    da2_ref[...] = dy + dx
    dvec[...] = jnp.concatenate([dg, db, jnp.sum(dyk, 0, keepdims=True), jnp.zeros((5, D), f32)], 0)
    for copy in leaving:
        copy.wait()


def cross_back_kernel(table, vec_ref, da2_ref, a1_ref, mem_ref, qkv_c, p_cross, mixed_c,
                      w_query, w_pair, w_cross,
                      da1_ref, dmem_ref, dprev_ref, keep_buf, send_buf, dvec, ds_ref):
    sc, pick = setting(table)
    width = sc[0].astype(f32)
    keep, heads = lane_mask(D, sc[0]), lane_mask(D, sc[1])
    vec = load_vectors(vec_ref)
    first = sc[7] == 0
    da2 = da2_ref[...]
    dyk = da2 * keep
    do = mm(stacked(dyk), w_cross[...], NT)
    dq, dk, dv = attend_back(do, qkv_c[:, :D], qkv_c[:, D:2 * D], qkv_c[:, 2 * D:], p_cross, ds_ref)
    dq, dk, dv = dq * heads, dk * heads, dv * heads
    n, rstd = norm(a1_ref[...], keep, width)
    normed = (n * vec[1:2] + vec[4:5]) * keep
    for i, (a, b) in enumerate(((mem_ref[...], normed), (mem_ref[...], mixed_c[...]), (dk, dq), (dv, dyk))):
        keep_buf[:, i * D:(i + 1) * D] = jnp.where(first, a, b)
        send_buf[:, i * D:(i + 1) * D] = jnp.where(first, b, a)
    dn = mm(stacked(dq), w_query[...], NT)
    dx, dg, db = norm_back(dn, n, rstd, vec[1:2], keep, width)
    da1_ref[...] = da2 + dx
    dmem = (mm(stacked(dk), w_pair[:, :D], NT) + mm(stacked(dv), w_pair[:, D:], NT)) * keep
    dmem_ref[...] = dmem
    dprev_ref[...] = dmem * pick[0]
    dvec[...] = jnp.concatenate(
        [dg, db] + [jnp.sum(t, 0, keepdims=True) for t in (dq, dv, dyk)] + [jnp.zeros((3, D), f32)], 0)


def self_back_kernel(gain_row, shift_row, with_memory, table, vec_ref, dy_ref, x_ref, qkv, p_ref, mixed,
                     dmem_ref, w_triple, w_out, dx_ref, keep_buf, send_buf, dvec, ds_ref):
    sc, pick = setting(table)
    width = sc[0].astype(f32)
    keep, heads = lane_mask(D, sc[0]), lane_mask(D, sc[1])
    vec = load_vectors(vec_ref)
    gain, shift = vec[gain_row:gain_row + 1], vec[shift_row:shift_row + 1]
    first = sc[7] == 0
    dy = dy_ref[...]
    dyk = dy * keep
    do = mm(stacked(dyk), w_out[...], NT)
    dq, dk, dv = attend_back(do, qkv[:, :D], qkv[:, D:2 * D], qkv[:, 2 * D:], p_ref, ds_ref)
    dq, dk, dv = dq * heads, dk * heads, dv * heads
    n, rstd = norm(x_ref[...], keep, width)
    normed = (n * gain + shift) * keep
    for i, (a, b) in enumerate(((normed, normed), (normed, mixed[...]), (dq, dv), (dk, dyk))):
        keep_buf[:, i * D:(i + 1) * D] = jnp.where(first, a, b)
        send_buf[:, i * D:(i + 1) * D] = jnp.where(first, b, a)
    dn = mm(stacked(dq), w_triple[:, :D], NT) + mm(stacked(dk), w_triple[:, D:2 * D], NT)
    dn += mm(stacked(dv), w_triple[:, 2 * D:], NT)
    dx, dg, db = norm_back(dn, n, rstd, gain, keep, width)
    dx = dx + dy
    if with_memory:
        dx = dx + pick[1] * dmem_ref[...]
    dx_ref[...] = dx
    dvec[...] = jnp.concatenate(
        [dg, db] + [jnp.sum(t, 0, keepdims=True) for t in (dq, dv, dyk)] + [jnp.zeros((3, D), f32)], 0)


def encoder_ffn_back_kernel(table, vec_ref, h_cot, h_dmem, h_middle, h_z, w_up, w_down,
                            dmid_ref, keep_buf, send_buf, dvec, dupb,
                            b_up, b_down, ns_ref, acc_ref, cot_ref, dmem_ref, middle, z_ref, sems, first_sems):
    first = fetch([(h_cot, cot_ref), (h_dmem, dmem_ref), (h_middle, middle)], first_sems)

    def tile_copies(sl, j):
        return (pltpu.make_async_copy(h_z.at[:, sl], z_ref.at[:, sl], sems.at[2, j]),
                pltpu.make_async_copy(w_down.at[sl, :], b_down.at[sl, :], sems.at[0, j]),
                pltpu.make_async_copy(w_up.at[:, sl], b_up.at[:, sl], sems.at[1, j]))

    for j in range(FF // TILE):
        for copy in tile_copies(pl.ds(j * TILE, TILE), j):
            copy.start()

    def arrive(sl, j):
        for copy in tile_copies(sl, j):
            copy.wait()

    sc, pick = setting(table)
    width = sc[0].astype(f32)
    keep = lane_mask(D, sc[0])
    vec = load_vectors(vec_ref)
    for copy in first:
        copy.wait()
    dy = (cot_ref[...] + pick[2] * dmem_ref[...]) * row_ok(sc[3], sc[4])
    dyk = dy * keep
    n, rstd = norm(middle[...], keep, width)
    ffn_backward(dyk, (n * vec[1:2] + vec[3:4]) * keep, z_ref, b_up, b_down, sc[2], sc[7], ns_ref,
                 keep_buf, send_buf, dupb, acc_ref, arrive)
    dx, dg, db = norm_back(acc_ref[...], n, rstd, vec[1:2], keep, width)
    dmid_ref[...] = dy + dx
    dvec[...] = jnp.concatenate([dg, db, jnp.sum(dyk, 0, keepdims=True), jnp.zeros((5, D), f32)], 0)


WIDE = 768


def ffn_grad_kernel(kept, got, out, at_s, buf_up, buf_down, sems):
    first = (lax.axis_index("dp") & 1) == 0
    for i, ref in enumerate((kept, got)):
        hi, lo = split(ref[:, :D].T)
        at_s[0, :, i * T:(i + 1) * T] = hi
        at_s[1, :, i * T:(i + 1) * T] = lo
    n_up, n_down = WIDE // 128 * 40, WIDE // 192
    left = lax.broadcasted_iota(jnp.int32, (320, 128), 1) < 64

    def up_copy(j, slot):
        rows = pl.ds(pl.multiple_of(j * n_up, 8), n_up)
        return pltpu.make_async_copy(buf_up.at[slot], out.at[:, rows, :], sems.at[slot])

    def down_copy(j, slot):
        rows = pl.ds(0, ROWS_FFN)
        return pltpu.make_async_copy(buf_down.at[slot], out.at[pl.ds(j * n_down, n_down), rows, :], sems.at[slot])

    def body(j, _):
        slot = j & 1
        cols = pl.ds(pl.multiple_of(j * WIDE + D, 128), WIDE)
        r = dot3((at_s[0], at_s[1]), split(jnp.concatenate([kept[:, cols], got[:, cols]], 0)), NN)
        tiles = [r[:, c * 128:(c + 1) * 128] for c in range(WIDE // 128)]

        @pl.when(first)
        def _():
            @pl.when(j >= 2)
            def _():
                up_copy(j - 2, slot).wait()

            for c, t in enumerate(tiles):
                buf_up[slot, :, c * 40:(c + 1) * 40, :] = t.reshape(16, 40, 128)
            up_copy(j, slot).start()

        @pl.when(jnp.logical_not(first))
        def _():
            @pl.when(j >= 2)
            def _():
                down_copy(j - 2, slot).wait()

            for p in range(n_down // 2):
                a, shared, b = tiles[3 * p:3 * p + 3]
                upper, lower = shared[:320], shared[320:]
                buf_down[slot, 2 * p, :D, :] = a
                buf_down[slot, 2 * p, D:, :] = jnp.where(left, upper, pltpu.roll(lower, 64, 1))
                buf_down[slot, 2 * p + 1, :D, :] = b
                buf_down[slot, 2 * p + 1, D:, :] = jnp.where(left, pltpu.roll(upper, 64, 1), lower)
            down_copy(j, slot).start()

        return 0

    steps = FF // WIDE
    lax.fori_loop(0, steps, body, 0)

    @pl.when(first)
    def _():
        for j in (steps - 2, steps - 1):
            up_copy(j, j & 1).wait()

    @pl.when(jnp.logical_not(first))
    def _():
        for j in (steps - 2, steps - 1):
            down_copy(j, j & 1).wait()


def small_block(out, base, ffn_vec, att_vec, upb, counts, group):
    lane = lax.broadcasted_iota(jnp.int32, (1, 128), 1)
    totals = jnp.where(lane == group, counts[0], 0) + jnp.where(lane == group + 4, counts[1], 0)
    totals = totals.astype(f32)
    for b in range(16):
        out[b, base:base + 16, :] = jnp.zeros((16, 128), f32)
        if ffn_vec is not None:
            out[b, base:base + 3, :40] = ffn_vec[:3, b * 40:(b + 1) * 40]
        out[b, base + 3:base + 8, :40] = att_vec[:5, b * 40:(b + 1) * 40]
        if upb is not None:
            for c in range(2):
                out[b, base + 8 + c:base + 9 + c, :96] = upb[:, b * 192 + c * 96:b * 192 + (c + 1) * 96]
        out[b, base + 15:base + 16, :] = totals


def att_grad_kernel(with_ffn, *refs):
    table = refs[0]
    whole, out, sem = refs[-3:]
    refs = list(refs[2:-3])
    group = lax.axis_index("sub")
    counts = (table[16] + table[17], table[18] + table[19])
    copies = []
    for n, ffn in enumerate(with_ffn):
        kept, got, att_vec = refs[:3]
        ffn_vec, upb = (refs[3], refs[4]) if ffn else (None, None)
        refs = refs[5 if ffn else 3:]
        base = n * ROWS_ATT
        small_block(out, base + 400, ffn_vec, att_vec, upb, counts, group)
        for i in range(2):
            a = jnp.concatenate([kept[:, i * D:(i + 1) * D].T, got[:, i * D:(i + 1) * D].T], 1)
            b = jnp.concatenate([kept[:, (i + 2) * D:(i + 3) * D], got[:, (i + 2) * D:(i + 3) * D]], 0)
            a, b = split(a), split(b)
            r = dot3(a, b, NN)
            for c in range(5):
                row = base + i * 200 + c * 40
                out[:, row:row + 40, :] = r[:, c * 128:(c + 1) * 128].reshape(16, 40, 128)
        copy = pltpu.make_async_copy(
            out.at[:, pl.ds(base, ROWS_ATT), :], whole.at[:, pl.ds(ROWS_FFN + base, ROWS_ATT), :], sem.at[n])
        copy.start()
        copies.append(copy)
    for copy in copies:
        copy.wait()


def usage_scale(cfg, totals, row_kind, rows, col_kind, cols):
    limit = {"keep": lambda g: cfg[4 * g], "head": lambda g: cfg[4 * g + 1] * HD, "ffn": lambda g: cfg[4 * g + 2]}
    usage = 0.0
    for g in range(4):
        part = jnp.where(rows < limit[row_kind](g), totals[g], 0.0)
        if col_kind is not None:
            part = jnp.where(cols < limit[col_kind](g), part, 0.0)
        usage = usage + part
    return lax.rsqrt(usage)


def finish_kernel(cfg, mine_d, other_d, mine_e, other_e, *refs):
    whole = refs[-1]
    outs = refs[:-1]
    pos = lax.axis_index("dp")
    px = lax.axis_index("sub")
    core = pos & 1
    sign = 1 - 2 * core
    first = core == 0
    for k in range(4):
        for refs_k, owner, from_x in (((mine_d, mine_e), core, (px - sign * k) & 3),
                                      ((other_d, other_e), 1 - core, (px + sign * k) & 3)):
            for ref, n, base in zip(refs_k, (448, 344), (0, 1792)):
                start = pl.multiple_of(base + from_x * n, 8)
                whole[owner, pl.ds(start, n), :] = ref[k]

    def half(owner, row):
        return jnp.where(first, whole[owner, row:row + 20, :], whole[owner, row + 20:row + 40, :])

    def iota(shape, dim):
        return lax.broadcasted_iota(jnp.int32, shape, dim)

    cols = iota((1, D), 1)
    odd = ((pos >> 1) & 1) == 1
    rows20, rows96 = pos * 20 + iota((20, 1), 0), pos * 96 + iota((96, 1), 0)
    lanes20, lanes96 = pos * 20 + iota((1, 20), 1), pos * 96 + iota((1, 96), 1)

    def job(out, col, owner, base, i, factor):
        for c in range(5):
            out[:, col + c * 128:col + (c + 1) * 128] = (
                half(owner, base + i * 200 + c * 40) * factor[:, c * 128:(c + 1) * 128])

    def small(base):
        both = whole[0, base + 400:base + 416, :] + whole[1, base + 400:base + 416, :]
        return both, jnp.where(first, both[:, :20], both[:, 20:40])

    def put(out, items):
        for i, (vec, k, factor) in enumerate(items):
            out[i:i + 1, :] = vec[k:k + 1, :] * factor

    c, s, a = 960, 960 + 416, 1792 + 960
    (c_all, c_vec), (_, s_vec), (a_all, a_vec) = small(c), small(s), small(a)
    for is_dec in (True, False):
        lane0 = 4 if is_dec else 0
        scale = functools.partial(usage_scale, cfg, [a_all[15:16, lane0 + g:lane0 + g + 1] for g in range(4)])
        keep_head = scale("keep", rows20, "head", cols)
        head_keep = scale("head", rows20, "keep", cols)
        keep_row = scale("keep", lanes20, None, None)
        head_row = scale("head", lanes20, None, None)
        keep_ffn = scale("keep", rows20, "ffn", iota((1, FF), 1))
        ffn_keep = scale("ffn", rows96, "keep", cols)
        if is_dec:
            gains, shifts, triple, output, query, pair, cross, biases, up, up_bias, down = outs[8:]
            put(gains, ((s_vec, 3, keep_row), (c_vec, 3, keep_row), (c_vec, 0, keep_row)))
            put(shifts, ((s_vec, 4, keep_row), (c_vec, 4, keep_row), (c_vec, 1, keep_row)))
            put(biases, ((s_vec, 5, head_row), (s_vec, 6, head_row), (s_vec, 7, keep_row),
                         (c_vec, 5, head_row), (c_vec, 6, head_row), (c_vec, 7, keep_row), (c_vec, 2, keep_row)))
            job(query, 0, 1, c, 0, keep_head)
            job(pair, 0, 0, c, 0, keep_head)
            job(pair, D, 0, c, 1, keep_head)
            job(cross, 0, 1, c, 1, head_keep)
            att, ffn, bias = s, 0, c_all
        else:
            gains, shifts, triple, output, biases, up, up_bias, down = outs[:8]
            put(gains, ((a_vec, 3, keep_row), (a_vec, 0, keep_row)))
            put(shifts, ((a_vec, 4, keep_row), (a_vec, 1, keep_row)))
            put(biases, ((a_vec, 5, head_row), (a_vec, 6, head_row), (a_vec, 7, keep_row), (a_vec, 2, keep_row)))
            att, ffn, bias = a, 1792, a_all
        job(triple, 0, 0, att, 0, keep_head)
        job(triple, D, 0, att, 1, keep_head)
        job(triple, 2 * D, 1, att, 0, keep_head)
        job(output, 0, 1, att, 1, head_keep)
        for t in range(24):
            up[:, t * 128:(t + 1) * 128] = half(0, ffn + t * 40) * keep_ffn[:, t * 128:(t + 1) * 128]
        tile = whole[1, ffn:ffn + D, :].T
        both = whole[1, ffn + D:ffn + ROWS_FFN, :].T
        rest = jnp.concatenate([both[:64], both[64:]], 1)
        units = jnp.where(odd, jnp.concatenate([rest, tile], 0), jnp.concatenate([tile, rest], 0))
        down[...] = jnp.where(first, units[:96], units[96:]) * ffn_keep
        bias_row = jnp.where(first, bias[8:9, :96], bias[9:10, :96])
        up_bias[...] = bias_row * scale("ffn", lanes96, None, None)


SMEM = pl.BlockSpec(memory_space=pltpu.SMEM)
VMEM = pl.BlockSpec(memory_space=pltpu.VMEM)
ANY = pl.BlockSpec(memory_space=pl.ANY)
HBM = pl.BlockSpec(memory_space=pltpu.HBM)


def arr(*shape):
    return jax.ShapeDtypeStruct(shape, f32)


def hbm(*shape):
    return pltpu.HBM(shape, f32)


def call(kernel, in_specs, outs, name, scratch=(), limit=56, flops=1 << 20, nbytes=1 << 20, out_spec=None):
    return pl.pallas_call(
        kernel,
        in_specs=in_specs,
        out_shape=outs,
        out_specs=out_spec or [VMEM] * len(outs),
        scratch_shapes=list(scratch),
        name=name,
        compiler_params=pltpu.CompilerParams(vmem_limit_bytes=limit << 20),
        cost_estimate=pl.CostEstimate(flops=flops, bytes_accessed=nbytes, transcendentals=0),
    )


def in_hbm(*arrays):
    return tuple(pltpu.with_memory_space_constraint(a, pltpu.HBM) for a in arrays)


def flat_perm(move):
    pairs = []
    for x in range(4):
        for y in range(4):
            for z in range(4):
                for c in range(2):
                    X, Y, Z, C = move(x, y, z, c)
                    pairs.append((x * 32 + y * 8 + z * 2 + c, (X % 4) * 32 + (Y % 4) * 8 + (Z % 4) * 2 + C % 2))
    return pairs


SWAP = flat_perm(lambda x, y, z, c: (x, y, z, 1 - c))
RING = {
    "x": flat_perm(lambda x, y, z, c: (x + 1 - 2 * c, y, z, c)),
    "y": flat_perm(lambda x, y, z, c: (x, y + 1 - 2 * c, z, c)),
    "z": flat_perm(lambda x, y, z, c: (x, y, z + 1 - 2 * c, c)),
}
HOP_X = [flat_perm(lambda x, y, z, c, k=k: (x + k - 2 * c * k, y, z, c)) for k in range(4)]


def turn(p, c):
    return p + (1 - 2 * c) * (1 - 2 * (p & 1))


PAIR = {
    "x": (flat_perm(lambda x, y, z, c: (turn(x, c), y, z, c)), flat_perm(lambda x, y, z, c: (x + 2, y, z, c))),
    "y": (flat_perm(lambda x, y, z, c: (x, turn(y, c), z, c)), flat_perm(lambda x, y, z, c: (x, y + 2, z, c))),
    "z": (flat_perm(lambda x, y, z, c: (x, y, turn(z, c), c)), flat_perm(lambda x, y, z, c: (x, y, z + 2, c))),
}


def move(x, perm):
    return lax.ppermute(x, MESH_AXES, perm)


def barrier(*trees):
    return lax.optimization_barrier(trees)


class Part:
    def __init__(self, array, rows, order, dims):
        self.array, self.rows, self.order, self.dims = array, rows, list(order), list(dims)
        self.step, self.got = 0, []

    @property
    def size(self):
        return self.rows[1] - self.rows[0]


def advance(parts, name):
    inputs = []

    def slot(array):
        for n, a in enumerate(inputs):
            if a is array:
                return n
        inputs.append(array)
        return len(inputs) - 1

    plans, routes, out_shapes = [], {}, []
    for part in parts:
        axis = part.order[0]
        d = part.dims.index(axis)
        plan = dict(src=slot(part.array), rows=part.rows, d=d, axis=axis, step=part.step, nd=len(part.dims),
                    got=[(slot(a), off) for a, off in part.got], m=part.size)
        if part.step == 2:
            plan["out"] = len(out_shapes)
            out_shapes.append((4,) * (len(part.dims) - 1) + (part.size, 128))
            if len(part.order) > 1:
                plan["next_axis"] = part.order[1]
                rest = [t for t in part.dims if t != axis]
                plan["next_d"] = rest.index(part.order[1])
        plans.append(plan)
        send_axis, kind = (axis, part.step) if part.step < 2 else (plan.get("next_axis"), 0)
        if send_axis is not None:
            nd = plan["nd"] if part.step < 2 else plan["nd"] - 1
            chunk_rows = 4 ** (nd - 1) * part.size
            route = routes.setdefault((send_axis, kind), [0, []])
            plan["route"], plan["offset"], plan["chunk"] = (send_axis, kind), route[0], chunk_rows
            route[0] += chunk_rows * (2 if kind == 0 else 1)
    n_state = len(out_shapes)
    route_list = list(routes)
    out_shapes += [(routes[r][0], 128) for r in route_list]
    n_in = len(inputs)

    def kernel(*refs):
        ins, outs = refs[:n_in], refs[n_in:]
        pos = lax.axis_index("dp")
        core = pos & 1
        place = {"x": lax.axis_index("sub"), "y": pos >> 3, "z": (pos >> 1) & 3}

        def chunk(ref, nd, d, k, rows):
            index = [slice(None)] * nd
            index[d] = k & 3
            return ref[tuple(index) + (slice(*rows), slice(None))].reshape(-1, 128)

        for plan in plans:
            src, nd, d, rows, m = ins[plan["src"]], plan["nd"], plan["d"], plan["rows"], plan["m"]
            p = place[plan["axis"]]
            n = 4 ** (nd - 1) * m
            got = [(ins[i], off) for i, off in plan["got"]]
            out = outs[n_state + route_list.index(plan["route"])] if "route" in plan else None
            off = plan.get("offset")
            if plan["step"] == 0:
                q = turn(p, core)
                out[off:off + n, :] = chunk(src, nd, d, q, rows)
                out[off + n:off + 2 * n, :] = chunk(src, nd, d, q + 2, rows)
            elif plan["step"] == 1:
                (a, a_off), = got
                out[off:off + n, :] = chunk(src, nd, d, p + 2, rows) + a[a_off + n:a_off + 2 * n, :]
            else:
                (a, a_off), (b, b_off) = got
                total = chunk(src, nd, d, p, rows) + a[a_off:a_off + n, :] + b[b_off:b_off + n, :]
                state = outs[plan["out"]]
                state[...] = total.reshape(state.shape)
                if out is not None:
                    nn = plan["chunk"]
                    q = turn(place[plan["next_axis"]], core)
                    out[off:off + nn, :] = chunk(state, nd - 1, plan["next_d"], q, (0, m))
                    out[off + nn:off + 2 * nn, :] = chunk(state, nd - 1, plan["next_d"], q + 2, (0, m))

    outs = call(kernel, [VMEM] * n_in, [arr(*t) for t in out_shapes], name, limit=24)(*inputs)
    sent = {r: move(outs[n_state + i], PAIR[r[0]][r[1]]) for i, r in enumerate(route_list)}
    for part, plan in zip(parts, plans):
        if part.step == 2:
            part.array, part.rows = outs[plan["out"]], (0, part.size)
            part.dims.remove(part.order.pop(0))
            part.step, part.got = 0, []
        if "route" in plan:
            part.got.append((plan["route"], plan["offset"]))
            part.step += 1
    return sent


def land(parts, sent):
    for part in parts:
        part.got = [(sent[a], off) if isinstance(a, tuple) else (a, off) for a, off in part.got]


def per_device(
    enc_in, prev_enc, dec_in, enc_cotan, dec_cotan, src_lengths, tgt_lengths, configs,
    enc_gains, enc_shifts, enc_triple, enc_output, enc_biases, enc_up, enc_up_bias, enc_down,
    dec_gains, dec_shifts, dec_triple, dec_output, dec_cross_query, dec_cross_pair, dec_cross_out,
    dec_biases, dec_up, dec_up_bias, dec_down,
):
    group = lax.axis_index("sub")
    pos = lax.axis_index("dp")
    core = pos & 1
    place = {"x": group, "y": pos >> 3, "z": (pos >> 1) & 3}
    sign = 1 - 2 * core
    upb = jnp.stack([enc_up_bias, dec_up_bias])
    table = jnp.concatenate([configs.reshape(16), src_lengths.reshape(2), tgt_lengths.reshape(2)])
    x, prev, y = enc_in.reshape(T, D), prev_enc.reshape(T, D), dec_in.reshape(T, D)
    e_cot, d_cot = enc_cotan.reshape(T, D), dec_cotan.reshape(T, D)
    act, act3, prob = arr(T, D), arr(T, 3 * D), arr(2 * H, LEN, LEN)
    act_out = hbm(T, D)
    vmem = pltpu.VMEM
    e_vec = jnp.concatenate([enc_gains.T, enc_shifts.T, enc_biases.T], 0)
    d_vec = jnp.concatenate([dec_gains.T, dec_shifts.T, dec_biases.T], 0)
    head = [SMEM, VMEM]

    encoded, e_qkv, e_p, e_mixed, e_mid, e_z = call(
        encoder_kernel, head + [VMEM] + [HBM] * 5,
        [act_out, hbm(T, 3 * D), hbm(2 * H, LEN, LEN), act_out, act_out, hbm(T, FF)], "encoder_forward", out_spec=[HBM] * 6, scratch=
        [vmem((D, 3 * D), bf16), vmem((D, D), bf16), vmem((D, FF), bf16), vmem((FF, D), bf16),
         vmem((2 * T, D), bf16), vmem((T, D), f32), vmem((T, D), f32),
         vmem((T, D), f32), vmem((T, 3 * D), f32), vmem((2 * H, LEN, LEN), f32), vmem((T, D), f32), vmem((T, D), f32),
         vmem((T, FF), f32), pltpu.SemaphoreType.DMA((5,)), pltpu.SemaphoreType.DMA((6,))], limit=30, flops=8 << 30, nbytes=24 << 20,
    )(table, e_vec, upb, *in_hbm(x, enc_triple, enc_output, enc_up, enc_down))

    (decoded, d_qkv, d_p, d_mixed, a1, mem, c_qkv, c_p, c_mixed, da2, f_keep, f_send, f_vec, f_upb) = call(
        decoder_kernel, head + [VMEM] * 5 + [HBM] * 8,
        [act_out, hbm(T, 3 * D), hbm(2 * H, LEN, LEN), act_out, act, act, act3, prob, act, act,
         hbm(T, D + FF), arr(T, D + FF), arr(8, D), arr(1, FF)], "decoder_forward",
        [vmem((D, 3 * D), bf16), vmem((D, D), bf16), vmem((D, D), bf16), vmem((D, 2 * D), bf16),
         vmem((D, D), bf16), vmem((D, FF), bf16), vmem((FF, D), bf16),
         vmem((2 * T, D), bf16), vmem((T, D), f32), vmem((T, FF), f32), vmem((T, D), f32),
         vmem((T, D), f32), vmem((T, 3 * D), f32), vmem((2 * H, LEN, LEN), f32), vmem((T, D), f32),
         vmem((T, D), f32), vmem((T, D + FF), f32),
         pltpu.SemaphoreType.DMA((8,)), pltpu.SemaphoreType.DMA((5,))], limit=36, out_spec=[HBM] * 4 + [VMEM] * 6 + [HBM] + [VMEM] * 3, flops=16 << 30, nbytes=48 << 20,
    )(table, d_vec, upb, y, prev, x, d_cot,
      *in_hbm(encoded, dec_triple, dec_output, dec_cross_query, dec_cross_pair, dec_cross_out, dec_up, dec_down))

    def ffn_grad(kept, got, rows, name, pinned=False):
        return pl.pallas_call(
            ffn_grad_kernel,
            in_specs=[VMEM, VMEM],
            out_shape=hbm(16, rows, 128) if pinned else arr(16, rows, 128),
            out_specs=ANY,
            scratch_shapes=[vmem((2, D, 2 * T), bf16), vmem((2, 16, WIDE // 128 * 40, 128), f32),
                            vmem((2, WIDE // 192, ROWS_FFN, 128), f32), pltpu.SemaphoreType.DMA((2,))],
            name=name,
            compiler_params=pltpu.CompilerParams(vmem_limit_bytes=26 << 20),
            cost_estimate=pl.CostEstimate(flops=6 << 30, bytes_accessed=16 << 20, transcendentals=0),
        )(kept, got)

    def att_grad(with_ffn, whole, operands, name, pinned=False):
        n = len(with_ffn)
        return pl.pallas_call(
            functools.partial(att_grad_kernel, with_ffn),
            in_specs=[SMEM, ANY] + [VMEM] * len(operands),
            out_shape=pltpu.HBM(whole.shape, f32) if pinned else arr(*whole.shape),
            out_specs=ANY,
            scratch_shapes=[vmem((16, ROWS_ATT * n, 128), f32), pltpu.SemaphoreType.DMA((n,))],
            input_output_aliases={1: 0},
            name=name,
            compiler_params=pltpu.CompilerParams(vmem_limit_bytes=24 << 20),
            cost_estimate=pl.CostEstimate(flops=3 << 30, bytes_accessed=10 << 20, transcendentals=0),
        )(table, whole, *operands)

    pair = arr(T, 4 * D)
    f_recv = move(f_send, SWAP)
    da1, dmem, dprev, c_keep, c_send, c_vec = call(
        cross_back_kernel, head + [VMEM] * 9, [act, act, act_out, pair, pair, arr(8, D)], "cross_backward", [vmem((2 * H, LEN, LEN), f32)], limit=14, flops=3 << 30, nbytes=16 << 20,
    )(table, d_vec, da2, a1, mem, c_qkv, c_p, c_mixed, dec_cross_query, dec_cross_pair, dec_cross_out)
    c_recv = move(c_send, SWAP)
    dy_in, s_keep, s_send, s_vec = call(
        functools.partial(self_back_kernel, 0, 3, False), head + [VMEM] * 8,
        [act_out, pair, pair, arr(8, D)], "self_backward", [vmem((2 * H, LEN, LEN), f32)], limit=14, flops=3 << 30, nbytes=16 << 20,
    )(table, d_vec, da1, y, d_qkv, d_p, d_mixed, dmem, dec_triple, dec_output)
    f_recv, s_send, s_keep, c_recv, dmem = barrier(f_recv, s_send, s_keep, c_recv, dmem)
    s_recv = move(s_send, SWAP)
    g_d = ffn_grad(f_keep, f_recv, ROWS_FFN + 2 * ROWS_ATT, "decoder_ffn_grad", True)
    g_d, s_recv = barrier(g_d, s_recv)
    g_d = att_grad((True, False), g_d, (c_keep, c_recv, c_vec, f_vec, f_upb, s_keep, s_recv, s_vec),
                   "decoder_attention_grad", True)
    cores = [[2 * i + c for i in range(16)] for c in range(2)]
    g_d, dmem = barrier(g_d, dmem)
    r_d = lax.psum_scatter(g_d, "dp", scatter_dimension=0, axis_index_groups=cores, tiled=True)

    dmid, h_keep, h_send, h_vec, h_upb = call(
        encoder_ffn_back_kernel, head + [HBM] * 6,
        [act, arr(T, D + FF), arr(T, D + FF), arr(8, D), arr(1, FF)], "encoder_ffn_backward",
        [vmem((D, FF), bf16), vmem((FF, D), bf16), vmem((2 * T, D), bf16), vmem((T, D), f32),
         vmem((T, D), f32), vmem((T, D), f32), vmem((T, D), f32), vmem((T, FF), f32),
         pltpu.SemaphoreType.DMA((3, FF // TILE)), pltpu.SemaphoreType.DMA((3,))], limit=24, flops=4 << 30, nbytes=24 << 20,
    )(table, e_vec, *in_hbm(e_cot, dmem, e_mid, e_z, enc_up, enc_down))
    h_recv = move(h_send, SWAP)
    dx_in, e_keep, e_send, e_vec_sum = call(
        functools.partial(self_back_kernel, 0, 2, True), head + [VMEM] * 8,
        [act_out, pair, pair, arr(8, D)], "encoder_attention_backward", [vmem((2 * H, LEN, LEN), f32)], limit=14, flops=3 << 30, nbytes=16 << 20,
    )(table, e_vec, dmid, x, e_qkv, e_p, e_mixed, dmem, enc_triple, enc_output)
    h_recv, e_send, e_keep = barrier(h_recv, e_send, e_keep)
    e_recv = move(e_send, SWAP)
    g_e = ffn_grad(h_keep, h_recv, ROWS_FFN + ROWS_ATT, "encoder_ffn_grad")
    g_e, e_recv = barrier(g_e, e_recv)
    g_e = att_grad((True,), g_e, (e_keep, e_recv, e_vec_sum, h_vec, h_upb), "encoder_attention_grad")

    g_e = g_e.reshape(4, 4, 4, 344, 128)
    enc_parts = [Part(g_e, rows, order, "yzx")
                 for rows, order in (((0, 184), "xyz"), ((184, 264), "yzx"), ((264, 344), "zxy"))]
    def settle(parts, sent, *others):
        keys = list(sent)
        arrived, others = barrier([sent[k] for k in keys], others)
        land(parts, dict(zip(keys, arrived)))
        return others

    def gather(parts):
        own = jnp.concatenate([p.array for p in parts], 0) if len(parts) > 1 else parts[0].array
        return [own] + [move(own, HOP_X[k]) for k in (1, 2, 3)]

    dec_parts, pieces = [], []
    for step in range(7):
        if step == 3:
            dec_parts = [Part(r_d.reshape(4, 448, 128), (0, 448), "x", "x")]
        active = [p for p in enc_parts + dec_parts if p.order]
        sent = advance(active, "step_%d" % step)
        if step == 2:
            (r_d,) = settle(active, sent, r_d)
        elif step == 5:
            pieces = settle(active, sent, *gather(dec_parts))
        elif step < 6:
            settle(active, sent)

    mine_d = jnp.stack(pieces, 0)
    other_d = move(mine_d, SWAP)
    pieces = gather(enc_parts)
    pieces, other_d = barrier(pieces, other_d)
    mine_e = jnp.stack(pieces, 0)
    other_e = move(mine_e, SWAP)

    enc_shapes = ((2, 20), (2, 20), (20, 3 * D), (20, D), (4, 20), (20, FF), (1, 96), (96, D))
    dec_shapes = ((3, 20), (3, 20), (20, 3 * D), (20, D), (20, D), (20, 2 * D), (20, D), (7, 20), (20, FF),
                  (1, 96), (96, D))
    grads = call(
        finish_kernel, [SMEM] + [VMEM] * 4, [arr(*t) for t in enc_shapes + dec_shapes], "finish",
        [vmem((2, 3168, 128), f32)], limit=24,
    )(table, mine_d, other_d, mine_e, other_e)
    grads = tuple(t.reshape(96) if t.shape == (1, 96) else t.T if t.shape[1] == 20 else t for t in grads)
    whole = (1, SENT, LEN, D)
    return (
        (encoded.reshape(whole), decoded.reshape(whole), dx_in.reshape(whole), dprev.reshape(whole),
         dy_in.reshape(whole)) + grads
    )


def solution(mesh):
    acts = P("sub", "dp", None, None)
    counts = P("sub", "dp")
    row, vector = P("dp", None), P("dp")
    in_specs = (acts,) * 5 + (counts,) * 2 + (P(),) * 20
    out_specs = (acts,) * 5 + (row,) * 6 + (vector, row) + (row,) * 9 + (vector, row)
    return jax.shard_map(per_device, mesh=mesh, in_specs=in_specs, out_specs=out_specs, check_vma=False)
```

```python
import functools
import math

import jax
import jax.numpy as jnp
from jax import lax
from jax.experimental import pallas as pl
from jax.experimental.pallas import tpu as pltpu
from jax.sharding import PartitionSpec as P

D = 640
H = 8
FF = 3072
LEN = 128
HD = 80
SENT = 2
T = SENT * LEN
TILE = 1024
ROWS_FFN = 960
ROWS_ATT = 416
f32 = jnp.float32
bf16 = jnp.bfloat16
NN = (((1,), (0,)), ((), ()))
NT = (((1,), (1,)), ((), ()))
TN = (((0,), (0,)), ((), ()))
MESH_AXES = ("sub", "dp")


def split(x):
    hi = x.astype(bf16)
    lo = (x - hi.astype(f32)).astype(bf16)
    return hi, lo


def stacked(x):
    return jnp.concatenate(split(x), 0)


def halves(r):
    n = r.shape[0] // 2
    return r[:n] + r[n:]


def mm(xs, w, dims=NN):
    return halves(lax.dot_general(xs, w, dims, preferred_element_type=f32))


def dot3(a, b, dims):
    ah, al = a
    bh, bl = b
    dg = functools.partial(lax.dot_general, dimension_numbers=dims, preferred_element_type=f32)
    if dims == NN:
        return dg(jnp.concatenate([al, ah, ah], 1), jnp.concatenate([bh, bl, bh], 0))
    return dg(al, bh) + dg(ah, bl) + dg(ah, bh)


def lane_mask(width, limit):
    return (lax.broadcasted_iota(jnp.int32, (1, width), 1) < limit).astype(f32)


def row_ok(len0, len1):
    row = lax.broadcasted_iota(jnp.int32, (T, 1), 0)
    limit = jnp.where(row < LEN, len0, LEN + len1)
    return (row < limit).astype(f32)


def norm(x, keep, width):
    mean = jnp.sum(x * keep, -1, keepdims=True) / width
    centred = (x - mean) * keep
    var = jnp.sum(centred * centred, -1, keepdims=True) / width
    rstd = lax.rsqrt(var + 1e-5)
    return centred * rstd, rstd


def norm_back(dy, n, rstd, gain, keep, width):
    dy = dy * keep
    dz = dy * gain
    m1 = jnp.sum(dz, -1, keepdims=True) / width
    m2 = jnp.sum(dz * n, -1, keepdims=True) / width
    dx = keep * rstd * (dz - m1 - n * m2)
    return dx, jnp.sum(dy * n, 0, keepdims=True), jnp.sum(dy, 0, keepdims=True)


def bell(z):
    cdf = 0.5 * (1.0 + lax.erf(z * (1.0 / math.sqrt(2.0))))
    pdf = jnp.exp(-0.5 * z * z) * (1.0 / math.sqrt(2.0 * math.pi))
    return cdf, pdf


def rows_of(pair, s, repeat):
    return jnp.concatenate([pair[i][s * LEN:(s + 1) * LEN] for i in repeat], 0)


def head(x, h):
    return x[:, h * HD:(h + 1) * HD]


def corners(r):
    return (r[LEN:, LEN:] + r[LEN:, :LEN]) + (r[:LEN, LEN:] + r[:LEN, :LEN])


def three(x):
    hi, lo = split(x)
    return jnp.concatenate([hi, lo, hi], 1)


def beside(pair, s, h):
    hi, lo = (head(x[s * LEN:(s + 1) * LEN], h) for x in pair)
    return jnp.concatenate([hi, jnp.zeros((LEN, LEN - HD), bf16), lo], 1)


def times(x, right):
    r = dot(stacked(x), right, NN)
    return (r[LEN:, :HD] + r[:LEN, LEN:]) + r[:LEN, :HD]


def dot(a, b, dims):
    return lax.dot_general(a, b, dims, preferred_element_type=f32)


def attend(q, k, v, lens, causal, p_ref):
    qs, ks, vs = split(q * (1.0 / math.sqrt(HD))), split(k), split(v)
    col = lax.broadcasted_iota(jnp.int32, (LEN, LEN), 1)
    for s in range(SENT):
        allowed = col < lens[s]
        if causal:
            allowed = allowed & (lax.broadcasted_iota(jnp.int32, (LEN, LEN), 0) >= col)
        q2, k2 = rows_of(qs, s, (0, 1)), rows_of(ks, s, (0, 1))
        for h in range(H):
            p_ref[s * H + h] = jnp.where(allowed, corners(dot(head(q2, h), head(k2, h), NT)), -1e30)
    for i in range(SENT * H):
        scores = p_ref[i]
        e = jnp.exp(scores - jnp.max(scores, -1, keepdims=True))
        p_ref[i] = e * (1.0 / jnp.sum(e, -1, keepdims=True))
    rows = []
    for s in range(SENT):
        v3 = rows_of(vs, s, (0, 0, 1))
        rows.append(jnp.concatenate([dot(three(p_ref[s * H + h]), head(v3, h), NN) for h in range(H)], 1))
    return jnp.concatenate(rows, 0)


def attend_back(do, q, k, v, p_ref, ds_ref):
    scale = 1.0 / math.sqrt(HD)
    dos, qs, ks, vs = split(do), split(q * scale), split(k * scale), split(v)
    for s in range(SENT):
        do2, v2 = rows_of(dos, s, (0, 1)), rows_of(vs, s, (0, 1))
        for h in range(H):
            ds_ref[s * H + h] = corners(dot(head(do2, h), head(v2, h), NT))
    for i in range(SENT * H):
        prob, dp = p_ref[i], ds_ref[i]
        ds_ref[i] = prob * (dp - jnp.sum(dp * prob, -1, keepdims=True))
    all_q, all_k, all_v = [], [], []
    for s in range(SENT):
        ids = [(s * H + h, h) for h in range(H)]
        all_q.append(jnp.concatenate([times(ds_ref[i], beside(ks, s, h)) for i, h in ids], 1))
        all_k.append(jnp.concatenate([times(ds_ref[i].T, beside(qs, s, h)) for i, h in ids], 1))
        all_v.append(jnp.concatenate([times(p_ref[i].T, beside(dos, s, h)) for i, h in ids], 1))
    return tuple(jnp.concatenate(x, 0) for x in (all_q, all_k, all_v))


def ffn_forward(ns, up, bias, down, ffn_limit, z_ref, acc_ref):
    acc_ref[...] = jnp.zeros_like(acc_ref)

    def body(j, _):
        sl = pl.ds(pl.multiple_of(j * TILE, TILE), TILE)
        z = mm(ns[...], up[:, sl]) + bias[:, sl].astype(f32)
        z_ref[:, sl] = z
        mask = (lax.broadcasted_iota(jnp.int32, (1, TILE), 1) + j * TILE < ffn_limit).astype(f32)
        u = z * bell(z)[0] * mask
        acc_ref[...] += mm(stacked(u), down[sl, :])
        return 0

    lax.fori_loop(0, FF // TILE, body, 0)


def ffn_backward(dyk, n, z_ref, up, down, ffn_limit, core, dys_ref, keep_ref, send_ref, bias_ref, acc_ref,
                 arrive=None):
    acc_ref[...] = jnp.zeros_like(acc_ref)
    dys_ref[...] = stacked(dyk)
    first = core == 0
    keep_ref[:, :D] = jnp.where(first, n, dyk)
    send_ref[:, :D] = jnp.where(first, dyk, n)

    def body(j, _):
        sl = pl.ds(pl.multiple_of(j * TILE, TILE), TILE)
        out = pl.ds(pl.multiple_of(j * TILE + D, 128), TILE)
        if arrive is not None:
            arrive(sl, j)
        du = mm(dys_ref[...], down[sl, :], NT)
        z = z_ref[:, sl]
        cdf, pdf = bell(z)
        mask = (lax.broadcasted_iota(jnp.int32, (1, TILE), 1) + j * TILE < ffn_limit).astype(f32)
        u = z * cdf * mask
        dz = du * mask * (cdf + z * pdf)
        keep_ref[:, out] = jnp.where(first, dz, u)
        send_ref[:, out] = jnp.where(first, u, dz)
        bias_ref[:, sl] = jnp.sum(dz, 0, keepdims=True)
        acc_ref[...] += mm(stacked(dz), up[:, sl], NT)
        return 0

    lax.fori_loop(0, FF // TILE, body, 0)


def load_vectors(ref):
    return ref[...].astype(f32)


def setting(table):
    g = lax.axis_index("sub")
    core = lax.axis_index("dp") & 1
    c = table[4 * g + 3]
    bits = [(c & 1).astype(f32), ((c >> 1) & 1).astype(f32), ((c >> 2) & 1).astype(f32)]
    total = bits[0] + bits[1] + bits[2]
    sc = (table[4 * g], table[4 * g + 1] * HD, table[4 * g + 2], table[16], table[17], table[18], table[19], core)
    return sc, [b / total for b in bits]


def fetch(pairs, sems):
    copies = [pltpu.make_async_copy(a, b, sems.at[i]) for i, (a, b) in enumerate(pairs)]
    for c in copies:
        c.start()
    return copies


def encoder_kernel(table, vec_ref, upb, x_ref, w_triple, w_out, w_up, w_down,
                   o_encoded, o_qkv, o_p, o_mixed, o_middle, o_z,
                   b_triple, b_out, b_up, b_down, ns_ref, acc_ref, b_x,
                   encoded, qkv, p_ref, mixed, middle, z_ref, sems, out_sems):
    read_x, *copies = fetch([(x_ref, b_x), (w_triple, b_triple), (w_out, b_out), (w_up, b_up), (w_down, b_down)], sems)
    leaving = []

    def leave(src, dst):
        copy = pltpu.make_async_copy(src, dst, out_sems.at[len(leaving)])
        copy.start()
        leaving.append(copy)

    sc, pick = setting(table)
    width = sc[0].astype(f32)
    keep, heads = lane_mask(D, sc[0]), lane_mask(D, sc[1])
    vec = load_vectors(vec_ref)
    read_x.wait()
    x = b_x[...]
    n, _ = norm(x, keep, width)
    ns = stacked((n * vec[0:1] + vec[2:3]) * keep)
    copies[0].wait()
    qkv[:, :D] = (mm(ns, b_triple[:, :D]) + vec[4:5]) * heads
    qkv[:, D:2 * D] = mm(ns, b_triple[:, D:2 * D]) * heads
    qkv[:, 2 * D:] = (mm(ns, b_triple[:, 2 * D:]) + vec[5:6]) * heads
    leave(qkv, o_qkv)
    o = attend(qkv[:, :D], qkv[:, D:2 * D], qkv[:, 2 * D:], (sc[3], sc[4]), False, p_ref)
    mixed[...] = o
    leave(p_ref, o_p)
    leave(mixed, o_mixed)
    copies[1].wait()
    mid = x + (mm(stacked(o), b_out[...]) + vec[6:7]) * keep
    middle[...] = mid
    leave(middle, o_middle)
    n, _ = norm(mid, keep, width)
    ns_ref[...] = stacked((n * vec[1:2] + vec[3:4]) * keep)
    copies[2].wait()
    copies[3].wait()
    ffn_forward(ns_ref, b_up, upb, b_down, sc[2], z_ref, acc_ref)
    leave(z_ref, o_z)
    encoded[...] = (middle[...] + (acc_ref[...] + vec[7:8]) * keep) * row_ok(sc[3], sc[4])
    leave(encoded, o_encoded)
    for copy in leaving:
        copy.wait()


def decoder_kernel(table, vec_ref, upb, x_ref, prev_ref, src_ref, cot_ref, enc_in,
                   w_triple, w_out, w_query, w_pair, w_cross, w_up, w_down,
                   o_decoded, o_qkv, o_p, o_mixed, a1_ref, mem_ref, qkv_c, p_cross, mixed_c, da2_ref,
                   o_keep, send_buf, dvec, dupb,
                   b_triple, b_out, b_query, b_pair, b_cross, b_up, b_down, ns_ref, acc_ref, z_ref, enc_ref,
                   decoded, qkv, p_self, mixed, a2_ref, keep_buf, sems, out_sems):
    copies = fetch([(w_triple, b_triple), (w_out, b_out), (w_query, b_query), (w_pair, b_pair),
                    (w_cross, b_cross), (w_up, b_up), (w_down, b_down), (enc_in, enc_ref)], sems)
    leaving = []

    def leave(src, dst):
        copy = pltpu.make_async_copy(src, dst, out_sems.at[len(leaving)])
        copy.start()
        leaving.append(copy)

    sc, pick = setting(table)
    width = sc[0].astype(f32)
    keep, heads = lane_mask(D, sc[0]), lane_mask(D, sc[1])
    vec = load_vectors(vec_ref)
    x = x_ref[...]
    n, _ = norm(x, keep, width)
    ns = stacked((n * vec[0:1] + vec[3:4]) * keep)
    copies[0].wait()
    qkv[:, :D] = (mm(ns, b_triple[:, :D]) + vec[6:7]) * heads
    qkv[:, D:2 * D] = mm(ns, b_triple[:, D:2 * D]) * heads
    qkv[:, 2 * D:] = (mm(ns, b_triple[:, 2 * D:]) + vec[7:8]) * heads
    o = attend(qkv[:, :D], qkv[:, D:2 * D], qkv[:, 2 * D:], (sc[5], sc[6]), True, p_self)
    mixed[...] = o
    leave(qkv, o_qkv)
    leave(p_self, o_p)
    leave(mixed, o_mixed)
    copies[1].wait()
    a1 = x + (mm(stacked(o), b_out[...]) + vec[8:9]) * keep
    a1_ref[...] = a1
    n, _ = norm(a1, keep, width)
    ns = stacked((n * vec[1:2] + vec[4:5]) * keep)
    copies[2].wait()
    qkv_c[:, :D] = (mm(ns, b_query[...]) + vec[9:10]) * heads
    copies[7].wait()
    memory = (pick[0] * prev_ref[...] + pick[1] * src_ref[...] + pick[2] * enc_ref[...]) * keep
    mem_ref[...] = memory
    ns = stacked(memory)
    copies[3].wait()
    qkv_c[:, D:2 * D] = mm(ns, b_pair[:, :D]) * heads
    qkv_c[:, 2 * D:] = (mm(ns, b_pair[:, D:]) + vec[10:11]) * heads
    o = attend(qkv_c[:, :D], qkv_c[:, D:2 * D], qkv_c[:, 2 * D:], (sc[3], sc[4]), False, p_cross)
    mixed_c[...] = o
    copies[4].wait()
    a2_ref[...] = a1_ref[...] + (mm(stacked(o), b_cross[...]) + vec[11:12]) * keep
    n, _ = norm(a2_ref[...], keep, width)
    ns_ref[...] = stacked((n * vec[2:3] + vec[5:6]) * keep)
    copies[5].wait()
    copies[6].wait()
    ffn_forward(ns_ref, b_up, upb, b_down, sc[2], z_ref, acc_ref)
    ok = row_ok(sc[5], sc[6])
    decoded[...] = (a2_ref[...] + (acc_ref[...] + vec[12:13]) * keep) * ok
    leave(decoded, o_decoded)
    dy = cot_ref[...] * ok
    dyk = dy * keep
    n, rstd = norm(a2_ref[...], keep, width)
    ffn_backward(dyk, (n * vec[2:3] + vec[5:6]) * keep, z_ref, b_up, b_down, sc[2], sc[7], ns_ref,
                 keep_buf, send_buf, dupb, acc_ref)
    leave(keep_buf, o_keep)
    dx, dg, db = norm_back(acc_ref[...], n, rstd, vec[2:3], keep, width)
    da2_ref[...] = dy + dx
    dvec[...] = jnp.concatenate([dg, db, jnp.sum(dyk, 0, keepdims=True), jnp.zeros((5, D), f32)], 0)
    for copy in leaving:
        copy.wait()


def cross_back_kernel(table, vec_ref, da2_ref, a1_ref, mem_ref, qkv_c, p_cross, mixed_c,
                      w_query, w_pair, w_cross,
                      da1_ref, dmem_ref, dprev_ref, keep_buf, send_buf, dvec, ds_ref):
    sc, pick = setting(table)
    width = sc[0].astype(f32)
    keep, heads = lane_mask(D, sc[0]), lane_mask(D, sc[1])
    vec = load_vectors(vec_ref)
    first = sc[7] == 0
    da2 = da2_ref[...]
    dyk = da2 * keep
    do = mm(stacked(dyk), w_cross[...], NT)
    dq, dk, dv = attend_back(do, qkv_c[:, :D], qkv_c[:, D:2 * D], qkv_c[:, 2 * D:], p_cross, ds_ref)
    dq, dk, dv = dq * heads, dk * heads, dv * heads
    n, rstd = norm(a1_ref[...], keep, width)
    normed = (n * vec[1:2] + vec[4:5]) * keep
    for i, (a, b) in enumerate(((mem_ref[...], normed), (mem_ref[...], mixed_c[...]), (dk, dq), (dv, dyk))):
        keep_buf[:, i * D:(i + 1) * D] = jnp.where(first, a, b)
        send_buf[:, i * D:(i + 1) * D] = jnp.where(first, b, a)
    dn = mm(stacked(dq), w_query[...], NT)
    dx, dg, db = norm_back(dn, n, rstd, vec[1:2], keep, width)
    da1_ref[...] = da2 + dx
    dmem = (mm(stacked(dk), w_pair[:, :D], NT) + mm(stacked(dv), w_pair[:, D:], NT)) * keep
    dmem_ref[...] = dmem
    dprev_ref[...] = dmem * pick[0]
    dvec[...] = jnp.concatenate(
        [dg, db] + [jnp.sum(t, 0, keepdims=True) for t in (dq, dv, dyk)] + [jnp.zeros((3, D), f32)], 0)


def self_back_kernel(gain_row, shift_row, with_memory, table, vec_ref, dy_ref, x_ref, qkv, p_ref, mixed,
                     dmem_ref, w_triple, w_out, dx_ref, keep_buf, send_buf, dvec, ds_ref):
    sc, pick = setting(table)
    width = sc[0].astype(f32)
    keep, heads = lane_mask(D, sc[0]), lane_mask(D, sc[1])
    vec = load_vectors(vec_ref)
    gain, shift = vec[gain_row:gain_row + 1], vec[shift_row:shift_row + 1]
    first = sc[7] == 0
    dy = dy_ref[...]
    dyk = dy * keep
    do = mm(stacked(dyk), w_out[...], NT)
    dq, dk, dv = attend_back(do, qkv[:, :D], qkv[:, D:2 * D], qkv[:, 2 * D:], p_ref, ds_ref)
    dq, dk, dv = dq * heads, dk * heads, dv * heads
    n, rstd = norm(x_ref[...], keep, width)
    normed = (n * gain + shift) * keep
    for i, (a, b) in enumerate(((normed, normed), (normed, mixed[...]), (dq, dv), (dk, dyk))):
        keep_buf[:, i * D:(i + 1) * D] = jnp.where(first, a, b)
        send_buf[:, i * D:(i + 1) * D] = jnp.where(first, b, a)
    dn = mm(stacked(dq), w_triple[:, :D], NT) + mm(stacked(dk), w_triple[:, D:2 * D], NT)
    dn += mm(stacked(dv), w_triple[:, 2 * D:], NT)
    dx, dg, db = norm_back(dn, n, rstd, gain, keep, width)
    dx = dx + dy
    if with_memory:
        dx = dx + pick[1] * dmem_ref[...]
    dx_ref[...] = dx
    dvec[...] = jnp.concatenate(
        [dg, db] + [jnp.sum(t, 0, keepdims=True) for t in (dq, dv, dyk)] + [jnp.zeros((3, D), f32)], 0)


def encoder_ffn_back_kernel(table, vec_ref, h_cot, h_dmem, h_middle, h_z, w_up, w_down,
                            dmid_ref, keep_buf, send_buf, dvec, dupb,
                            b_up, b_down, ns_ref, acc_ref, cot_ref, dmem_ref, middle, z_ref, sems, first_sems):
    first = fetch([(h_cot, cot_ref), (h_dmem, dmem_ref), (h_middle, middle)], first_sems)

    def tile_copies(sl, j):
        return (pltpu.make_async_copy(h_z.at[:, sl], z_ref.at[:, sl], sems.at[2, j]),
                pltpu.make_async_copy(w_down.at[sl, :], b_down.at[sl, :], sems.at[0, j]),
                pltpu.make_async_copy(w_up.at[:, sl], b_up.at[:, sl], sems.at[1, j]))

    for j in range(FF // TILE):
        for copy in tile_copies(pl.ds(j * TILE, TILE), j):
            copy.start()

    def arrive(sl, j):
        for copy in tile_copies(sl, j):
            copy.wait()

    sc, pick = setting(table)
    width = sc[0].astype(f32)
    keep = lane_mask(D, sc[0])
    vec = load_vectors(vec_ref)
    for copy in first:
        copy.wait()
    dy = (cot_ref[...] + pick[2] * dmem_ref[...]) * row_ok(sc[3], sc[4])
    dyk = dy * keep
    n, rstd = norm(middle[...], keep, width)
    ffn_backward(dyk, (n * vec[1:2] + vec[3:4]) * keep, z_ref, b_up, b_down, sc[2], sc[7], ns_ref,
                 keep_buf, send_buf, dupb, acc_ref, arrive)
    dx, dg, db = norm_back(acc_ref[...], n, rstd, vec[1:2], keep, width)
    dmid_ref[...] = dy + dx
    dvec[...] = jnp.concatenate([dg, db, jnp.sum(dyk, 0, keepdims=True), jnp.zeros((5, D), f32)], 0)


WIDE = 768


def ffn_grad_kernel(kept, got, out, at_s, buf_up, buf_down, sems):
    first = (lax.axis_index("dp") & 1) == 0
    for i, ref in enumerate((kept, got)):
        hi, lo = split(ref[:, :D].T)
        at_s[0, :, i * T:(i + 1) * T] = hi
        at_s[1, :, i * T:(i + 1) * T] = lo
    n_up, n_down = WIDE // 128 * 40, WIDE // 192
    left = lax.broadcasted_iota(jnp.int32, (320, 128), 1) < 64

    def up_copy(j, slot):
        rows = pl.ds(pl.multiple_of(j * n_up, 8), n_up)
        return pltpu.make_async_copy(buf_up.at[slot], out.at[:, rows, :], sems.at[slot])

    def down_copy(j, slot):
        rows = pl.ds(0, ROWS_FFN)
        return pltpu.make_async_copy(buf_down.at[slot], out.at[pl.ds(j * n_down, n_down), rows, :], sems.at[slot])

    def body(j, _):
        slot = j & 1
        cols = pl.ds(pl.multiple_of(j * WIDE + D, 128), WIDE)
        r = dot3((at_s[0], at_s[1]), split(jnp.concatenate([kept[:, cols], got[:, cols]], 0)), NN)
        tiles = [r[:, c * 128:(c + 1) * 128] for c in range(WIDE // 128)]

        @pl.when(first)
        def _():
            @pl.when(j >= 2)
            def _():
                up_copy(j - 2, slot).wait()

            for c, t in enumerate(tiles):
                buf_up[slot, :, c * 40:(c + 1) * 40, :] = t.reshape(16, 40, 128)
            up_copy(j, slot).start()

        @pl.when(jnp.logical_not(first))
        def _():
            @pl.when(j >= 2)
            def _():
                down_copy(j - 2, slot).wait()

            for p in range(n_down // 2):
                a, shared, b = tiles[3 * p:3 * p + 3]
                upper, lower = shared[:320], shared[320:]
                buf_down[slot, 2 * p, :D, :] = a
                buf_down[slot, 2 * p, D:, :] = jnp.where(left, upper, pltpu.roll(lower, 64, 1))
                buf_down[slot, 2 * p + 1, :D, :] = b
                buf_down[slot, 2 * p + 1, D:, :] = jnp.where(left, pltpu.roll(upper, 64, 1), lower)
            down_copy(j, slot).start()

        return 0

    steps = FF // WIDE
    lax.fori_loop(0, steps, body, 0)

    @pl.when(first)
    def _():
        for j in (steps - 2, steps - 1):
            up_copy(j, j & 1).wait()

    @pl.when(jnp.logical_not(first))
    def _():
        for j in (steps - 2, steps - 1):
            down_copy(j, j & 1).wait()


def small_block(out, base, ffn_vec, att_vec, upb, counts, group):
    lane = lax.broadcasted_iota(jnp.int32, (1, 128), 1)
    totals = jnp.where(lane == group, counts[0], 0) + jnp.where(lane == group + 4, counts[1], 0)
    totals = totals.astype(f32)
    for b in range(16):
        out[b, base:base + 16, :] = jnp.zeros((16, 128), f32)
        if ffn_vec is not None:
            out[b, base:base + 3, :40] = ffn_vec[:3, b * 40:(b + 1) * 40]
        out[b, base + 3:base + 8, :40] = att_vec[:5, b * 40:(b + 1) * 40]
        if upb is not None:
            for c in range(2):
                out[b, base + 8 + c:base + 9 + c, :96] = upb[:, b * 192 + c * 96:b * 192 + (c + 1) * 96]
        out[b, base + 15:base + 16, :] = totals


def att_grad_kernel(with_ffn, *refs):
    table = refs[0]
    whole, out, sem = refs[-3:]
    refs = list(refs[2:-3])
    group = lax.axis_index("sub")
    counts = (table[16] + table[17], table[18] + table[19])
    copies = []
    for n, ffn in enumerate(with_ffn):
        kept, got, att_vec = refs[:3]
        ffn_vec, upb = (refs[3], refs[4]) if ffn else (None, None)
        refs = refs[5 if ffn else 3:]
        base = n * ROWS_ATT
        small_block(out, base + 400, ffn_vec, att_vec, upb, counts, group)
        for i in range(2):
            a = jnp.concatenate([kept[:, i * D:(i + 1) * D].T, got[:, i * D:(i + 1) * D].T], 1)
            b = jnp.concatenate([kept[:, (i + 2) * D:(i + 3) * D], got[:, (i + 2) * D:(i + 3) * D]], 0)
            a, b = split(a), split(b)
            r = dot3(a, b, NN)
            for c in range(5):
                row = base + i * 200 + c * 40
                out[:, row:row + 40, :] = r[:, c * 128:(c + 1) * 128].reshape(16, 40, 128)
        copy = pltpu.make_async_copy(
            out.at[:, pl.ds(base, ROWS_ATT), :], whole.at[:, pl.ds(ROWS_FFN + base, ROWS_ATT), :], sem.at[n])
        copy.start()
        copies.append(copy)
    for copy in copies:
        copy.wait()


def usage_scale(cfg, totals, row_kind, rows, col_kind, cols):
    limit = {"keep": lambda g: cfg[4 * g], "head": lambda g: cfg[4 * g + 1] * HD, "ffn": lambda g: cfg[4 * g + 2]}
    usage = 0.0
    for g in range(4):
        part = jnp.where(rows < limit[row_kind](g), totals[g], 0.0)
        if col_kind is not None:
            part = jnp.where(cols < limit[col_kind](g), part, 0.0)
        usage = usage + part
    return lax.rsqrt(usage)


def finish_kernel(is_dec, cfg, mine, other, *refs):
    whole = refs[-1]
    outs = refs[:-1]
    pos = lax.axis_index("dp")
    px = lax.axis_index("sub")
    core = pos & 1
    sign = 1 - 2 * core
    first = core == 0
    n = mine.shape[1]
    for k in range(4):
        for ref, owner, from_x in ((mine, core, (px - sign * k) & 3), (other, 1 - core, (px + sign * k) & 3)):
            whole[owner, pl.ds(pl.multiple_of(from_x * n, 8), n), :] = ref[k]

    def half(owner, row):
        return jnp.where(first, whole[owner, row:row + 20, :], whole[owner, row + 20:row + 40, :])

    def iota(shape, dim):
        return lax.broadcasted_iota(jnp.int32, shape, dim)

    cols = iota((1, D), 1)
    odd = ((pos >> 1) & 1) == 1
    rows20, rows96 = pos * 20 + iota((20, 1), 0), pos * 96 + iota((96, 1), 0)
    lanes20, lanes96 = pos * 20 + iota((1, 20), 1), pos * 96 + iota((1, 96), 1)

    def job(out, col, owner, base, i, factor):
        for c in range(5):
            out[:, col + c * 128:col + (c + 1) * 128] = (
                half(owner, base + i * 200 + c * 40) * factor[:, c * 128:(c + 1) * 128])

    def small(base):
        both = whole[0, base + 400:base + 416, :] + whole[1, base + 400:base + 416, :]
        return both, jnp.where(first, both[:, :20], both[:, 20:40])

    def put(out, items):
        for i, (vec, k, factor) in enumerate(items):
            out[i:i + 1, :] = vec[k:k + 1, :] * factor

    c_all, c_vec = small(ROWS_FFN)
    scale = functools.partial(
        usage_scale, cfg, [c_all[15:16, 4 * is_dec + g:4 * is_dec + g + 1] for g in range(4)])
    keep_head = scale("keep", rows20, "head", cols)
    head_keep = scale("head", rows20, "keep", cols)
    keep_row = scale("keep", lanes20, None, None)
    head_row = scale("head", lanes20, None, None)
    keep_ffn = scale("keep", rows20, "ffn", iota((1, FF), 1))
    ffn_keep = scale("ffn", rows96, "keep", cols)
    att, ffn, bias = ROWS_FFN, 0, c_all
    if is_dec:
        c, att = ROWS_FFN, ROWS_FFN + ROWS_ATT
        s_vec = small(att)[1]
        gains, shifts, triple, output, query, pair, cross, biases, up, up_bias, down = outs
        put(gains, ((s_vec, 3, keep_row), (c_vec, 3, keep_row), (c_vec, 0, keep_row)))
        put(shifts, ((s_vec, 4, keep_row), (c_vec, 4, keep_row), (c_vec, 1, keep_row)))
        put(biases, ((s_vec, 5, head_row), (s_vec, 6, head_row), (s_vec, 7, keep_row),
                     (c_vec, 5, head_row), (c_vec, 6, head_row), (c_vec, 7, keep_row), (c_vec, 2, keep_row)))
        job(query, 0, 1, c, 0, keep_head)
        job(pair, 0, 0, c, 0, keep_head)
        job(pair, D, 0, c, 1, keep_head)
        job(cross, 0, 1, c, 1, head_keep)
    else:
        gains, shifts, triple, output, biases, up, up_bias, down = outs
        put(gains, ((c_vec, 3, keep_row), (c_vec, 0, keep_row)))
        put(shifts, ((c_vec, 4, keep_row), (c_vec, 1, keep_row)))
        put(biases, ((c_vec, 5, head_row), (c_vec, 6, head_row), (c_vec, 7, keep_row), (c_vec, 2, keep_row)))
    job(triple, 0, 0, att, 0, keep_head)
    job(triple, D, 0, att, 1, keep_head)
    job(triple, 2 * D, 1, att, 0, keep_head)
    job(output, 0, 1, att, 1, head_keep)
    for t in range(24):
        up[:, t * 128:(t + 1) * 128] = half(0, ffn + t * 40) * keep_ffn[:, t * 128:(t + 1) * 128]
    tile = whole[1, ffn:ffn + D, :].T
    both = whole[1, ffn + D:ffn + ROWS_FFN, :].T
    rest = jnp.concatenate([both[:64], both[64:]], 1)
    units = jnp.where(odd, jnp.concatenate([rest, tile], 0), jnp.concatenate([tile, rest], 0))
    down[...] = jnp.where(first, units[:96], units[96:]) * ffn_keep
    bias_row = jnp.where(first, bias[8:9, :96], bias[9:10, :96])
    up_bias[...] = bias_row * scale("ffn", lanes96, None, None)


SMEM = pl.BlockSpec(memory_space=pltpu.SMEM)
VMEM = pl.BlockSpec(memory_space=pltpu.VMEM)
ANY = pl.BlockSpec(memory_space=pl.ANY)
HBM = pl.BlockSpec(memory_space=pltpu.HBM)


def arr(*shape):
    return jax.ShapeDtypeStruct(shape, f32)


def hbm(*shape):
    return pltpu.HBM(shape, f32)


def call(kernel, in_specs, outs, name, scratch=(), limit=56, flops=1 << 20, nbytes=1 << 20, out_spec=None):
    return pl.pallas_call(
        kernel,
        in_specs=in_specs,
        out_shape=outs,
        out_specs=out_spec or [VMEM] * len(outs),
        scratch_shapes=list(scratch),
        name=name,
        compiler_params=pltpu.CompilerParams(vmem_limit_bytes=limit << 20),
        cost_estimate=pl.CostEstimate(flops=flops, bytes_accessed=nbytes, transcendentals=0),
    )


def in_hbm(*arrays):
    return tuple(pltpu.with_memory_space_constraint(a, pltpu.HBM) for a in arrays)


def flat_perm(move):
    pairs = []
    for x in range(4):
        for y in range(4):
            for z in range(4):
                for c in range(2):
                    X, Y, Z, C = move(x, y, z, c)
                    pairs.append((x * 32 + y * 8 + z * 2 + c, (X % 4) * 32 + (Y % 4) * 8 + (Z % 4) * 2 + C % 2))
    return pairs


SWAP = flat_perm(lambda x, y, z, c: (x, y, z, 1 - c))
RING = {
    "x": flat_perm(lambda x, y, z, c: (x + 1 - 2 * c, y, z, c)),
    "y": flat_perm(lambda x, y, z, c: (x, y + 1 - 2 * c, z, c)),
    "z": flat_perm(lambda x, y, z, c: (x, y, z + 1 - 2 * c, c)),
}
HOP_X = [flat_perm(lambda x, y, z, c, k=k: (x + k - 2 * c * k, y, z, c)) for k in range(4)]


def turn(p, c):
    return p + (1 - 2 * c) * (1 - 2 * (p & 1))


PAIR = {
    "x": (flat_perm(lambda x, y, z, c: (turn(x, c), y, z, c)), flat_perm(lambda x, y, z, c: (x + 2, y, z, c))),
    "y": (flat_perm(lambda x, y, z, c: (x, turn(y, c), z, c)), flat_perm(lambda x, y, z, c: (x, y + 2, z, c))),
    "z": (flat_perm(lambda x, y, z, c: (x, y, turn(z, c), c)), flat_perm(lambda x, y, z, c: (x, y, z + 2, c))),
}


def move(x, perm):
    return lax.ppermute(x, MESH_AXES, perm)


def barrier(*trees):
    return lax.optimization_barrier(trees)


class Part:
    def __init__(self, array, rows, order, dims):
        self.array, self.rows, self.order, self.dims = array, rows, list(order), list(dims)
        self.step, self.got = 0, []

    @property
    def size(self):
        return self.rows[1] - self.rows[0]


def advance(parts, name):
    inputs = []

    def slot(array):
        for n, a in enumerate(inputs):
            if a is array:
                return n
        inputs.append(array)
        return len(inputs) - 1

    plans, routes, out_shapes = [], {}, []
    for part in parts:
        axis = part.order[0]
        d = part.dims.index(axis)
        plan = dict(src=slot(part.array), rows=part.rows, d=d, axis=axis, step=part.step, nd=len(part.dims),
                    got=[(slot(a), off) for a, off in part.got], m=part.size)
        if part.step == 2:
            plan["out"] = len(out_shapes)
            out_shapes.append((4,) * (len(part.dims) - 1) + (part.size, 128))
            if len(part.order) > 1:
                plan["next_axis"] = part.order[1]
                rest = [t for t in part.dims if t != axis]
                plan["next_d"] = rest.index(part.order[1])
        plans.append(plan)
        send_axis, kind = (axis, part.step) if part.step < 2 else (plan.get("next_axis"), 0)
        if send_axis is not None:
            nd = plan["nd"] if part.step < 2 else plan["nd"] - 1
            chunk_rows = 4 ** (nd - 1) * part.size
            route = routes.setdefault((send_axis, kind), [0, []])
            plan["route"], plan["offset"], plan["chunk"] = (send_axis, kind), route[0], chunk_rows
            route[0] += chunk_rows * (2 if kind == 0 else 1)
    n_state = len(out_shapes)
    route_list = list(routes)
    out_shapes += [(routes[r][0], 128) for r in route_list]
    n_in = len(inputs)

    def kernel(*refs):
        ins, outs = refs[:n_in], refs[n_in:]
        pos = lax.axis_index("dp")
        core = pos & 1
        place = {"x": lax.axis_index("sub"), "y": pos >> 3, "z": (pos >> 1) & 3}

        def chunk(ref, nd, d, k, rows):
            index = [slice(None)] * nd
            index[d] = k & 3
            return ref[tuple(index) + (slice(*rows), slice(None))].reshape(-1, 128)

        for plan in plans:
            src, nd, d, rows, m = ins[plan["src"]], plan["nd"], plan["d"], plan["rows"], plan["m"]
            p = place[plan["axis"]]
            n = 4 ** (nd - 1) * m
            got = [(ins[i], off) for i, off in plan["got"]]
            out = outs[n_state + route_list.index(plan["route"])] if "route" in plan else None
            off = plan.get("offset")
            if plan["step"] == 0:
                q = turn(p, core)
                out[off:off + n, :] = chunk(src, nd, d, q, rows)
                out[off + n:off + 2 * n, :] = chunk(src, nd, d, q + 2, rows)
            elif plan["step"] == 1:
                (a, a_off), = got
                out[off:off + n, :] = chunk(src, nd, d, p + 2, rows) + a[a_off + n:a_off + 2 * n, :]
            else:
                (a, a_off), (b, b_off) = got
                total = chunk(src, nd, d, p, rows) + a[a_off:a_off + n, :] + b[b_off:b_off + n, :]
                state = outs[plan["out"]]
                state[...] = total.reshape(state.shape)
                if out is not None:
                    nn = plan["chunk"]
                    q = turn(place[plan["next_axis"]], core)
                    out[off:off + nn, :] = chunk(state, nd - 1, plan["next_d"], q, (0, m))
                    out[off + nn:off + 2 * nn, :] = chunk(state, nd - 1, plan["next_d"], q + 2, (0, m))

    outs = call(kernel, [VMEM] * n_in, [arr(*t) for t in out_shapes], name, limit=24)(*inputs)
    sent = {r: move(outs[n_state + i], PAIR[r[0]][r[1]]) for i, r in enumerate(route_list)}
    for part, plan in zip(parts, plans):
        if part.step == 2:
            part.array, part.rows = outs[plan["out"]], (0, part.size)
            part.dims.remove(part.order.pop(0))
            part.step, part.got = 0, []
        if "route" in plan:
            part.got.append((plan["route"], plan["offset"]))
            part.step += 1
    return sent


def land(parts, sent):
    for part in parts:
        part.got = [(sent[a], off) if isinstance(a, tuple) else (a, off) for a, off in part.got]


def per_device(
    enc_in, prev_enc, dec_in, enc_cotan, dec_cotan, src_lengths, tgt_lengths, configs,
    enc_gains, enc_shifts, enc_triple, enc_output, enc_biases, enc_up, enc_up_bias, enc_down,
    dec_gains, dec_shifts, dec_triple, dec_output, dec_cross_query, dec_cross_pair, dec_cross_out,
    dec_biases, dec_up, dec_up_bias, dec_down,
):
    group = lax.axis_index("sub")
    pos = lax.axis_index("dp")
    core = pos & 1
    place = {"x": group, "y": pos >> 3, "z": (pos >> 1) & 3}
    sign = 1 - 2 * core
    e_upb, d_upb = enc_up_bias.reshape(1, FF), dec_up_bias.reshape(1, FF)
    table = jnp.concatenate([configs.reshape(16), src_lengths.reshape(2), tgt_lengths.reshape(2)])
    x, prev, y = enc_in.reshape(T, D), prev_enc.reshape(T, D), dec_in.reshape(T, D)
    e_cot, d_cot = enc_cotan.reshape(T, D), dec_cotan.reshape(T, D)
    act, act3, prob = arr(T, D), arr(T, 3 * D), arr(2 * H, LEN, LEN)
    act_out = hbm(T, D)
    vmem = pltpu.VMEM
    e_vec = jnp.concatenate([enc_gains.T, enc_shifts.T, enc_biases.T], 0)
    d_vec = jnp.concatenate([dec_gains.T, dec_shifts.T, dec_biases.T], 0)
    head = [SMEM, VMEM]

    encoded, e_qkv, e_p, e_mixed, e_mid, e_z = call(
        encoder_kernel, head + [VMEM] + [HBM] * 5,
        [act_out, hbm(T, 3 * D), hbm(2 * H, LEN, LEN), act_out, act_out, hbm(T, FF)], "encoder_forward", out_spec=[HBM] * 6, scratch=
        [vmem((D, 3 * D), bf16), vmem((D, D), bf16), vmem((D, FF), bf16), vmem((FF, D), bf16),
         vmem((2 * T, D), bf16), vmem((T, D), f32), vmem((T, D), f32),
         vmem((T, D), f32), vmem((T, 3 * D), f32), vmem((2 * H, LEN, LEN), f32), vmem((T, D), f32), vmem((T, D), f32),
         vmem((T, FF), f32), pltpu.SemaphoreType.DMA((5,)), pltpu.SemaphoreType.DMA((6,))], limit=30, flops=8 << 30, nbytes=24 << 20,
    )(table, e_vec, e_upb, *in_hbm(x, enc_triple, enc_output, enc_up, enc_down))

    (decoded, d_qkv, d_p, d_mixed, a1, mem, c_qkv, c_p, c_mixed, da2, f_keep, f_send, f_vec, f_upb) = call(
        decoder_kernel, head + [VMEM] * 5 + [HBM] * 8,
        [act_out, hbm(T, 3 * D), hbm(2 * H, LEN, LEN), act_out, act, act, act3, prob, act, act,
         hbm(T, D + FF), arr(T, D + FF), arr(8, D), arr(1, FF)], "decoder_forward",
        [vmem((D, 3 * D), bf16), vmem((D, D), bf16), vmem((D, D), bf16), vmem((D, 2 * D), bf16),
         vmem((D, D), bf16), vmem((D, FF), bf16), vmem((FF, D), bf16),
         vmem((2 * T, D), bf16), vmem((T, D), f32), vmem((T, FF), f32), vmem((T, D), f32),
         vmem((T, D), f32), vmem((T, 3 * D), f32), vmem((2 * H, LEN, LEN), f32), vmem((T, D), f32),
         vmem((T, D), f32), vmem((T, D + FF), f32),
         pltpu.SemaphoreType.DMA((8,)), pltpu.SemaphoreType.DMA((5,))], limit=36, out_spec=[HBM] * 4 + [VMEM] * 6 + [HBM] + [VMEM] * 3, flops=16 << 30, nbytes=48 << 20,
    )(table, d_vec, d_upb, y, prev, x, d_cot,
      *in_hbm(encoded, dec_triple, dec_output, dec_cross_query, dec_cross_pair, dec_cross_out, dec_up, dec_down))

    def ffn_grad(kept, got, rows, name, pinned=False):
        return pl.pallas_call(
            ffn_grad_kernel,
            in_specs=[VMEM, VMEM],
            out_shape=hbm(16, rows, 128) if pinned else arr(16, rows, 128),
            out_specs=ANY,
            scratch_shapes=[vmem((2, D, 2 * T), bf16), vmem((2, 16, WIDE // 128 * 40, 128), f32),
                            vmem((2, WIDE // 192, ROWS_FFN, 128), f32), pltpu.SemaphoreType.DMA((2,))],
            name=name,
            compiler_params=pltpu.CompilerParams(vmem_limit_bytes=26 << 20),
            cost_estimate=pl.CostEstimate(flops=6 << 30, bytes_accessed=16 << 20, transcendentals=0),
        )(kept, got)

    def att_grad(with_ffn, whole, operands, name, pinned=False):
        n = len(with_ffn)
        return pl.pallas_call(
            functools.partial(att_grad_kernel, with_ffn),
            in_specs=[SMEM, ANY] + [VMEM] * len(operands),
            out_shape=pltpu.HBM(whole.shape, f32) if pinned else arr(*whole.shape),
            out_specs=ANY,
            scratch_shapes=[vmem((16, ROWS_ATT * n, 128), f32), pltpu.SemaphoreType.DMA((n,))],
            input_output_aliases={1: 0},
            name=name,
            compiler_params=pltpu.CompilerParams(vmem_limit_bytes=24 << 20),
            cost_estimate=pl.CostEstimate(flops=3 << 30, bytes_accessed=10 << 20, transcendentals=0),
        )(table, whole, *operands)

    pair = arr(T, 4 * D)
    f_recv = move(f_send, SWAP)
    da1, dmem, dprev, c_keep, c_send, c_vec = call(
        cross_back_kernel, head + [VMEM] * 9, [act, act, act_out, pair, pair, arr(8, D)], "cross_backward", [vmem((2 * H, LEN, LEN), f32)], limit=14, flops=3 << 30, nbytes=16 << 20,
    )(table, d_vec, da2, a1, mem, c_qkv, c_p, c_mixed, dec_cross_query, dec_cross_pair, dec_cross_out)
    c_recv = move(c_send, SWAP)
    dy_in, s_keep, s_send, s_vec = call(
        functools.partial(self_back_kernel, 0, 3, False), head + [VMEM] * 8,
        [act_out, pair, pair, arr(8, D)], "self_backward", [vmem((2 * H, LEN, LEN), f32)], limit=14, flops=3 << 30, nbytes=16 << 20,
    )(table, d_vec, da1, y, d_qkv, d_p, d_mixed, dmem, dec_triple, dec_output)
    f_recv, s_send, s_keep, c_recv, dmem = barrier(f_recv, s_send, s_keep, c_recv, dmem)
    s_recv = move(s_send, SWAP)
    g_d = ffn_grad(f_keep, f_recv, ROWS_FFN + 2 * ROWS_ATT, "decoder_ffn_grad", True)
    g_d, s_recv = barrier(g_d, s_recv)
    g_d = att_grad((True, False), g_d, (c_keep, c_recv, c_vec, f_vec, f_upb, s_keep, s_recv, s_vec),
                   "decoder_attention_grad", True)
    cores = [[2 * i + c for i in range(16)] for c in range(2)]
    g_d, dmem = barrier(g_d, dmem)
    r_d = lax.psum_scatter(g_d, "dp", scatter_dimension=0, axis_index_groups=cores, tiled=True)

    dmid, h_keep, h_send, h_vec, h_upb = call(
        encoder_ffn_back_kernel, head + [HBM] * 6,
        [act, arr(T, D + FF), arr(T, D + FF), arr(8, D), arr(1, FF)], "encoder_ffn_backward",
        [vmem((D, FF), bf16), vmem((FF, D), bf16), vmem((2 * T, D), bf16), vmem((T, D), f32),
         vmem((T, D), f32), vmem((T, D), f32), vmem((T, D), f32), vmem((T, FF), f32),
         pltpu.SemaphoreType.DMA((3, FF // TILE)), pltpu.SemaphoreType.DMA((3,))], limit=24, flops=4 << 30, nbytes=24 << 20,
    )(table, e_vec, *in_hbm(e_cot, dmem, e_mid, e_z, enc_up, enc_down))
    h_recv = move(h_send, SWAP)
    dx_in, e_keep, e_send, e_vec_sum = call(
        functools.partial(self_back_kernel, 0, 2, True), head + [VMEM] * 8,
        [act_out, pair, pair, arr(8, D)], "encoder_attention_backward", [vmem((2 * H, LEN, LEN), f32)], limit=14, flops=3 << 30, nbytes=16 << 20,
    )(table, e_vec, dmid, x, e_qkv, e_p, e_mixed, dmem, enc_triple, enc_output)
    h_recv, e_send, e_keep = barrier(h_recv, e_send, e_keep)
    e_recv = move(e_send, SWAP)
    g_e = ffn_grad(h_keep, h_recv, ROWS_FFN + ROWS_ATT, "encoder_ffn_grad")
    g_e, e_recv = barrier(g_e, e_recv)
    g_e = att_grad((True,), g_e, (e_keep, e_recv, e_vec_sum, h_vec, h_upb), "encoder_attention_grad")

    g_e = g_e.reshape(4, 4, 4, 344, 128)
    enc_parts = [Part(g_e, rows, order, "yzx")
                 for rows, order in (((0, 184), "xyz"), ((184, 264), "yxz"), ((264, 344), "zxy"))]
    def settle(parts, sent, *others):
        keys = list(sent)
        arrived, others = barrier([sent[k] for k in keys], others)
        land(parts, dict(zip(keys, arrived)))
        return others

    def gather(parts):
        own = jnp.concatenate([p.array for p in parts], 0) if len(parts) > 1 else parts[0].array
        return [own] + [move(own, HOP_X[k]) for k in (1, 2, 3)]

    dec_parts, flying, pieces = [], {}, []
    for step in range(7):
        active = enc_parts + (dec_parts if step in (4, 5) else [])
        sent = advance([p for p in active if p.order], "step_%d" % step)
        if step == 2:
            dec_parts = [Part(r_d.reshape(4, 448, 128), (0, 448), "x", "x")]
            flying = advance(dec_parts, "decoder_step")
        if step == 3:
            settle(enc_parts + dec_parts, {**sent, **flying})
        elif step == 5:
            pieces = settle(enc_parts, sent, *gather(dec_parts))
        elif step < 6:
            settle(active, sent)

    def finish(is_dec, mine, other, shapes, name):
        outs = call(
            functools.partial(finish_kernel, is_dec), [SMEM] + [VMEM] * 2, [arr(*t) for t in shapes], name,
            [vmem((2, 4 * mine.shape[1], 128), f32)], limit=24,
        )(table, mine, other)
        return tuple(t.reshape(96) if t.shape == (1, 96) else t.T if t.shape[1] == 20 else t for t in outs)

    mine_d = jnp.stack(pieces, 0)
    other_d = move(mine_d, SWAP)
    pieces = gather(enc_parts)
    dec_grads = finish(True, mine_d, other_d, (
        (3, 20), (3, 20), (20, 3 * D), (20, D), (20, D), (20, 2 * D), (20, D), (7, 20), (20, FF), (1, 96), (96, D)),
        "decoder_finish")
    pieces, dec_grads = barrier(pieces, dec_grads)
    mine_e = jnp.stack(pieces, 0)
    other_e = move(mine_e, SWAP)
    grads = finish(False, mine_e, other_e, (
        (2, 20), (2, 20), (20, 3 * D), (20, D), (4, 20), (20, FF), (1, 96), (96, D)), "encoder_finish") + dec_grads
    whole = (1, SENT, LEN, D)
    return (
        (encoded.reshape(whole), decoded.reshape(whole), dx_in.reshape(whole), dprev.reshape(whole),
         dy_in.reshape(whole)) + grads
    )


def solution(mesh):
    acts = P("sub", "dp", None, None)
    counts = P("sub", "dp")
    row, vector = P("dp", None), P("dp")
    in_specs = (acts,) * 5 + (counts,) * 2 + (P(),) * 20
    out_specs = (acts,) * 5 + (row,) * 6 + (vector, row) + (row,) * 9 + (vector, row)
    return jax.shard_map(per_device, mesh=mesh, in_specs=in_specs, out_specs=out_specs, check_vma=False)
```

```python
import functools
import math

import jax
import jax.numpy as jnp
from jax import lax
from jax.experimental import pallas as pl
from jax.experimental.pallas import tpu as pltpu
from jax.sharding import PartitionSpec as P

D = 640
H = 8
FF = 3072
LEN = 128
HD = 80
SENT = 2
T = SENT * LEN
TILE = 1024
ROWS_FFN = 960
ROWS_ATT = 416
f32 = jnp.float32
bf16 = jnp.bfloat16
NN = (((1,), (0,)), ((), ()))
NT = (((1,), (1,)), ((), ()))
TN = (((0,), (0,)), ((), ()))
MESH_AXES = ("sub", "dp")


def split(x):
    hi = x.astype(bf16)
    lo = (x - hi.astype(f32)).astype(bf16)
    return hi, lo


def stacked(x):
    return jnp.concatenate(split(x), 0)


def halves(r):
    n = r.shape[0] // 2
    return r[:n] + r[n:]


def mm(xs, w, dims=NN):
    return halves(lax.dot_general(xs, w, dims, preferred_element_type=f32))


def dot3(a, b, dims):
    ah, al = a
    bh, bl = b
    dg = functools.partial(lax.dot_general, dimension_numbers=dims, preferred_element_type=f32)
    if dims == NN:
        return dg(jnp.concatenate([al, ah, ah], 1), jnp.concatenate([bh, bl, bh], 0))
    return dg(al, bh) + dg(ah, bl) + dg(ah, bh)


def lane_mask(width, limit):
    return (lax.broadcasted_iota(jnp.int32, (1, width), 1) < limit).astype(f32)


def row_ok(len0, len1):
    row = lax.broadcasted_iota(jnp.int32, (T, 1), 0)
    limit = jnp.where(row < LEN, len0, LEN + len1)
    return (row < limit).astype(f32)


def norm(x, keep, width):
    mean = jnp.sum(x * keep, -1, keepdims=True) / width
    centred = (x - mean) * keep
    var = jnp.sum(centred * centred, -1, keepdims=True) / width
    rstd = lax.rsqrt(var + 1e-5)
    return centred * rstd, rstd


def norm_back(dy, n, rstd, gain, keep, width):
    dy = dy * keep
    dz = dy * gain
    m1 = jnp.sum(dz, -1, keepdims=True) / width
    m2 = jnp.sum(dz * n, -1, keepdims=True) / width
    dx = keep * rstd * (dz - m1 - n * m2)
    return dx, jnp.sum(dy * n, 0, keepdims=True), jnp.sum(dy, 0, keepdims=True)


def bell(z):
    cdf = 0.5 * (1.0 + lax.erf(z * (1.0 / math.sqrt(2.0))))
    pdf = jnp.exp(-0.5 * z * z) * (1.0 / math.sqrt(2.0 * math.pi))
    return cdf, pdf


def rows_of(pair, s, repeat):
    return jnp.concatenate([pair[i][s * LEN:(s + 1) * LEN] for i in repeat], 0)


def head(x, h):
    return x[:, h * HD:(h + 1) * HD]


def corners(r):
    return (r[LEN:, LEN:] + r[LEN:, :LEN]) + (r[:LEN, LEN:] + r[:LEN, :LEN])


def three(x):
    hi, lo = split(x)
    return jnp.concatenate([hi, lo, hi], 1)


def beside(pair, s, h):
    hi, lo = (head(x[s * LEN:(s + 1) * LEN], h) for x in pair)
    return jnp.concatenate([hi, jnp.zeros((LEN, LEN - HD), bf16), lo], 1)


def times(x, right):
    r = dot(stacked(x), right, NN)
    return (r[LEN:, :HD] + r[:LEN, LEN:]) + r[:LEN, :HD]


def dot(a, b, dims):
    return lax.dot_general(a, b, dims, preferred_element_type=f32)


def attend(q, k, v, lens, causal, p_ref):
    qs, ks, vs = split(q * (1.0 / math.sqrt(HD))), split(k), split(v)
    col = lax.broadcasted_iota(jnp.int32, (LEN, LEN), 1)
    for s in range(SENT):
        allowed = col < lens[s]
        if causal:
            allowed = allowed & (lax.broadcasted_iota(jnp.int32, (LEN, LEN), 0) >= col)
        q2, k2 = rows_of(qs, s, (0, 1)), rows_of(ks, s, (0, 1))
        for h in range(H):
            p_ref[s * H + h] = jnp.where(allowed, corners(dot(head(q2, h), head(k2, h), NT)), -1e30)
    for i in range(SENT * H):
        scores = p_ref[i]
        e = jnp.exp(scores - jnp.max(scores, -1, keepdims=True))
        p_ref[i] = e * (1.0 / jnp.sum(e, -1, keepdims=True))
    rows = []
    for s in range(SENT):
        v3 = rows_of(vs, s, (0, 0, 1))
        rows.append(jnp.concatenate([dot(three(p_ref[s * H + h]), head(v3, h), NN) for h in range(H)], 1))
    return jnp.concatenate(rows, 0)


def attend_back(do, q, k, v, p_ref, ds_ref):
    scale = 1.0 / math.sqrt(HD)
    dos, qs, ks, vs = split(do), split(q * scale), split(k * scale), split(v)
    for s in range(SENT):
        do2, v2 = rows_of(dos, s, (0, 1)), rows_of(vs, s, (0, 1))
        for h in range(H):
            ds_ref[s * H + h] = corners(dot(head(do2, h), head(v2, h), NT))
    for i in range(SENT * H):
        prob, dp = p_ref[i], ds_ref[i]
        ds_ref[i] = prob * (dp - jnp.sum(dp * prob, -1, keepdims=True))
    all_q, all_k, all_v = [], [], []
    for s in range(SENT):
        ids = [(s * H + h, h) for h in range(H)]
        all_q.append(jnp.concatenate([times(ds_ref[i], beside(ks, s, h)) for i, h in ids], 1))
        all_k.append(jnp.concatenate([times(ds_ref[i].T, beside(qs, s, h)) for i, h in ids], 1))
        all_v.append(jnp.concatenate([times(p_ref[i].T, beside(dos, s, h)) for i, h in ids], 1))
    return tuple(jnp.concatenate(x, 0) for x in (all_q, all_k, all_v))


def ffn_forward(ns, up, bias, down, ffn_limit, z_ref, acc_ref):
    acc_ref[...] = jnp.zeros_like(acc_ref)

    def body(j, _):
        sl = pl.ds(pl.multiple_of(j * TILE, TILE), TILE)
        z = mm(ns[...], up[:, sl]) + bias[sl].astype(f32).reshape(1, TILE)
        z_ref[:, sl] = z
        mask = (lax.broadcasted_iota(jnp.int32, (1, TILE), 1) + j * TILE < ffn_limit).astype(f32)
        u = z * bell(z)[0] * mask
        acc_ref[...] += mm(stacked(u), down[sl, :])
        return 0

    lax.fori_loop(0, FF // TILE, body, 0)


def ffn_backward(dyk, n, z_ref, up, down, ffn_limit, core, dys_ref, keep_ref, send_ref, bias_ref, acc_ref,
                 arrive=None):
    acc_ref[...] = jnp.zeros_like(acc_ref)
    dys_ref[...] = stacked(dyk)
    first = core == 0
    keep_ref[:, :D] = jnp.where(first, n, dyk)
    send_ref[:, :D] = jnp.where(first, dyk, n)

    def body(j, _):
        sl = pl.ds(pl.multiple_of(j * TILE, TILE), TILE)
        out = pl.ds(pl.multiple_of(j * TILE + D, 128), TILE)
        if arrive is not None:
            arrive(sl, j)
        du = mm(dys_ref[...], down[sl, :], NT)
        z = z_ref[:, sl]
        cdf, pdf = bell(z)
        mask = (lax.broadcasted_iota(jnp.int32, (1, TILE), 1) + j * TILE < ffn_limit).astype(f32)
        u = z * cdf * mask
        dz = du * mask * (cdf + z * pdf)
        keep_ref[:, out] = jnp.where(first, dz, u)
        send_ref[:, out] = jnp.where(first, u, dz)
        bias_ref[:, sl] = jnp.sum(dz, 0, keepdims=True)
        acc_ref[...] += mm(stacked(dz), up[:, sl], NT)
        return 0

    lax.fori_loop(0, FF // TILE, body, 0)


def load_vectors(ref):
    return ref[...].astype(f32)


def setting(table):
    g = lax.axis_index("sub")
    core = lax.axis_index("dp") & 1
    c = table[4 * g + 3]
    bits = [(c & 1).astype(f32), ((c >> 1) & 1).astype(f32), ((c >> 2) & 1).astype(f32)]
    total = bits[0] + bits[1] + bits[2]
    sc = (table[4 * g], table[4 * g + 1] * HD, table[4 * g + 2], table[16], table[17], table[18], table[19], core)
    return sc, [b / total for b in bits]


def fetch(pairs, sems):
    copies = [pltpu.make_async_copy(a, b, sems.at[i]) for i, (a, b) in enumerate(pairs)]
    for c in copies:
        c.start()
    return copies


def encoder_kernel(table, vec_ref, upb, x_ref, w_triple, w_out, w_up, w_down,
                   o_encoded, o_qkv, o_p, o_mixed, o_middle, o_z,
                   b_triple, b_out, b_up, b_down, ns_ref, acc_ref, b_x,
                   encoded, qkv, p_ref, mixed, middle, z_ref, sems, out_sems):
    read_x, *copies = fetch([(x_ref, b_x), (w_triple, b_triple), (w_out, b_out), (w_up, b_up), (w_down, b_down)], sems)
    leaving = []

    def leave(src, dst):
        copy = pltpu.make_async_copy(src, dst, out_sems.at[len(leaving)])
        copy.start()
        leaving.append(copy)

    sc, pick = setting(table)
    width = sc[0].astype(f32)
    keep, heads = lane_mask(D, sc[0]), lane_mask(D, sc[1])
    vec = load_vectors(vec_ref)
    read_x.wait()
    x = b_x[...]
    n, _ = norm(x, keep, width)
    ns = stacked((n * vec[0:1] + vec[2:3]) * keep)
    copies[0].wait()
    qkv[:, :D] = (mm(ns, b_triple[:, :D]) + vec[4:5]) * heads
    qkv[:, D:2 * D] = mm(ns, b_triple[:, D:2 * D]) * heads
    qkv[:, 2 * D:] = (mm(ns, b_triple[:, 2 * D:]) + vec[5:6]) * heads
    leave(qkv, o_qkv)
    o = attend(qkv[:, :D], qkv[:, D:2 * D], qkv[:, 2 * D:], (sc[3], sc[4]), False, p_ref)
    mixed[...] = o
    leave(p_ref, o_p)
    leave(mixed, o_mixed)
    copies[1].wait()
    mid = x + (mm(stacked(o), b_out[...]) + vec[6:7]) * keep
    middle[...] = mid
    leave(middle, o_middle)
    n, _ = norm(mid, keep, width)
    ns_ref[...] = stacked((n * vec[1:2] + vec[3:4]) * keep)
    copies[2].wait()
    copies[3].wait()
    ffn_forward(ns_ref, b_up, upb, b_down, sc[2], z_ref, acc_ref)
    leave(z_ref, o_z)
    encoded[...] = (middle[...] + (acc_ref[...] + vec[7:8]) * keep) * row_ok(sc[3], sc[4])
    leave(encoded, o_encoded)
    for copy in leaving:
        copy.wait()


def decoder_kernel(table, vec_ref, upb, x_ref, prev_ref, src_ref, cot_ref, enc_in,
                   w_triple, w_out, w_query, w_pair, w_cross, w_up, w_down,
                   o_decoded, o_qkv, o_p, o_mixed, a1_ref, mem_ref, qkv_c, p_cross, mixed_c, da2_ref,
                   o_keep, send_buf, dvec, dupb,
                   b_triple, b_out, b_query, b_pair, b_cross, b_up, b_down, ns_ref, acc_ref, z_ref, enc_ref,
                   decoded, qkv, p_self, mixed, a2_ref, keep_buf, sems, out_sems):
    copies = fetch([(w_triple, b_triple), (w_out, b_out), (w_query, b_query), (w_pair, b_pair),
                    (w_cross, b_cross), (w_up, b_up), (w_down, b_down), (enc_in, enc_ref)], sems)
    leaving = []

    def leave(src, dst):
        copy = pltpu.make_async_copy(src, dst, out_sems.at[len(leaving)])
        copy.start()
        leaving.append(copy)

    sc, pick = setting(table)
    width = sc[0].astype(f32)
    keep, heads = lane_mask(D, sc[0]), lane_mask(D, sc[1])
    vec = load_vectors(vec_ref)
    x = x_ref[...]
    n, _ = norm(x, keep, width)
    ns = stacked((n * vec[0:1] + vec[3:4]) * keep)
    copies[0].wait()
    qkv[:, :D] = (mm(ns, b_triple[:, :D]) + vec[6:7]) * heads
    qkv[:, D:2 * D] = mm(ns, b_triple[:, D:2 * D]) * heads
    qkv[:, 2 * D:] = (mm(ns, b_triple[:, 2 * D:]) + vec[7:8]) * heads
    o = attend(qkv[:, :D], qkv[:, D:2 * D], qkv[:, 2 * D:], (sc[5], sc[6]), True, p_self)
    mixed[...] = o
    leave(qkv, o_qkv)
    leave(p_self, o_p)
    leave(mixed, o_mixed)
    copies[1].wait()
    a1 = x + (mm(stacked(o), b_out[...]) + vec[8:9]) * keep
    a1_ref[...] = a1
    n, _ = norm(a1, keep, width)
    ns = stacked((n * vec[1:2] + vec[4:5]) * keep)
    copies[2].wait()
    qkv_c[:, :D] = (mm(ns, b_query[...]) + vec[9:10]) * heads
    copies[7].wait()
    memory = (pick[0] * prev_ref[...] + pick[1] * src_ref[...] + pick[2] * enc_ref[...]) * keep
    mem_ref[...] = memory
    ns = stacked(memory)
    copies[3].wait()
    qkv_c[:, D:2 * D] = mm(ns, b_pair[:, :D]) * heads
    qkv_c[:, 2 * D:] = (mm(ns, b_pair[:, D:]) + vec[10:11]) * heads
    o = attend(qkv_c[:, :D], qkv_c[:, D:2 * D], qkv_c[:, 2 * D:], (sc[3], sc[4]), False, p_cross)
    mixed_c[...] = o
    copies[4].wait()
    a2_ref[...] = a1_ref[...] + (mm(stacked(o), b_cross[...]) + vec[11:12]) * keep
    n, _ = norm(a2_ref[...], keep, width)
    ns_ref[...] = stacked((n * vec[2:3] + vec[5:6]) * keep)
    copies[5].wait()
    copies[6].wait()
    ffn_forward(ns_ref, b_up, upb, b_down, sc[2], z_ref, acc_ref)
    ok = row_ok(sc[5], sc[6])
    decoded[...] = (a2_ref[...] + (acc_ref[...] + vec[12:13]) * keep) * ok
    leave(decoded, o_decoded)
    dy = cot_ref[...] * ok
    dyk = dy * keep
    n, rstd = norm(a2_ref[...], keep, width)
    ffn_backward(dyk, (n * vec[2:3] + vec[5:6]) * keep, z_ref, b_up, b_down, sc[2], sc[7], ns_ref,
                 keep_buf, send_buf, dupb, acc_ref)
    leave(keep_buf, o_keep)
    dx, dg, db = norm_back(acc_ref[...], n, rstd, vec[2:3], keep, width)
    da2_ref[...] = dy + dx
    dvec[...] = jnp.concatenate([dg, db, jnp.sum(dyk, 0, keepdims=True), jnp.zeros((5, D), f32)], 0)
    for copy in leaving:
        copy.wait()


def cross_back_kernel(table, vec_ref, da2_ref, a1_ref, mem_ref, qkv_c, p_cross, mixed_c,
                      w_query, w_pair, w_cross,
                      da1_ref, dmem_ref, dprev_ref, keep_buf, send_buf, dvec, ds_ref):
    sc, pick = setting(table)
    width = sc[0].astype(f32)
    keep, heads = lane_mask(D, sc[0]), lane_mask(D, sc[1])
    vec = load_vectors(vec_ref)
    first = sc[7] == 0
    da2 = da2_ref[...]
    dyk = da2 * keep
    do = mm(stacked(dyk), w_cross[...], NT)
    dq, dk, dv = attend_back(do, qkv_c[:, :D], qkv_c[:, D:2 * D], qkv_c[:, 2 * D:], p_cross, ds_ref)
    dq, dk, dv = dq * heads, dk * heads, dv * heads
    n, rstd = norm(a1_ref[...], keep, width)
    normed = (n * vec[1:2] + vec[4:5]) * keep
    for i, (a, b) in enumerate(((mem_ref[...], normed), (mem_ref[...], mixed_c[...]), (dk, dq), (dv, dyk))):
        keep_buf[:, i * D:(i + 1) * D] = jnp.where(first, a, b)
        send_buf[:, i * D:(i + 1) * D] = jnp.where(first, b, a)
    dn = mm(stacked(dq), w_query[...], NT)
    dx, dg, db = norm_back(dn, n, rstd, vec[1:2], keep, width)
    da1_ref[...] = da2 + dx
    dmem = (mm(stacked(dk), w_pair[:, :D], NT) + mm(stacked(dv), w_pair[:, D:], NT)) * keep
    dmem_ref[...] = dmem
    dprev_ref[...] = dmem * pick[0]
    dvec[...] = jnp.concatenate(
        [dg, db] + [jnp.sum(t, 0, keepdims=True) for t in (dq, dv, dyk)] + [jnp.zeros((3, D), f32)], 0)


def self_back_kernel(gain_row, shift_row, with_memory, table, vec_ref, dy_ref, x_ref, qkv, p_ref, mixed,
                     dmem_ref, w_triple, w_out, dx_ref, keep_buf, send_buf, dvec, ds_ref):
    sc, pick = setting(table)
    width = sc[0].astype(f32)
    keep, heads = lane_mask(D, sc[0]), lane_mask(D, sc[1])
    vec = load_vectors(vec_ref)
    gain, shift = vec[gain_row:gain_row + 1], vec[shift_row:shift_row + 1]
    first = sc[7] == 0
    dy = dy_ref[...]
    dyk = dy * keep
    do = mm(stacked(dyk), w_out[...], NT)
    dq, dk, dv = attend_back(do, qkv[:, :D], qkv[:, D:2 * D], qkv[:, 2 * D:], p_ref, ds_ref)
    dq, dk, dv = dq * heads, dk * heads, dv * heads
    n, rstd = norm(x_ref[...], keep, width)
    normed = (n * gain + shift) * keep
    for i, (a, b) in enumerate(((normed, normed), (normed, mixed[...]), (dq, dv), (dk, dyk))):
        keep_buf[:, i * D:(i + 1) * D] = jnp.where(first, a, b)
        send_buf[:, i * D:(i + 1) * D] = jnp.where(first, b, a)
    dn = mm(stacked(dq), w_triple[:, :D], NT) + mm(stacked(dk), w_triple[:, D:2 * D], NT)
    dn += mm(stacked(dv), w_triple[:, 2 * D:], NT)
    dx, dg, db = norm_back(dn, n, rstd, gain, keep, width)
    dx = dx + dy
    if with_memory:
        dx = dx + pick[1] * dmem_ref[...]
    dx_ref[...] = dx
    dvec[...] = jnp.concatenate(
        [dg, db] + [jnp.sum(t, 0, keepdims=True) for t in (dq, dv, dyk)] + [jnp.zeros((3, D), f32)], 0)


def encoder_ffn_back_kernel(table, vec_ref, h_cot, h_dmem, h_middle, h_z, w_up, w_down,
                            dmid_ref, keep_buf, send_buf, dvec, dupb,
                            b_up, b_down, ns_ref, acc_ref, cot_ref, dmem_ref, middle, z_ref, sems, first_sems):
    first = fetch([(h_cot, cot_ref), (h_dmem, dmem_ref), (h_middle, middle)], first_sems)

    def tile_copies(sl, j):
        return (pltpu.make_async_copy(h_z.at[:, sl], z_ref.at[:, sl], sems.at[2, j]),
                pltpu.make_async_copy(w_down.at[sl, :], b_down.at[sl, :], sems.at[0, j]),
                pltpu.make_async_copy(w_up.at[:, sl], b_up.at[:, sl], sems.at[1, j]))

    for j in range(FF // TILE):
        for copy in tile_copies(pl.ds(j * TILE, TILE), j):
            copy.start()

    def arrive(sl, j):
        for copy in tile_copies(sl, j):
            copy.wait()

    sc, pick = setting(table)
    width = sc[0].astype(f32)
    keep = lane_mask(D, sc[0])
    vec = load_vectors(vec_ref)
    for copy in first:
        copy.wait()
    dy = (cot_ref[...] + pick[2] * dmem_ref[...]) * row_ok(sc[3], sc[4])
    dyk = dy * keep
    n, rstd = norm(middle[...], keep, width)
    ffn_backward(dyk, (n * vec[1:2] + vec[3:4]) * keep, z_ref, b_up, b_down, sc[2], sc[7], ns_ref,
                 keep_buf, send_buf, dupb, acc_ref, arrive)
    dx, dg, db = norm_back(acc_ref[...], n, rstd, vec[1:2], keep, width)
    dmid_ref[...] = dy + dx
    dvec[...] = jnp.concatenate([dg, db, jnp.sum(dyk, 0, keepdims=True), jnp.zeros((5, D), f32)], 0)


WIDE = 768


def ffn_grad_kernel(kept, got, out, at_s, buf_up, buf_down, sems):
    first = (lax.axis_index("dp") & 1) == 0
    for i, ref in enumerate((kept, got)):
        hi, lo = split(ref[:, :D].T)
        at_s[0, :, i * T:(i + 1) * T] = hi
        at_s[1, :, i * T:(i + 1) * T] = lo
    n_up, n_down = WIDE // 128 * 40, WIDE // 192
    left = lax.broadcasted_iota(jnp.int32, (320, 128), 1) < 64

    def up_copy(j, slot):
        rows = pl.ds(pl.multiple_of(j * n_up, 8), n_up)
        return pltpu.make_async_copy(buf_up.at[slot], out.at[:, rows, :], sems.at[slot])

    def down_copy(j, slot):
        rows = pl.ds(0, ROWS_FFN)
        return pltpu.make_async_copy(buf_down.at[slot], out.at[pl.ds(j * n_down, n_down), rows, :], sems.at[slot])

    def body(j, _):
        slot = j & 1
        cols = pl.ds(pl.multiple_of(j * WIDE + D, 128), WIDE)
        r = dot3((at_s[0], at_s[1]), split(jnp.concatenate([kept[:, cols], got[:, cols]], 0)), NN)
        tiles = [r[:, c * 128:(c + 1) * 128] for c in range(WIDE // 128)]

        @pl.when(first)
        def _():
            @pl.when(j >= 2)
            def _():
                up_copy(j - 2, slot).wait()

            for c, t in enumerate(tiles):
                buf_up[slot, :, c * 40:(c + 1) * 40, :] = t.reshape(16, 40, 128)
            up_copy(j, slot).start()

        @pl.when(jnp.logical_not(first))
        def _():
            @pl.when(j >= 2)
            def _():
                down_copy(j - 2, slot).wait()

            for p in range(n_down // 2):
                a, shared, b = tiles[3 * p:3 * p + 3]
                upper, lower = shared[:320], shared[320:]
                buf_down[slot, 2 * p, :D, :] = a
                buf_down[slot, 2 * p, D:, :] = jnp.where(left, upper, pltpu.roll(lower, 64, 1))
                buf_down[slot, 2 * p + 1, :D, :] = b
                buf_down[slot, 2 * p + 1, D:, :] = jnp.where(left, pltpu.roll(upper, 64, 1), lower)
            down_copy(j, slot).start()

        return 0

    steps = FF // WIDE
    lax.fori_loop(0, steps, body, 0)

    @pl.when(first)
    def _():
        for j in (steps - 2, steps - 1):
            up_copy(j, j & 1).wait()

    @pl.when(jnp.logical_not(first))
    def _():
        for j in (steps - 2, steps - 1):
            down_copy(j, j & 1).wait()


def small_block(out, base, ffn_vec, att_vec, upb, counts, group):
    lane = lax.broadcasted_iota(jnp.int32, (1, 128), 1)
    totals = jnp.where(lane == group, counts[0], 0) + jnp.where(lane == group + 4, counts[1], 0)
    totals = totals.astype(f32)
    for b in range(16):
        out[b, base:base + 16, :] = jnp.zeros((16, 128), f32)
        if ffn_vec is not None:
            out[b, base:base + 3, :40] = ffn_vec[:3, b * 40:(b + 1) * 40]
        out[b, base + 3:base + 8, :40] = att_vec[:5, b * 40:(b + 1) * 40]
        if upb is not None:
            for c in range(2):
                out[b, base + 8 + c:base + 9 + c, :96] = upb[:, b * 192 + c * 96:b * 192 + (c + 1) * 96]
        out[b, base + 15:base + 16, :] = totals


def att_grad_kernel(with_ffn, *refs):
    table = refs[0]
    whole, out, sem = refs[-3:]
    refs = list(refs[2:-3])
    group = lax.axis_index("sub")
    counts = (table[16] + table[17], table[18] + table[19])
    copies = []
    for n, ffn in enumerate(with_ffn):
        kept, got, att_vec = refs[:3]
        ffn_vec, upb = (refs[3], refs[4]) if ffn else (None, None)
        refs = refs[5 if ffn else 3:]
        base = n * ROWS_ATT
        small_block(out, base + 400, ffn_vec, att_vec, upb, counts, group)
        for i in range(2):
            a = jnp.concatenate([kept[:, i * D:(i + 1) * D].T, got[:, i * D:(i + 1) * D].T], 1)
            b = jnp.concatenate([kept[:, (i + 2) * D:(i + 3) * D], got[:, (i + 2) * D:(i + 3) * D]], 0)
            a, b = split(a), split(b)
            r = dot3(a, b, NN)
            for c in range(5):
                row = base + i * 200 + c * 40
                out[:, row:row + 40, :] = r[:, c * 128:(c + 1) * 128].reshape(16, 40, 128)
        copy = pltpu.make_async_copy(
            out.at[:, pl.ds(base, ROWS_ATT), :], whole.at[:, pl.ds(ROWS_FFN + base, ROWS_ATT), :], sem.at[n])
        copy.start()
        copies.append(copy)
    for copy in copies:
        copy.wait()


def usage_scale(cfg, totals, row_kind, rows, col_kind, cols):
    limit = {"keep": lambda g: cfg[4 * g], "head": lambda g: cfg[4 * g + 1] * HD, "ffn": lambda g: cfg[4 * g + 2]}
    usage = 0.0
    for g in range(4):
        part = jnp.where(rows < limit[row_kind](g), totals[g], 0.0)
        if col_kind is not None:
            part = jnp.where(cols < limit[col_kind](g), part, 0.0)
        usage = usage + part
    return lax.rsqrt(usage)


def finish_kernel(is_dec, cfg, mine, other, *refs):
    whole = refs[-1]
    outs = refs[:-1]
    pos = lax.axis_index("dp")
    px = lax.axis_index("sub")
    core = pos & 1
    sign = 1 - 2 * core
    first = core == 0
    n = mine.shape[1]
    for k in range(4):
        for ref, owner, from_x in ((mine, core, (px - sign * k) & 3), (other, 1 - core, (px + sign * k) & 3)):
            whole[owner, pl.ds(pl.multiple_of(from_x * n, 8), n), :] = ref[k]

    def half(owner, row):
        return jnp.where(first, whole[owner, row:row + 20, :], whole[owner, row + 20:row + 40, :])

    def iota(shape, dim):
        return lax.broadcasted_iota(jnp.int32, shape, dim)

    cols = iota((1, D), 1)
    odd = ((pos >> 1) & 1) == 1
    rows20, rows96 = pos * 20 + iota((20, 1), 0), pos * 96 + iota((96, 1), 0)
    lanes20, lanes96 = pos * 20 + iota((1, 20), 1), pos * 96 + iota((1, 96), 1)

    def job(out, col, owner, base, i, factor):
        for c in range(5):
            out[:, col + c * 128:col + (c + 1) * 128] = (
                half(owner, base + i * 200 + c * 40) * factor[:, c * 128:(c + 1) * 128])

    def small(base):
        both = whole[0, base + 400:base + 416, :] + whole[1, base + 400:base + 416, :]
        return both, jnp.where(first, both[:, :20], both[:, 20:40])

    def put(out, items):
        for i, (vec, k, factor) in enumerate(items):
            out[i:i + 1, :] = vec[k:k + 1, :] * factor

    c_all, c_vec = small(ROWS_FFN)
    scale = functools.partial(
        usage_scale, cfg, [c_all[15:16, 4 * is_dec + g:4 * is_dec + g + 1] for g in range(4)])
    keep_head = scale("keep", rows20, "head", cols)
    head_keep = scale("head", rows20, "keep", cols)
    keep_row = scale("keep", lanes20, None, None)
    head_row = scale("head", lanes20, None, None)
    keep_ffn = scale("keep", rows20, "ffn", iota((1, FF), 1))
    ffn_keep = scale("ffn", rows96, "keep", cols)
    att, ffn, bias = ROWS_FFN, 0, c_all
    if is_dec:
        c, att = ROWS_FFN, ROWS_FFN + ROWS_ATT
        s_vec = small(att)[1]
        gains, shifts, triple, output, query, pair, cross, biases, up, up_bias, down = outs
        put(gains, ((s_vec, 3, keep_row), (c_vec, 3, keep_row), (c_vec, 0, keep_row)))
        put(shifts, ((s_vec, 4, keep_row), (c_vec, 4, keep_row), (c_vec, 1, keep_row)))
        put(biases, ((s_vec, 5, head_row), (s_vec, 6, head_row), (s_vec, 7, keep_row),
                     (c_vec, 5, head_row), (c_vec, 6, head_row), (c_vec, 7, keep_row), (c_vec, 2, keep_row)))
        job(query, 0, 1, c, 0, keep_head)
        job(pair, 0, 0, c, 0, keep_head)
        job(pair, D, 0, c, 1, keep_head)
        job(cross, 0, 1, c, 1, head_keep)
    else:
        gains, shifts, triple, output, biases, up, up_bias, down = outs
        put(gains, ((c_vec, 3, keep_row), (c_vec, 0, keep_row)))
        put(shifts, ((c_vec, 4, keep_row), (c_vec, 1, keep_row)))
        put(biases, ((c_vec, 5, head_row), (c_vec, 6, head_row), (c_vec, 7, keep_row), (c_vec, 2, keep_row)))
    job(triple, 0, 0, att, 0, keep_head)
    job(triple, D, 0, att, 1, keep_head)
    job(triple, 2 * D, 1, att, 0, keep_head)
    job(output, 0, 1, att, 1, head_keep)
    for t in range(24):
        up[:, t * 128:(t + 1) * 128] = half(0, ffn + t * 40) * keep_ffn[:, t * 128:(t + 1) * 128]
    tile = whole[1, ffn:ffn + D, :].T
    both = whole[1, ffn + D:ffn + ROWS_FFN, :].T
    rest = jnp.concatenate([both[:64], both[64:]], 1)
    units = jnp.where(odd, jnp.concatenate([rest, tile], 0), jnp.concatenate([tile, rest], 0))
    down[...] = jnp.where(first, units[:96], units[96:]) * ffn_keep
    bias_row = jnp.where(first, bias[8:9, :96], bias[9:10, :96])
    up_bias[...] = bias_row * scale("ffn", lanes96, None, None)


SMEM = pl.BlockSpec(memory_space=pltpu.SMEM)
VMEM = pl.BlockSpec(memory_space=pltpu.VMEM)
ANY = pl.BlockSpec(memory_space=pl.ANY)
HBM = pl.BlockSpec(memory_space=pltpu.HBM)


def arr(*shape):
    return jax.ShapeDtypeStruct(shape, f32)


def hbm(*shape):
    return pltpu.HBM(shape, f32)


def call(kernel, in_specs, outs, name, scratch=(), limit=56, flops=1 << 20, nbytes=1 << 20, out_spec=None):
    return pl.pallas_call(
        kernel,
        in_specs=in_specs,
        out_shape=outs,
        out_specs=out_spec or [VMEM] * len(outs),
        scratch_shapes=list(scratch),
        name=name,
        compiler_params=pltpu.CompilerParams(vmem_limit_bytes=limit << 20),
        cost_estimate=pl.CostEstimate(flops=flops, bytes_accessed=nbytes, transcendentals=0),
    )


def in_hbm(*arrays):
    return tuple(pltpu.with_memory_space_constraint(a, pltpu.HBM) for a in arrays)


def flat_perm(move):
    pairs = []
    for x in range(4):
        for y in range(4):
            for z in range(4):
                for c in range(2):
                    X, Y, Z, C = move(x, y, z, c)
                    pairs.append((x * 32 + y * 8 + z * 2 + c, (X % 4) * 32 + (Y % 4) * 8 + (Z % 4) * 2 + C % 2))
    return pairs


SWAP = flat_perm(lambda x, y, z, c: (x, y, z, 1 - c))
RING = {
    "x": flat_perm(lambda x, y, z, c: (x + 1 - 2 * c, y, z, c)),
    "y": flat_perm(lambda x, y, z, c: (x, y + 1 - 2 * c, z, c)),
    "z": flat_perm(lambda x, y, z, c: (x, y, z + 1 - 2 * c, c)),
}
HOP_X = [flat_perm(lambda x, y, z, c, k=k: (x + k - 2 * c * k, y, z, c)) for k in range(4)]


def turn(p, c):
    return p + (1 - 2 * c) * (1 - 2 * (p & 1))


PAIR = {
    "x": (flat_perm(lambda x, y, z, c: (turn(x, c), y, z, c)), flat_perm(lambda x, y, z, c: (x + 2, y, z, c))),
    "y": (flat_perm(lambda x, y, z, c: (x, turn(y, c), z, c)), flat_perm(lambda x, y, z, c: (x, y + 2, z, c))),
    "z": (flat_perm(lambda x, y, z, c: (x, y, turn(z, c), c)), flat_perm(lambda x, y, z, c: (x, y, z + 2, c))),
}


def move(x, perm):
    return lax.ppermute(x, MESH_AXES, perm)


def barrier(*trees):
    return lax.optimization_barrier(trees)


class Part:
    def __init__(self, array, rows, order, dims):
        self.array, self.rows, self.order, self.dims = array, rows, list(order), list(dims)
        self.step, self.got = 0, []

    @property
    def size(self):
        return self.rows[1] - self.rows[0]


def advance(parts, name):
    inputs = []

    def slot(array):
        for n, a in enumerate(inputs):
            if a is array:
                return n
        inputs.append(array)
        return len(inputs) - 1

    plans, routes, out_shapes = [], {}, []
    for part in parts:
        axis = part.order[0]
        d = part.dims.index(axis)
        plan = dict(src=slot(part.array), rows=part.rows, d=d, axis=axis, step=part.step, nd=len(part.dims),
                    got=[(slot(a), off) for a, off in part.got], m=part.size)
        if part.step == 2:
            plan["out"] = len(out_shapes)
            out_shapes.append((4,) * (len(part.dims) - 1) + (part.size, 128))
            if len(part.order) > 1:
                plan["next_axis"] = part.order[1]
                rest = [t for t in part.dims if t != axis]
                plan["next_d"] = rest.index(part.order[1])
        plans.append(plan)
        send_axis, kind = (axis, part.step) if part.step < 2 else (plan.get("next_axis"), 0)
        if send_axis is not None:
            nd = plan["nd"] if part.step < 2 else plan["nd"] - 1
            chunk_rows = 4 ** (nd - 1) * part.size
            route = routes.setdefault((send_axis, kind), [0, []])
            plan["route"], plan["offset"], plan["chunk"] = (send_axis, kind), route[0], chunk_rows
            route[0] += chunk_rows * (2 if kind == 0 else 1)
    n_state = len(out_shapes)
    route_list = sorted(routes, key=lambda r: "yzx".index(r[0]))
    out_shapes += [(routes[r][0], 128) for r in route_list]
    n_in = len(inputs)

    def kernel(*refs):
        ins, outs = refs[:n_in], refs[n_in:]
        pos = lax.axis_index("dp")
        core = pos & 1
        place = {"x": lax.axis_index("sub"), "y": pos >> 3, "z": (pos >> 1) & 3}

        def chunk(ref, nd, d, k, rows):
            index = [slice(None)] * nd
            index[d] = k & 3
            return ref[tuple(index) + (slice(*rows), slice(None))].reshape(-1, 128)

        for plan in plans:
            src, nd, d, rows, m = ins[plan["src"]], plan["nd"], plan["d"], plan["rows"], plan["m"]
            p = place[plan["axis"]]
            n = 4 ** (nd - 1) * m
            got = [(ins[i], off) for i, off in plan["got"]]
            out = outs[n_state + route_list.index(plan["route"])] if "route" in plan else None
            off = plan.get("offset")
            if plan["step"] == 0:
                q = turn(p, core)
                out[off:off + n, :] = chunk(src, nd, d, q, rows)
                out[off + n:off + 2 * n, :] = chunk(src, nd, d, q + 2, rows)
            elif plan["step"] == 1:
                (a, a_off), = got
                out[off:off + n, :] = chunk(src, nd, d, p + 2, rows) + a[a_off + n:a_off + 2 * n, :]
            else:
                (a, a_off), (b, b_off) = got
                total = chunk(src, nd, d, p, rows) + a[a_off:a_off + n, :] + b[b_off:b_off + n, :]
                state = outs[plan["out"]]
                state[...] = total.reshape(state.shape)
                if out is not None:
                    nn = plan["chunk"]
                    q = turn(place[plan["next_axis"]], core)
                    out[off:off + nn, :] = chunk(state, nd - 1, plan["next_d"], q, (0, m))
                    out[off + nn:off + 2 * nn, :] = chunk(state, nd - 1, plan["next_d"], q + 2, (0, m))

    outs = call(kernel, [VMEM] * n_in, [arr(*t) for t in out_shapes], name, limit=24)(*inputs)
    sent = {r: move(outs[n_state + i], PAIR[r[0]][r[1]]) for i, r in enumerate(route_list)}
    for part, plan in zip(parts, plans):
        if part.step == 2:
            part.array, part.rows = outs[plan["out"]], (0, part.size)
            part.dims.remove(part.order.pop(0))
            part.step, part.got = 0, []
        if "route" in plan:
            part.got.append((plan["route"], plan["offset"]))
            part.step += 1
    return sent


def land(parts, sent):
    for part in parts:
        part.got = [(sent[a], off) if isinstance(a, tuple) else (a, off) for a, off in part.got]


def per_device(
    enc_in, prev_enc, dec_in, enc_cotan, dec_cotan, src_lengths, tgt_lengths, configs,
    enc_gains, enc_shifts, enc_triple, enc_output, enc_biases, enc_up, enc_up_bias, enc_down,
    dec_gains, dec_shifts, dec_triple, dec_output, dec_cross_query, dec_cross_pair, dec_cross_out,
    dec_biases, dec_up, dec_up_bias, dec_down,
):
    group = lax.axis_index("sub")
    pos = lax.axis_index("dp")
    core = pos & 1
    place = {"x": group, "y": pos >> 3, "z": (pos >> 1) & 3}
    sign = 1 - 2 * core
    table = jnp.concatenate([configs.reshape(16), src_lengths.reshape(2), tgt_lengths.reshape(2)])
    x, prev, y = enc_in.reshape(T, D), prev_enc.reshape(T, D), dec_in.reshape(T, D)
    e_cot, d_cot = enc_cotan.reshape(T, D), dec_cotan.reshape(T, D)
    act, act3, prob = arr(T, D), arr(T, 3 * D), arr(2 * H, LEN, LEN)
    act_out = hbm(T, D)
    vmem = pltpu.VMEM
    e_vec = jnp.concatenate([enc_gains.T, enc_shifts.T, enc_biases.T], 0)
    d_vec = jnp.concatenate([dec_gains.T, dec_shifts.T, dec_biases.T], 0)
    head = [SMEM, VMEM]

    encoded, e_qkv, e_p, e_mixed, e_mid, e_z = call(
        encoder_kernel, head + [VMEM] + [HBM] * 5,
        [act_out, hbm(T, 3 * D), hbm(2 * H, LEN, LEN), act_out, act_out, hbm(T, FF)], "encoder_forward", out_spec=[HBM] * 6, scratch=
        [vmem((D, 3 * D), bf16), vmem((D, D), bf16), vmem((D, FF), bf16), vmem((FF, D), bf16),
         vmem((2 * T, D), bf16), vmem((T, D), f32), vmem((T, D), f32),
         vmem((T, D), f32), vmem((T, 3 * D), f32), vmem((2 * H, LEN, LEN), f32), vmem((T, D), f32), vmem((T, D), f32),
         vmem((T, FF), f32), pltpu.SemaphoreType.DMA((5,)), pltpu.SemaphoreType.DMA((6,))], limit=30, flops=8 << 30, nbytes=24 << 20,
    )(table, e_vec, enc_up_bias, *in_hbm(x, enc_triple, enc_output, enc_up, enc_down))

    (decoded, d_qkv, d_p, d_mixed, a1, mem, c_qkv, c_p, c_mixed, da2, f_keep, f_send, f_vec, f_upb) = call(
        decoder_kernel, head + [VMEM] * 5 + [HBM] * 8,
        [act_out, hbm(T, 3 * D), hbm(2 * H, LEN, LEN), act_out, act, act, act3, prob, act, act,
         hbm(T, D + FF), arr(T, D + FF), arr(8, D), arr(1, FF)], "decoder_forward",
        [vmem((D, 3 * D), bf16), vmem((D, D), bf16), vmem((D, D), bf16), vmem((D, 2 * D), bf16),
         vmem((D, D), bf16), vmem((D, FF), bf16), vmem((FF, D), bf16),
         vmem((2 * T, D), bf16), vmem((T, D), f32), vmem((T, FF), f32), vmem((T, D), f32),
         vmem((T, D), f32), vmem((T, 3 * D), f32), vmem((2 * H, LEN, LEN), f32), vmem((T, D), f32),
         vmem((T, D), f32), vmem((T, D + FF), f32),
         pltpu.SemaphoreType.DMA((8,)), pltpu.SemaphoreType.DMA((5,))], limit=36, out_spec=[HBM] * 4 + [VMEM] * 6 + [HBM] + [VMEM] * 3, flops=16 << 30, nbytes=48 << 20,
    )(table, d_vec, dec_up_bias, y, prev, x, d_cot,
      *in_hbm(encoded, dec_triple, dec_output, dec_cross_query, dec_cross_pair, dec_cross_out, dec_up, dec_down))

    def ffn_grad(kept, got, rows, name, pinned=False):
        return pl.pallas_call(
            ffn_grad_kernel,
            in_specs=[VMEM, VMEM],
            out_shape=hbm(16, rows, 128) if pinned else arr(16, rows, 128),
            out_specs=ANY,
            scratch_shapes=[vmem((2, D, 2 * T), bf16), vmem((2, 16, WIDE // 128 * 40, 128), f32),
                            vmem((2, WIDE // 192, ROWS_FFN, 128), f32), pltpu.SemaphoreType.DMA((2,))],
            name=name,
            compiler_params=pltpu.CompilerParams(vmem_limit_bytes=26 << 20),
            cost_estimate=pl.CostEstimate(flops=6 << 30, bytes_accessed=16 << 20, transcendentals=0),
        )(kept, got)

    def att_grad(with_ffn, whole, operands, name, pinned=False):
        n = len(with_ffn)
        return pl.pallas_call(
            functools.partial(att_grad_kernel, with_ffn),
            in_specs=[SMEM, ANY] + [VMEM] * len(operands),
            out_shape=pltpu.HBM(whole.shape, f32) if pinned else arr(*whole.shape),
            out_specs=ANY,
            scratch_shapes=[vmem((16, ROWS_ATT * n, 128), f32), pltpu.SemaphoreType.DMA((n,))],
            input_output_aliases={1: 0},
            name=name,
            compiler_params=pltpu.CompilerParams(vmem_limit_bytes=24 << 20),
            cost_estimate=pl.CostEstimate(flops=3 << 30, bytes_accessed=10 << 20, transcendentals=0),
        )(table, whole, *operands)

    pair = arr(T, 4 * D)
    f_recv = move(f_send, SWAP)
    da1, dmem, dprev, c_keep, c_send, c_vec = call(
        cross_back_kernel, head + [VMEM] * 9, [act, act, act_out, pair, pair, arr(8, D)], "cross_backward", [vmem((2 * H, LEN, LEN), f32)], limit=14, flops=3 << 30, nbytes=16 << 20,
    )(table, d_vec, da2, a1, mem, c_qkv, c_p, c_mixed, dec_cross_query, dec_cross_pair, dec_cross_out)
    c_recv = move(c_send, SWAP)
    dy_in, s_keep, s_send, s_vec = call(
        functools.partial(self_back_kernel, 0, 3, False), head + [VMEM] * 8,
        [act_out, pair, pair, arr(8, D)], "self_backward", [vmem((2 * H, LEN, LEN), f32)], limit=14, flops=3 << 30, nbytes=16 << 20,
    )(table, d_vec, da1, y, d_qkv, d_p, d_mixed, dmem, dec_triple, dec_output)
    f_recv, s_send, s_keep, c_recv, dmem = barrier(f_recv, s_send, s_keep, c_recv, dmem)
    s_recv = move(s_send, SWAP)
    g_d = ffn_grad(f_keep, f_recv, ROWS_FFN + 2 * ROWS_ATT, "decoder_ffn_grad", True)
    g_d, s_recv = barrier(g_d, s_recv)
    g_d = att_grad((True, False), g_d, (c_keep, c_recv, c_vec, f_vec, f_upb, s_keep, s_recv, s_vec),
                   "decoder_attention_grad", True)
    cores = [[2 * i + c for i in range(16)] for c in range(2)]
    g_d, dmem = barrier(g_d, dmem)
    r_d = lax.psum_scatter(g_d, "dp", scatter_dimension=0, axis_index_groups=cores, tiled=True)

    dmid, h_keep, h_send, h_vec, h_upb = call(
        encoder_ffn_back_kernel, head + [HBM] * 6,
        [act, arr(T, D + FF), arr(T, D + FF), arr(8, D), arr(1, FF)], "encoder_ffn_backward",
        [vmem((D, FF), bf16), vmem((FF, D), bf16), vmem((2 * T, D), bf16), vmem((T, D), f32),
         vmem((T, D), f32), vmem((T, D), f32), vmem((T, D), f32), vmem((T, FF), f32),
         pltpu.SemaphoreType.DMA((3, FF // TILE)), pltpu.SemaphoreType.DMA((3,))], limit=24, flops=4 << 30, nbytes=24 << 20,
    )(table, e_vec, *in_hbm(e_cot, dmem, e_mid, e_z, enc_up, enc_down))
    h_recv = move(h_send, SWAP)
    dx_in, e_keep, e_send, e_vec_sum = call(
        functools.partial(self_back_kernel, 0, 2, True), head + [VMEM] * 8,
        [act_out, pair, pair, arr(8, D)], "encoder_attention_backward", [vmem((2 * H, LEN, LEN), f32)], limit=14, flops=3 << 30, nbytes=16 << 20,
    )(table, e_vec, dmid, x, e_qkv, e_p, e_mixed, dmem, enc_triple, enc_output)
    h_recv, e_send, e_keep = barrier(h_recv, e_send, e_keep)
    e_recv = move(e_send, SWAP)
    g_e = ffn_grad(h_keep, h_recv, ROWS_FFN + ROWS_ATT, "encoder_ffn_grad")
    g_e, e_recv = barrier(g_e, e_recv)
    g_e = att_grad((True,), g_e, (e_keep, e_recv, e_vec_sum, h_vec, h_upb), "encoder_attention_grad")

    g_e = g_e.reshape(4, 4, 4, 344, 128)
    enc_parts = [Part(g_e, rows, order, "yzx")
                 for rows, order in (((0, 184), "xyz"), ((184, 264), "yxz"), ((264, 344), "zxy"))]
    def settle(parts, sent, *others):
        keys = list(sent)
        arrived, others = barrier([sent[k] for k in keys], others)
        land(parts, dict(zip(keys, arrived)))
        return others

    def gather(parts):
        own = jnp.concatenate([p.array for p in parts], 0) if len(parts) > 1 else parts[0].array
        return [own] + [move(own, HOP_X[k]) for k in (1, 2, 3)]

    dec_parts, flying, pieces = [], {}, []
    for step in range(7):
        active = enc_parts + (dec_parts if step in (4, 5) else [])
        sent = advance([p for p in active if p.order], "step_%d" % step)
        if step == 2:
            dec_parts = [Part(r_d.reshape(4, 448, 128), (0, 448), "x", "x")]
            flying = advance(dec_parts, "decoder_step")
        if step == 3:
            settle(enc_parts + dec_parts, {**sent, **flying})
        elif step == 5:
            pieces = settle(enc_parts, sent, *gather(dec_parts))
        elif step < 6:
            settle(active, sent)

    def finish(is_dec, mine, other, shapes, name):
        outs = call(
            functools.partial(finish_kernel, is_dec), [SMEM] + [VMEM] * 2, [arr(*t) for t in shapes], name,
            [vmem((2, 4 * mine.shape[1], 128), f32)], limit=24,
        )(table, mine, other)
        return tuple(t.reshape(96) if t.shape == (1, 96) else t.T if t.shape[1] == 20 else t for t in outs)

    mine_d = jnp.stack(pieces, 0)
    other_d = move(mine_d, SWAP)
    pieces = gather(enc_parts)
    dec_grads = finish(True, mine_d, other_d, (
        (3, 20), (3, 20), (20, 3 * D), (20, D), (20, D), (20, 2 * D), (20, D), (7, 20), (20, FF), (1, 96), (96, D)),
        "decoder_finish")
    pieces, dec_grads = barrier(pieces, dec_grads)
    mine_e = jnp.stack(pieces, 0)
    other_e = move(mine_e, SWAP)
    grads = finish(False, mine_e, other_e, (
        (2, 20), (2, 20), (20, 3 * D), (20, D), (4, 20), (20, FF), (1, 96), (96, D)), "encoder_finish") + dec_grads
    whole = (1, SENT, LEN, D)
    return (
        (encoded.reshape(whole), decoded.reshape(whole), dx_in.reshape(whole), dprev.reshape(whole),
         dy_in.reshape(whole)) + grads
    )


def solution(mesh):
    acts = P("sub", "dp", None, None)
    counts = P("sub", "dp")
    row, vector = P("dp", None), P("dp")
    in_specs = (acts,) * 5 + (counts,) * 2 + (P(),) * 20
    out_specs = (acts,) * 5 + (row,) * 6 + (vector, row) + (row,) * 9 + (vector, row)
    return jax.shard_map(per_device, mesh=mesh, in_specs=in_specs, out_specs=out_specs, check_vma=False)
```
